128 devices in a mesh: ctx: 32 (over y_lo, z, x), fsdp: 4 (over y_hi, core).
Axes of the slice: x: 4, y: 4 (y_hi: 2, y_lo: 2; y = y_hi * 2 + y_lo), z: 4, core: 2. Of those that a mesh axis runs over, the one named last changes fastest.
Arguments:
- inputs: bfloat16 [4, 4096, 4096], P('fsdp', 'ctx'), may hold values from -6 to 6
- values: bfloat16 [4, 4096, 8192], P('fsdp', 'ctx'), may hold values from -6 to 6
- cotangent: bfloat16 [4, 4096, 8192], P('fsdp', 'ctx'), may hold values from -6 to 6
- weight: bfloat16 [4096, 1152], P('fsdp'), may hold values from -0.0234375 to 0.0234375
- init_state: bfloat16 [4, 128, 4096], P('fsdp'), may hold values from -1.1953125 to 1.1953125
- resets: int32 [4, 4096], P('fsdp', 'ctx'), may hold values from 0 to 1, as said below
- dt_bias: float32 [128], replicated, may hold values from -5 to -3
- decay_rate: float32 [128], replicated, may hold values from 9.765625e-05 to 1.5
- skip: float32 [128], replicated, may hold values from 0.5 to 1.5
Outputs:
- grad_inputs: bfloat16 [4, 4096, 4096], P('fsdp', 'ctx')
- grad_values: bfloat16 [4, 4096, 8192], P('fsdp', 'ctx')
- grad_weight: float32 [4096, 1152], P('fsdp')
The draws below stay inside these ranges and needn't reach their ends.
Inputs may be any that keep to these rules, and one draw needn't show every extreme that they name: `resets`: each stream flags one or two of its positions.
All inputs are finite; a program needn't handle non-finite values.
Results may differ from the reference program's by a relative error of at most 0.015.
Values may be sent and summed in bfloat16 or wider, within the bound.
A program may use at most 256 MiB of HBM per device.

```python
import math
import jax
import jax.numpy as jnp
from jax import lax

D = 4096
HEADS = 128
HEAD_DIM = 64
STATE = 64
GROUPS = 8
TOK_DEV = 128
COLS = 1152
STREAMS = 4
LENGTH = 4096


def draw_resets(key, part):
    key = jax.random.fold_in(key, 11)
    spots = jax.random.randint(key, (STREAMS, 2), 1, LENGTH)
    marked = jnp.arange(LENGTH)[None, None, :] == spots[:, :, None]
    return jnp.max(marked.astype(jnp.int32), axis=1)


def draw_decay_rate(key, part):
    key = jax.random.fold_in(key, 23)
    lowest = jnp.log(0.4 / LENGTH)
    highest = jnp.log(1.5)
    spread = jax.random.uniform(key, (HEADS,), jnp.float32)
    return jnp.exp(lowest + (highest - lowest) * spread).astype(jnp.float32)


def raised(entries, key, source, target, shards_of, factor):
    owner, partner = [(jnp.arange(entries.shape[axis_at]) // (entries.shape[axis_at] // shards_of)).reshape([-1 if axis == axis_at else 1 for axis in range(entries.ndim)]) for axis_at in (source, target)]
    chosen = jax.random.permutation(key, shards_of)[partner]
    strong = (owner == chosen) | (owner == (partner + shards_of // 2) % shards_of)
    return jnp.where(strong, factor * entries, entries)


def levels(own_key, dims, cuts, low, high):
    def one(dim, parts):
        draws = jax.random.uniform(jax.random.fold_in(jax.random.fold_in(own_key, 6), dim), (parts,), jnp.float32, low / len(cuts), high / len(cuts))
        return jnp.repeat(jnp.exp(draws), dims[dim] // parts).reshape((-1,) + (1,) * (len(dims) - dim - 1))

    factor_of = one(*cuts[0])
    for cut in cuts[1:]:
        factor_of = factor_of * one(*cut)
    return factor_of


def noise(rng, extent, scale, bound, shards=(), kind=jnp.bfloat16):
    entries = scale * jax.random.normal(rng, extent, jnp.float32)
    if shards:
        entries = entries * levels(rng, extent, shards, -0.22, 0.18)
    return jnp.clip(entries, -bound, bound).astype(kind)


def bell_draw_with(key, extent, scale, most, shards, heavy, dtype=jnp.bfloat16):
    entries = scale * jax.random.normal(key, extent, jnp.float32)
    if shards:
        entries = entries * levels(key, extent, shards, -0.22, 0.18)
    return jnp.clip(raised(entries, jax.random.fold_in(key, 3), *heavy), -most, most).astype(dtype)


def setup_inputs(seed: int = 0) -> dict:
    arg_keys = jax.random.split(jax.random.key(seed), 10)
    return {
        "inputs": bell_draw_with(arg_keys[0], (STREAMS, LENGTH, D), 1.0, 6.0, ((0, 4), (1, 32)), (0, 2, 4, 2.0)),
        "values": noise(arg_keys[1], (STREAMS, LENGTH, HEADS * HEAD_DIM), 1.0, 6.0, ((0, 4), (1, 32))),
        "cotangent": noise(arg_keys[2], (STREAMS, LENGTH, HEADS * HEAD_DIM), 1.0, 6.0, ((0, 4), (1, 32))),
        "weight": noise(arg_keys[3], (D, COLS), (16 * D) ** -0.5, 0.0234375, ((0, 4),)),
        "init_state": noise(arg_keys[4], (STREAMS, HEADS, HEAD_DIM * STATE), 0.2, 1.1953125, ((0, 4),)),
        "resets": draw_resets(jax.random.fold_in(arg_keys[9], 71), 0),
        "dt_bias": jnp.clip(jax.random.uniform(arg_keys[6], (HEADS,), jnp.float32, -5.0, -3.0), -5.0, -3.0),
        "decay_rate": draw_decay_rate(jax.random.fold_in(arg_keys[9], 71), 0),
        "skip": jnp.clip(jax.random.uniform(arg_keys[8], (HEADS,), jnp.float32, 0.5, 1.5), 0.5, 1.5),
    }


def prepare(raw_step, value_rows, dt_bias):
    step_size = jax.nn.softplus(raw_step + dt_bias[None, :])
    discrete = (step_size[:, :, None] * value_rows.astype(jnp.float32)).astype(jnp.bfloat16)
    return (step_size, discrete)

def block_stats(b_proj, step_size, discrete, decay_rate, segment):
    tokens, heads = step_size.shape
    per_group = heads // GROUPS
    log_decay = jnp.cumsum(-decay_rate[None, :] * step_size, axis=0)
    final = log_decay[-1]
    same = segment == segment[-1]
    tail = jnp.where(same[:, None], jnp.exp(final[None, :] - log_decay), 0.0)
    total = jnp.where(segment[-1] == 0, jnp.exp(final), 0.0)
    weighted = (tail[:, :, None] * discrete.astype(jnp.float32)).astype(jnp.bfloat16)
    local = jnp.einsum('sgkp,sgn->gkpn', weighted.reshape(tokens, GROUPS, per_group, HEAD_DIM).astype(jnp.float32), b_proj.astype(jnp.float32))
    return (total, local.reshape(heads, HEAD_DIM * STATE))

def group_terms(c_group, b_group, log_group, disc_group, state_group, valid, fresh):
    scores = jnp.einsum('tn,sn->ts', c_group.astype(jnp.float32), b_group.astype(jnp.float32))
    spans = log_group.T[:, :, None] - log_group.T[:, None, :]
    weights = jnp.where(valid, jnp.exp(jnp.where(valid, spans, 0.0)), 0.0)
    mixed = (weights * scores[None, :, :]).astype(jnp.bfloat16)
    inner = jnp.einsum('kts,skp->tkp', mixed.astype(jnp.float32), disc_group.astype(jnp.float32))
    carried = jnp.einsum('tn,kpn->tkp', c_group.astype(jnp.float32), state_group, precision=lax.Precision.HIGHEST)
    reach = jnp.where(fresh[:, None], jnp.exp(log_group), 0.0)
    return inner + reach[:, :, None] * carried

def block_out(b_proj, c_proj, step_size, discrete, value_rows, start_state, decay_rate, skip, segment):
    tokens, heads = step_size.shape
    per_group = heads // GROUPS
    log_decay = jnp.cumsum(-decay_rate[None, :] * step_size, axis=0)
    position = jnp.arange(tokens)
    valid = (position[None, :] <= position[:, None]) & (segment[:, None] == segment[None, :])
    fresh = segment == 0
    state_three = start_state.reshape(heads, HEAD_DIM, STATE)
    pieces = []
    for which in range(GROUPS):
        first_head = which * per_group
        last_head = first_head + per_group
        pieces.append(jax.checkpoint(group_terms)(c_proj[:, which], b_proj[:, which], log_decay[:, first_head:last_head], discrete[:, first_head:last_head], state_three[first_head:last_head], valid, fresh))
    return jnp.concatenate(pieces, axis=1) + skip[None, :, None] * value_rows.astype(jnp.float32)

def reference(inputs, values, cotangent, weight, init_state, resets, dt_bias, decay_rate, skip):
    width = GROUPS * STATE
    blocks = LENGTH // TOK_DEV

    def one_stream(packed):
        rows, vals, cots, first, flags = packed
        proj = jnp.dot(rows, weight, preferred_element_type=jnp.float32)
        b_all = proj[:, :width].astype(jnp.bfloat16).reshape(LENGTH, GROUPS, STATE)
        c_all = proj[:, width:2 * width].astype(jnp.bfloat16).reshape(LENGTH, GROUPS, STATE)
        raw_step = proj[:, 2 * width:]
        value_rows = vals.reshape(LENGTH, HEADS, HEAD_DIM)
        segment = jnp.cumsum(flags.reshape(blocks, TOK_DEV), axis=1).astype(jnp.int32)

        def forward(b_in, c_in, raw_in, val_in):
            step_all, disc_all = prepare(raw_in, val_in, dt_bias)

            def advance(state, piece):
                b_blk, c_blk, step_blk, disc_blk, val_blk, seg_blk = piece
                total, local = block_stats(b_blk, step_blk, disc_blk, decay_rate, seg_blk)
                heads_out = block_out(b_blk, c_blk, step_blk, disc_blk, val_blk, state, decay_rate, skip, seg_blk)
                return (total[:, None] * state + local, heads_out)
            pieces = (b_in.reshape(blocks, TOK_DEV, GROUPS, STATE), c_in.reshape(blocks, TOK_DEV, GROUPS, STATE), step_all.reshape(blocks, TOK_DEV, HEADS), disc_all.reshape(blocks, TOK_DEV, HEADS, HEAD_DIM), val_in.reshape(blocks, TOK_DEV, HEADS, HEAD_DIM), segment)
            _, outs = lax.scan(jax.checkpoint(advance), first.astype(jnp.float32), pieces)
            return outs.reshape(LENGTH, HEADS, HEAD_DIM)
        _, pullback = jax.vjp(forward, b_all, c_all, raw_step, value_rows)
        d_b, d_c, d_raw, d_val = pullback(cots.reshape(LENGTH, HEADS, HEAD_DIM).astype(jnp.float32))
        d_proj = jnp.concatenate([d_b.reshape(LENGTH, width), d_c.reshape(LENGTH, width), d_raw.astype(jnp.bfloat16)], axis=1)
        grad_in = jnp.dot(d_proj, weight.T, preferred_element_type=jnp.float32).astype(jnp.bfloat16)
        grad_w = jnp.dot(rows.T, d_proj, preferred_element_type=jnp.float32)
        return (grad_in, d_val.reshape(LENGTH, HEADS * HEAD_DIM), grad_w)
    grad_in, grad_vals, grad_w = lax.map(one_stream, (inputs, values, cotangent, init_state, resets))
    scale = 1.0 / math.sqrt(STREAMS * LENGTH)
    return (grad_in, grad_vals, lax.optimization_barrier(jnp.sum(grad_w, axis=0)) * scale)
```

```python
import functools
import math

import jax
import jax.numpy as jnp
from jax import lax
from jax.experimental import pallas as pl
from jax.experimental.pallas import tpu as pltpu
from jax.sharding import PartitionSpec as P

MESH = pl.DeviceIdType.MESH
F32 = jnp.float32
BF16 = jnp.bfloat16
TOK = 128
HEADS = 128
GROUPS = 8
STATE = 64
WIDE = 1024
COLS = 1152
MSG = 144
OWN = 256
VMEM = pl.BlockSpec(memory_space=pltpu.VMEM)


def nn(a, b):
    return lax.dot_general(a, b, (((1,), (0,)), ((), ())), preferred_element_type=F32)


def nt(a, b):
    return lax.dot_general(a, b, (((1,), (1,)), ((), ())), preferred_element_type=F32)


def tn(a, b):
    return lax.dot_general(a, b, (((0,), (0,)), ((), ())), preferred_element_type=F32)


def split2(x):
    high = x.astype(BF16)
    return high, (x - high.astype(F32)).astype(BF16)


def split3(x):
    high, rest = x.astype(BF16), None
    rest = x - high.astype(F32)
    mid = rest.astype(BF16)
    return high, mid, (rest - mid.astype(F32)).astype(BF16)


def exact(mat, x):
    return sum(nn(mat, part) for part in split3(x))


def remote(src, dst, ssem, rsem, to):
    return pltpu.make_async_remote_copy(
        src_ref=src, dst_ref=dst, send_sem=ssem, recv_sem=rsem, device_id=to, device_id_type=MESH
    )


def project_kernel(x_ref, w_ref, b_ref, c_ref, raw_ref, wsib_ref, xr_ref, xs_ref,
                   part_bc, part_raw, got_bc, got_raw, ssem, rsem):
    me, f = lax.axis_index("ctx"), lax.axis_index("fsdp")
    core = lax.rem(f, 2)
    chip = f // 2
    sib = (me, f + 1 - 2 * core)
    far = (me, lax.rem(f + 2, 4))
    bar = pltpu.get_barrier_semaphore()
    for to in (sib, far):
        pl.semaphore_signal(bar, inc=1, device_id=to, device_id_type=MESH)
    pl.semaphore_wait(bar, 2)
    send_x = remote(x_ref.at[:, pl.ds(pl.multiple_of((1 - chip) * 2048, 2048), 2048)], xr_ref,
                    ssem.at[0], rsem.at[0], far)
    send_x.start()
    send_w = remote(w_ref, wsib_ref, ssem.at[1], rsem.at[1], sib)
    send_w.start()
    mine = pl.multiple_of(core * 1024, 1024)
    other = pl.multiple_of((1 - core) * 1024, 1024)
    base = chip * 2048
    send_xo = remote(x_ref.at[:, pl.ds(pl.multiple_of(base + other, 1024), 1024)], xs_ref.at[0],
                     ssem.at[2], rsem.at[2], sib)
    send_xo.start()
    own = nn(x_ref[:, pl.ds(pl.multiple_of(base + mine, 1024), 1024)], w_ref[...])
    send_w.wait_recv()
    own += nn(x_ref[:, pl.ds(pl.multiple_of(base + other, 1024), 1024)], wsib_ref[...])
    send_x.wait_recv()
    send_xr = remote(xr_ref.at[:, pl.ds(other, 1024)], xs_ref.at[1], ssem.at[3], rsem.at[3], sib)
    send_xr.start()
    away = nn(xr_ref[:, pl.ds(mine, 1024)], w_ref[...]) + nn(xr_ref[:, pl.ds(other, 1024)], wsib_ref[...])
    part_bc[...] = away[:, :1024].astype(BF16)
    part_raw[...] = away[:, 1024:]
    send_bc = remote(part_bc, got_bc, ssem.at[4], rsem.at[4], far)
    send_bc.start()
    send_raw = remote(part_raw, got_raw, ssem.at[5], rsem.at[5], far)
    send_raw.start()
    send_bc.wait_recv()
    send_raw.wait_recv()
    full = (own[:, :1024] + got_bc[...].astype(F32)).astype(BF16)
    for g in range(GROUPS):
        b_ref[g] = full[:, g * STATE:(g + 1) * STATE]
        c_ref[g] = full[:, 512 + g * STATE:512 + (g + 1) * STATE]
    raw_ref[...] = own[:, 1024:] + got_raw[...]
    for one in (send_xo, send_xr):
        one.wait_recv()
    for one in (send_x, send_w, send_xo, send_xr, send_bc, send_raw):
        one.wait_send()


def project(x, w):
    shapes = (
        jax.ShapeDtypeStruct((GROUPS, TOK, STATE), BF16),
        jax.ShapeDtypeStruct((GROUPS, TOK, STATE), BF16),
        jax.ShapeDtypeStruct((TOK, HEADS), F32),
        jax.ShapeDtypeStruct((1024, COLS), BF16),
        jax.ShapeDtypeStruct((TOK, 2048), BF16),
        jax.ShapeDtypeStruct((2, TOK, 1024), BF16),
    )
    return pl.pallas_call(
        project_kernel,
        out_shape=shapes,
        in_specs=[VMEM] * 2,
        out_specs=[VMEM] * 6,
        scratch_shapes=[
            pltpu.VMEM((TOK, 1024), BF16),
            pltpu.VMEM((TOK, HEADS), F32),
            pltpu.VMEM((TOK, 1024), BF16),
            pltpu.VMEM((TOK, HEADS), F32),
            pltpu.SemaphoreType.DMA((6,)),
            pltpu.SemaphoreType.DMA((6,)),
        ],
        compiler_params=pltpu.CompilerParams(
            collective_id=0, has_side_effects=True, vmem_limit_bytes=48 * 2**20
        ),
        name="project",
    )(x, w)


def block_masks(resets_ref):
    flags = resets_ref[...].astype(F32)
    row = lax.broadcasted_iota(jnp.int32, (TOK, TOK), 0)
    col = lax.broadcasted_iota(jnp.int32, (TOK, TOK), 1)
    seg_col = jnp.sum(jnp.where(col <= row, flags, 0.0), axis=1, keepdims=True)
    flag_col = jnp.sum(jnp.where(col == row, flags, 0.0), axis=1, keepdims=True)
    seg_row = jnp.sum(jnp.where(row <= col, flag_col, 0.0), axis=0, keepdims=True)
    valid = (col <= row) & (seg_col == seg_row)
    return row, col, valid, seg_col


def spread_matrix(g):
    head = lax.rem(lax.broadcasted_iota(jnp.int32, (256, WIDE), 0), 128)
    lane = lax.broadcasted_iota(jnp.int32, (256, WIDE), 1) // STATE
    return jnp.where(head == lane + 16 * g, 1.0, 0.0).astype(BF16)


def gather_matrix(g):
    lane = lax.broadcasted_iota(jnp.int32, (WIDE, HEADS), 0) // STATE
    head = lax.broadcasted_iota(jnp.int32, (WIDE, HEADS), 1)
    return jnp.where(head == lane + 16 * g, 1.0, 0.0).astype(BF16)


def per_head(x, mat):
    high, low = split2(x)
    return nn(high, mat) + nn(low, mat)


def states_kernel(b_ref, c_ref, raw_ref, val_ref, cot_ref, resets_ref, bias_ref, rate_ref, skip_ref,
                  init_ref, dproj_ref, gval_ref,
                  disc_ref, wgt_ref, rc_ref, step_ref, skipx_ref, totx_ref, dd_ref, logt_ref, logd_ref,
                  dlog_ref, dstep_ref, db_ref, dc_ref, out_ref, in_ref, back_ref, home_ref,
                  s1, r1, s2, r2, lsem):
    n = lax.axis_size("ctx")
    me, f = lax.axis_index("ctx"), lax.axis_index("fsdp")
    my_row, my_x = me // 4, lax.rem(me, 4)
    bar = pltpu.get_barrier_semaphore()

    def greet(i, carry):
        pl.semaphore_signal(bar, inc=1, device_id=(lax.rem(me + i, n), f), device_id_type=MESH)
        return carry

    lax.fori_loop(1, n, greet, 0)
    row, col, valid, seg_col = block_masks(resets_ref)
    raw = raw_ref[...] + bias_ref[...]
    step = jnp.maximum(raw, 0.0) + jnp.log1p(jnp.exp(-jnp.abs(raw)))
    low_tri = jnp.where(col <= row, 1.0, 0.0).astype(BF16)
    log_decay = exact(low_tri, -rate_ref[...] * step)
    final = log_decay[TOK - 1:, :]
    last_seg = seg_col[TOK - 1:, :]
    tail = jnp.where(seg_col == last_seg, jnp.exp(final - log_decay), 0.0)
    reach = jnp.where(seg_col == 0.0, jnp.exp(log_decay), 0.0)
    total = jnp.where(last_seg == 0.0, jnp.exp(final), 0.0)
    logd_ref[...] = log_decay
    logt_ref[...] = jnp.transpose(log_decay)
    few = lax.broadcasted_iota(jnp.int32, (16, HEADS), 0)
    extra = jnp.where(few < 8, skip_ref[...], total)
    stack = jnp.concatenate([step, tail, reach, extra], axis=0)
    stack = jnp.concatenate(split2(stack), axis=1)
    pl.semaphore_wait(bar, n - 1)

    def wide(g):
        return pl.ds(pl.multiple_of(g * WIDE, WIDE), WIDE)

    def out_copy(to):
        return remote(out_ref.at[to], in_ref.at[me], s1.at[to], r1.at[me], (to, f))

    def own_copy():
        return pltpu.make_async_copy(out_ref.at[me], in_ref.at[me], lsem)

    def produce(i, carry):
        g = lax.rem(my_row + i, GROUPS)
        spread = nn(stack, spread_matrix(g))
        step_x = spread[:TOK]
        cot = cot_ref[:, wide(g)].astype(F32)
        disc = (step_x * val_ref[:, wide(g)].astype(F32)).astype(BF16)
        wgt = (spread[TOK:2 * TOK] * disc.astype(F32)).astype(BF16)
        rc = (spread[2 * TOK:3 * TOK] * cot).astype(BF16)
        step_ref[g] = step_x
        skipx_ref[g] = spread[3 * TOK:3 * TOK + 8]
        totx_ref[g] = spread[3 * TOK + 8:3 * TOK + 16]
        disc_ref[g] = disc
        wgt_ref[g] = wgt
        rc_ref[g] = rc
        local = tn(b_ref[g], wgt).astype(BF16)
        first = tn(c_ref[g], rc).astype(BF16)
        tot = spread[3 * TOK + 8:3 * TOK + 9]
        high, low = split2(tot)
        which = lax.broadcasted_iota(jnp.int32, (16, WIDE), 0)
        tots = jnp.where(which == 0, high.astype(F32), jnp.where(which == 1, low.astype(F32), 0.0)).astype(BF16)
        for j in range(4):
            to = g * 4 + j
            lanes = slice(j * OWN, (j + 1) * OWN)
            out_ref[to, :64, :] = local[:, lanes]
            out_ref[to, 64:128, :] = first[:, lanes]
            out_ref[to, 128:, :] = tots[:, lanes]
        for j in range(4):
            to = g * 4 + lax.rem(my_x + j, 4)

            @pl.when(to != me)
            def _():
                out_copy(to).start()

            @pl.when(to == me)
            def _():
                own_copy().start()

        return carry

    lax.fori_loop(0, GROUPS, produce, 0)

    dlog_ref[...] = jnp.zeros_like(dlog_ref)
    half = lax.broadcasted_iota(jnp.int32, (1, TOK), 1) < STATE
    left = jnp.where(half, 1.0, 0.0)
    left_b = left.astype(BF16)
    right_b = (1.0 - left).astype(BF16)
    bad = jnp.where(valid, 0.0, 1.0)

    def inside(g, carry):
        b, c = b_ref[g], c_ref[g]
        scores = nt(c, b)
        logs = pltpu.roll(logd_ref[...], lax.rem(HEADS - 16 * g, HEADS), 1)
        d_scores = jnp.zeros((TOK, TOK), F32)
        errs = []
        for q in range(8):
            lanes = pl.ds(pl.multiple_of(g * WIDE + q * 128, 128), 128)
            cot_p = cot_ref[:, lanes]
            disc_p = disc_ref[g, :, q * 128:(q + 1) * 128]
            stacked = jnp.concatenate([disc_p * left_b, disc_p * right_b], axis=0)
            d_mixed = nt(cot_p, stacked)
            mixed = []
            for k in range(2):
                head = 2 * q + k
                span = logs[:, head:head + 1] - logt_ref[pl.ds(g * 16 + head, 1), :]
                weights = jnp.exp(jnp.where(valid, span, -1e30))
                d_scores += d_mixed[:, k * TOK:(k + 1) * TOK] * weights
                mixed.append((weights * scores).astype(BF16))
            mixed = jnp.concatenate(mixed, axis=1)
            inner = nn(mixed, stacked)
            both = tn(mixed, cot_p)
            dd = both[:TOK] * left + both[TOK:] * (1.0 - left)
            dd_ref[g, :, q * 128:(q + 1) * 128] = dd.astype(BF16)
            errs.append(cot_p.astype(F32) * inner - disc_p.astype(F32) * dd)
        dlog_ref[...] += per_head(jnp.concatenate(errs, axis=1), gather_matrix(g))
        ds = d_scores.astype(BF16)
        dc_ref[g] = nn(ds, b)
        db_ref[g] = tn(ds, c)
        return carry

    lax.fori_loop(0, GROUPS, inside, 0)

    own_copy().wait()

    def arrive(i, carry):
        src = lax.rem(me + n - i, n)
        remote(out_ref.at[src], in_ref.at[src], s1.at[src], r1.at[src], (src, f)).wait_recv()
        return carry

    lax.fori_loop(1, n, arrive, 0)

    def lap_total(j):
        return jnp.sum(in_ref[j, 128:, :].astype(F32), axis=0, keepdims=True)

    def forward(j, state):
        back_ref[j, :64, :] = state.astype(BF16)
        return lap_total(j) * state + in_ref[j, :64, :].astype(F32)

    lax.fori_loop(0, n, forward, init_ref[...].astype(F32))

    def backward(i, state):
        j = n - 1 - i
        back_ref[j, 64:, :] = state.astype(BF16)
        return in_ref[j, 64:128, :].astype(F32) + lap_total(j) * state

    lax.fori_loop(0, n, backward, jnp.zeros((STATE, OWN), F32))

    def back_copy(to):
        return remote(back_ref.at[to], home_ref.at[me], s2.at[to], r2.at[me], (to, f))

    def own_back():
        return pltpu.make_async_copy(back_ref.at[me], home_ref.at[me], lsem)

    own_back().start()

    def send_back(i, carry):
        back_copy(lax.rem(me + i, n)).start()
        return carry

    lax.fori_loop(1, n, send_back, 0)
    own_back().wait()
    dstep_ref[...] = jnp.zeros_like(dstep_ref)

    def consume(i, carry):
        g = lax.rem(my_row + GROUPS - i, GROUPS)
        for j in range(4):
            src = g * 4 + j

            @pl.when(src != me)
            def _():
                remote(back_ref.at[src], home_ref.at[src], s2.at[src], r2.at[src], (src, f)).wait_recv()

        got = jnp.concatenate([home_ref[g * 4 + j] for j in range(4)], axis=1)
        start, end = got[:64], got[64:]
        b, c = b_ref[g], c_ref[g]
        rc, wgt, disc = rc_ref[g], wgt_ref[g], disc_ref[g].astype(F32)
        carried = nn(c, start)
        d_wgt = nn(b, end)
        dc_ref[g] += nt(rc, start)
        db_ref[g] += nt(wgt, end)
        pull = wgt.astype(F32) * d_wgt
        mat = gather_matrix(g)
        err = rc.astype(F32) * carried - pull
        ends = jnp.sum(pull, axis=0, keepdims=True)
        ends += totx_ref[g, :1, :] * jnp.sum(start.astype(F32) * end.astype(F32), axis=0, keepdims=True)
        at_end = lax.broadcasted_iota(jnp.int32, (TOK, WIDE), 0) == TOK - 1
        err = err + jnp.where(at_end, ends, 0.0)
        dlog_ref[...] += per_head(err, mat)
        spread = nn(stack[TOK:2 * TOK], spread_matrix(g))
        d_disc = dd_ref[g].astype(F32) + spread * d_wgt
        val = val_ref[:, wide(g)].astype(F32)
        dstep_ref[...] += per_head(d_disc * val, mat)
        gval = skipx_ref[g, :1, :] * cot_ref[:, wide(g)].astype(F32) + step_ref[g] * d_disc
        gval_ref[:, wide(g)] = gval.astype(BF16)
        return carry

    lax.fori_loop(0, GROUPS, consume, 0)
    up_tri = jnp.where(col >= row, 1.0, 0.0).astype(BF16)
    d_inc = exact(up_tri, dlog_ref[...])
    d_step = dstep_ref[...] - rate_ref[...] * d_inc
    d_raw = d_step / (1.0 + jnp.exp(-raw))
    pieces = [db_ref[g] for g in range(GROUPS)] + [dc_ref[g] for g in range(GROUPS)] + [d_raw]
    dproj_ref[...] = jnp.concatenate(pieces, axis=1).astype(BF16)

    def drain(i, carry):
        to = lax.rem(me + i, n)
        out_copy(to).wait_send()
        back_copy(to).wait_send()
        return carry

    lax.fori_loop(1, n, drain, 0)


def states(b, c, raw, val, cot, resets, bias, rate, skip, init):
    n = 32
    slab = (GROUPS, TOK, WIDE)
    return pl.pallas_call(
        states_kernel,
        out_shape=(
            jax.ShapeDtypeStruct((TOK, COLS), BF16),
            jax.ShapeDtypeStruct((TOK, GROUPS * WIDE), BF16),
        ),
        in_specs=[VMEM] * 10,
        out_specs=[VMEM] * 2,
        scratch_shapes=[
            pltpu.VMEM(slab, BF16),
            pltpu.VMEM(slab, BF16),
            pltpu.VMEM(slab, BF16),
            pltpu.VMEM(slab, F32),
            pltpu.VMEM((GROUPS, 8, WIDE), F32),
            pltpu.VMEM((GROUPS, 8, WIDE), F32),
            pltpu.VMEM(slab, BF16),
            pltpu.VMEM((HEADS, TOK), F32),
            pltpu.VMEM((TOK, HEADS), F32),
            pltpu.VMEM((TOK, HEADS), F32),
            pltpu.VMEM((TOK, HEADS), F32),
            pltpu.VMEM((GROUPS, TOK, STATE), F32),
            pltpu.VMEM((GROUPS, TOK, STATE), F32),
            pltpu.VMEM((n, MSG, OWN), BF16),
            pltpu.VMEM((n, MSG, OWN), BF16),
            pltpu.VMEM((n, 128, OWN), BF16),
            pltpu.VMEM((n, 128, OWN), BF16),
            pltpu.SemaphoreType.DMA((n,)),
            pltpu.SemaphoreType.DMA((n,)),
            pltpu.SemaphoreType.DMA((n,)),
            pltpu.SemaphoreType.DMA((n,)),
            pltpu.SemaphoreType.DMA,
        ],
        compiler_params=pltpu.CompilerParams(
            collective_id=1, has_side_effects=True, vmem_limit_bytes=56 * 2**20
        ),
        name="states",
    )(b, c, raw, val, cot, resets, bias, rate, skip, init)


def grads_kernel(scale, dp_ref, x_ref, xr_ref, xs_ref, w_ref, wsib_ref, gin_ref, gw_ref,
                 dps, away, gin_in, part, got, mine_b, full, ssem, rsem, s1, r1, s2, r2, lsem):
    n = lax.axis_size("ctx")
    me, f = lax.axis_index("ctx"), lax.axis_index("fsdp")
    core, chip = lax.rem(f, 2), f // 2
    sib = (me, f + 1 - 2 * core)
    far = (me, lax.rem(f + 2, 4))
    bar = pltpu.get_barrier_semaphore()
    for to in (sib, far):
        pl.semaphore_signal(bar, inc=1, device_id=to, device_id_type=MESH)

    def greet(i, carry):
        pl.semaphore_signal(bar, inc=1, device_id=(lax.rem(me + i, n), f), device_id_type=MESH)
        return carry

    lax.fori_loop(1, n, greet, 0)
    pl.semaphore_wait(bar, n + 1)
    send_far = remote(dp_ref, dps.at[0], ssem.at[0], rsem.at[0], far)
    send_far.start()
    send_sib = remote(dp_ref, dps.at[1], ssem.at[1], rsem.at[1], sib)
    send_sib.start()
    mine = pl.multiple_of(core * 1024, 1024)
    other = pl.multiple_of((1 - core) * 1024, 1024)
    base = chip * 2048
    own_at = pl.multiple_of(base + mine, 1024)
    other_at = pl.multiple_of(base + other, 1024)
    gin_ref[:, pl.ds(own_at, 1024)] = nt(dp_ref[...], w_ref[...]).astype(BF16)
    gin_ref[:, pl.ds(other_at, 1024)] = nt(dp_ref[...], wsib_ref[...]).astype(BF16)
    send_far.wait_recv()
    send_fwd = remote(dps.at[0], dps.at[2], ssem.at[2], rsem.at[2], sib)
    send_fwd.start()
    away[:, pl.ds(mine, 1024)] = nt(dps[0], w_ref[...]).astype(BF16)
    away[:, pl.ds(other, 1024)] = nt(dps[0], wsib_ref[...]).astype(BF16)
    send_gin = remote(away, gin_in, ssem.at[3], rsem.at[3], far)
    send_sib.wait_recv()
    send_fwd.wait_recv()
    xa = x_ref[:, pl.ds(own_at, 1024)]
    xb = xr_ref[:, pl.ds(mine, 1024)]
    xall = jnp.concatenate([xa, xb, xs_ref[0], xs_ref[1]], axis=0)
    dall = jnp.concatenate([dp_ref[...], dps[0], dps[1], dps[2]], axis=0)
    part[...] = tn(xall, dall).astype(BF16)

    def rows(k):
        return pl.ds(pl.multiple_of(k * 32, 32), 32)

    def out_copy(to):
        return remote(part.at[rows(to), :], got.at[me], s1.at[to], r1.at[me], (to, f))

    def own_copy():
        return pltpu.make_async_copy(part.at[rows(me), :], got.at[me], lsem)

    own_copy().start()

    def send(i, carry):
        out_copy(lax.rem(me + i, n)).start()
        return carry

    lax.fori_loop(1, n, send, 0)
    send_gin.start()
    own_copy().wait()

    def collect(i, total):
        src = lax.rem(me + n - i, n)
        remote(part.at[rows(src), :], got.at[src], s1.at[src], r1.at[src], (src, f)).wait_recv()
        return total + got[src].astype(F32)

    total = lax.fori_loop(1, n, collect, got[me].astype(F32))
    mine_b[...] = total.astype(BF16)
    full[rows(me), :] = mine_b[...]

    def share_copy(to):
        return remote(mine_b, full.at[rows(me), :], s2.at[to], r2.at[me], (to, f))

    def share(i, carry):
        share_copy(lax.rem(me + i, n)).start()
        return carry

    lax.fori_loop(1, n, share, 0)
    send_gin.wait_recv()
    gin_ref[:, pl.ds(pl.multiple_of((1 - chip) * 2048, 2048), 2048)] = gin_in[...]
    gw_ref[rows(me), :] = full[rows(me), :].astype(F32) * scale

    def take(i, carry):
        src = lax.rem(me + n - i, n)
        remote(mine_b, full.at[rows(src), :], s2.at[src], r2.at[src], (src, f)).wait_recv()
        gw_ref[rows(src), :] = full[rows(src), :].astype(F32) * scale
        return carry

    lax.fori_loop(1, n, take, 0)

    def drain(i, carry):
        to = lax.rem(me + i, n)
        out_copy(to).wait_send()
        share_copy(to).wait_send()
        return carry

    lax.fori_loop(1, n, drain, 0)
    for one in (send_far, send_sib, send_fwd, send_gin):
        one.wait_send()


def grads(scale, dp, x, xr, xs, w, wsib):
    n = 32
    return pl.pallas_call(
        functools.partial(grads_kernel, scale),
        out_shape=(
            jax.ShapeDtypeStruct((TOK, 4096), BF16),
            jax.ShapeDtypeStruct((1024, COLS), F32),
        ),
        in_specs=[VMEM] * 6,
        out_specs=[VMEM] * 2,
        scratch_shapes=[
            pltpu.VMEM((3, TOK, COLS), BF16),
            pltpu.VMEM((TOK, 2048), BF16),
            pltpu.VMEM((TOK, 2048), BF16),
            pltpu.VMEM((1024, COLS), BF16),
            pltpu.VMEM((n, 32, COLS), BF16),
            pltpu.VMEM((32, COLS), BF16),
            pltpu.VMEM((1024, COLS), BF16),
            pltpu.SemaphoreType.DMA((4,)),
            pltpu.SemaphoreType.DMA((4,)),
            pltpu.SemaphoreType.DMA((n,)),
            pltpu.SemaphoreType.DMA((n,)),
            pltpu.SemaphoreType.DMA((n,)),
            pltpu.SemaphoreType.DMA((n,)),
            pltpu.SemaphoreType.DMA,
        ],
        compiler_params=pltpu.CompilerParams(
            collective_id=2, has_side_effects=True, vmem_limit_bytes=56 * 2**20
        ),
        name="grads",
    )(dp, x, xr, xs, w, wsib)


def body(inputs, values, cotangent, weight, init_state, resets, dt_bias, decay_rate, skip):
    x = inputs[0]
    me = lax.axis_index("ctx")
    n = lax.axis_size("ctx")
    scale = 1.0 / math.sqrt(lax.axis_size("fsdp") * TOK * n)
    first = lax.dynamic_slice_in_dim(init_state[0], me * 4, 4, 0)
    first = first.reshape(OWN, STATE).T
    b, c, raw, wsib, xr, xs = project(x, weight)
    dp, gval = states(b, c, raw, values[0], cotangent[0], resets, dt_bias[None], decay_rate[None], skip[None], first)
    gin, gw = grads(scale, dp, x, xr, xs, weight, wsib)
    return (gin[None], gval[None], gw)


def solution(mesh):
    in_specs = (
        P("fsdp", "ctx", None),
        P("fsdp", "ctx", None),
        P("fsdp", "ctx", None),
        P("fsdp", None),
        P("fsdp", None, None),
        P("fsdp", "ctx"),
        P(),
        P(),
        P(),
    )
    out_specs = (P("fsdp", "ctx", None), P("fsdp", "ctx", None), P("fsdp", None))
    return jax.shard_map(body, mesh=mesh, in_specs=in_specs, out_specs=out_specs, check_vma=False)
```

```python
import functools
import math

import jax
import jax.numpy as jnp
from jax import lax
from jax.experimental import pallas as pl
from jax.experimental.pallas import tpu as pltpu
from jax.sharding import PartitionSpec as P

MESH = pl.DeviceIdType.MESH
F32 = jnp.float32
BF16 = jnp.bfloat16
TOK = 128
HEADS = 128
GROUPS = 8
STATE = 64
WIDE = 1024
COLS = 1152
MSG = 144
OWN = 256
VMEM = pl.BlockSpec(memory_space=pltpu.VMEM)


def nn(a, b):
    return lax.dot_general(a, b, (((1,), (0,)), ((), ())), preferred_element_type=F32)


def nt(a, b):
    return lax.dot_general(a, b, (((1,), (1,)), ((), ())), preferred_element_type=F32)


def tn(a, b):
    return lax.dot_general(a, b, (((0,), (0,)), ((), ())), preferred_element_type=F32)


def split2(x):
    high = x.astype(BF16)
    return high, (x - high.astype(F32)).astype(BF16)


def split3(x):
    high, rest = x.astype(BF16), None
    rest = x - high.astype(F32)
    mid = rest.astype(BF16)
    return high, mid, (rest - mid.astype(F32)).astype(BF16)


def exact(mat, x):
    return sum(nn(mat, part) for part in split3(x))


def remote(src, dst, ssem, rsem, to):
    return pltpu.make_async_remote_copy(
        src_ref=src, dst_ref=dst, send_sem=ssem, recv_sem=rsem, device_id=to, device_id_type=MESH
    )


def block_masks(resets_ref):
    flags = resets_ref[...].astype(F32)
    row = lax.broadcasted_iota(jnp.int32, (TOK, TOK), 0)
    col = lax.broadcasted_iota(jnp.int32, (TOK, TOK), 1)
    seg_col = jnp.sum(jnp.where(col <= row, flags, 0.0), axis=1, keepdims=True)
    flag_col = jnp.sum(jnp.where(col == row, flags, 0.0), axis=1, keepdims=True)
    seg_row = jnp.sum(jnp.where(row <= col, flag_col, 0.0), axis=0, keepdims=True)
    valid = (col <= row) & (seg_col == seg_row)
    return row, col, valid, seg_col


def spread_matrix(g):
    head = lax.rem(lax.broadcasted_iota(jnp.int32, (256, WIDE), 0), 128)
    lane = lax.broadcasted_iota(jnp.int32, (256, WIDE), 1) // STATE
    return jnp.where(head == lane + 16 * g, 1.0, 0.0).astype(BF16)


def gather_matrix(g):
    lane = lax.broadcasted_iota(jnp.int32, (WIDE, HEADS), 0) // STATE
    head = lax.broadcasted_iota(jnp.int32, (WIDE, HEADS), 1)
    return jnp.where(head == lane + 16 * g, 1.0, 0.0).astype(BF16)


def per_head(x, mat):
    high, low = split2(x)
    return nn(high, mat) + nn(low, mat)


def layer_kernel(x_hbm, w_hbm, val_hbm, cot_hbm, init_hbm, resets_ref, bias_ref, rate_ref, skip_ref,
                 gin_hbm, gval_hbm, gw_hbm,
                 x_ref, w_ref, wsib_ref, xall, xo_ref, own_ref, away_ref, put_b, put_c, put_raw,
                 got_b, got_c, got_raw, b_ref, c_ref, val_ref, cot_ref, init_ref,
                 disc_ref, wgt_ref, rc_ref, step_ref, skipx_ref, totx_ref, dd_ref, logt_ref, logd_ref,
                 dlog_ref, dstep_ref, db_ref, dc_ref, out_ref, in_ref, back_ref, home_ref,
                 dall, gin_ref, ginfar_ref, part, ra1, rb1, a1, b1, ra2, rb2, s3, r3, f3, g3, a32, b32, a128, b128,
                 ssem, rsem, lsem, s1, r1, s2, r2):
    n = lax.axis_size("ctx")
    me, f = lax.axis_index("ctx"), lax.axis_index("fsdp")
    core, chip = lax.rem(f, 2), f // 2
    my_row, my_x = me // 4, lax.rem(me, 4)
    my_z, my_y = lax.rem(my_row, 4), my_row // 4
    sib = (me, f + 1 - 2 * core)
    far = (me, lax.rem(f + 2, 4))
    pair = (lax.rem(me + 16, n), f)
    bar = pltpu.get_barrier_semaphore()
    for to in (far, sib):
        pl.semaphore_signal(bar, inc=1, device_id=to, device_id_type=MESH)

    def greet(i, carry):
        pl.semaphore_signal(bar, inc=1, device_id=(lax.rem(me + i, n), f), device_id_type=MESH)
        return carry

    lax.fori_loop(1, n, greet, 0)
    mine = pl.multiple_of(core * 1024, 1024)
    other = pl.multiple_of((1 - core) * 1024, 1024)
    base = pl.multiple_of(chip * 2048, 2048)
    far_base = pl.multiple_of((1 - chip) * 2048, 2048)
    own_at = pl.multiple_of(base + mine, 1024)
    other_at = pl.multiple_of(base + other, 1024)
    init_at = pl.multiple_of((me // 4) * 16, 16)
    loads = [
        pltpu.make_async_copy(w_hbm, w_ref, lsem.at[0]),
        pltpu.make_async_copy(x_hbm, x_ref, lsem.at[1]),
        pltpu.make_async_copy(cot_hbm, cot_ref, lsem.at[2]),
        pltpu.make_async_copy(val_hbm, val_ref, lsem.at[3]),
        pltpu.make_async_copy(init_hbm.at[pl.ds(init_at, 16), :], init_ref, lsem.at[4]),
    ]
    for one in loads:
        one.start()
    pl.semaphore_wait(bar, n + 1)

    def link(k, source, target, to):
        return remote(source, target, ssem.at[k], rsem.at[k], to)

    send_x0 = link(0, x_hbm.at[:, pl.ds(pl.multiple_of(far_base + mine, 1024), 1024)], xall.at[pl.ds(128, 128), :], far)
    send_x1 = link(1, x_hbm.at[:, pl.ds(pl.multiple_of(far_base + other, 1024), 1024)], xo_ref, far)
    send_w = link(2, w_hbm, wsib_ref, sib)
    send_xo = link(3, x_hbm.at[:, pl.ds(other_at, 1024)], xall.at[pl.ds(256, 128), :], sib)
    for one in (send_x0, send_x1, send_w, send_xo):
        one.start()
    row, col, valid, seg_col = block_masks(resets_ref)
    loads[0].wait()
    loads[1].wait()
    xall[:128, :] = x_ref[:, pl.ds(own_at, 1024)]
    own_ref[...] = nn(xall[:128, :], w_ref[...])
    send_w.wait_recv()
    own_ref[...] += nn(x_ref[:, pl.ds(other_at, 1024)], wsib_ref[...])
    send_x0.wait_recv()
    away_ref[...] = nn(xall[128:256, :], w_ref[...])
    send_x1.wait_recv()
    send_fwd = link(4, xo_ref, xall.at[pl.ds(384, 128), :], sib)
    send_fwd.start()
    put_raw[...] = away_ref[:, 1024:] + nn(xo_ref[...], wsib_ref[:, 1024:])
    send_raw = link(5, put_raw, got_raw, far)
    send_raw.start()
    put_b[...] = (away_ref[:, :512] + nn(xo_ref[...], wsib_ref[:, :512])).astype(BF16)
    send_b = link(6, put_b, got_b, far)
    send_b.start()
    put_c[...] = (away_ref[:, 512:1024] + nn(xo_ref[...], wsib_ref[:, 512:1024])).astype(BF16)
    send_c = link(7, put_c, got_c, far)
    send_c.start()

    send_raw.wait_recv()
    raw = own_ref[:, 1024:] + got_raw[...] + bias_ref[...]
    step = jnp.maximum(raw, 0.0) + jnp.log1p(jnp.exp(-jnp.abs(raw)))
    low_tri = jnp.where(col <= row, 1.0, 0.0).astype(BF16)
    log_decay = exact(low_tri, -rate_ref[...] * step)
    final = log_decay[TOK - 1:, :]
    last_seg = seg_col[TOK - 1:, :]
    tail = jnp.where(seg_col == last_seg, jnp.exp(final - log_decay), 0.0)
    reach = jnp.where(seg_col == 0.0, jnp.exp(log_decay), 0.0)
    total = jnp.where(last_seg == 0.0, jnp.exp(final), 0.0)
    logd_ref[...] = log_decay
    logt_ref[...] = jnp.transpose(log_decay)
    few = lax.broadcasted_iota(jnp.int32, (16, HEADS), 0)
    extra = jnp.where(few < 8, skip_ref[...], total)
    stack = jnp.concatenate([step, tail, reach, extra], axis=0)
    stack = jnp.concatenate(split2(stack), axis=1)
    loads[2].wait()
    loads[3].wait()
    send_b.wait_recv()
    full_b = (own_ref[:, :512] + got_b[...].astype(F32)).astype(BF16)
    for g in range(GROUPS):
        b_ref[g] = full_b[:, g * STATE:(g + 1) * STATE]
    send_c.wait_recv()
    full_c = (own_ref[:, 512:1024] + got_c[...].astype(F32)).astype(BF16)
    for g in range(GROUPS):
        c_ref[g] = full_c[:, g * STATE:(g + 1) * STATE]

    def wide(g):
        return pl.ds(pl.multiple_of(g * WIDE, WIDE), WIDE)

    def out_copy(to):
        return remote(out_ref.at[to], in_ref.at[me], s1.at[to], r1.at[me], (to, f))

    def own_copy():
        return pltpu.make_async_copy(out_ref.at[me], in_ref.at[me], lsem.at[5])

    def produce(i, carry):
        g = lax.rem(my_row + i, GROUPS)
        spread = nn(stack, spread_matrix(g))
        step_x = spread[:TOK]
        cot = cot_ref[:, wide(g)].astype(F32)
        disc = (step_x * val_ref[:, wide(g)].astype(F32)).astype(BF16)
        wgt = (spread[TOK:2 * TOK] * disc.astype(F32)).astype(BF16)
        rc = (spread[2 * TOK:3 * TOK] * cot).astype(BF16)
        step_ref[g] = step_x
        skipx_ref[g] = spread[3 * TOK:3 * TOK + 8]
        totx_ref[g] = spread[3 * TOK + 8:3 * TOK + 16]
        disc_ref[g] = disc
        wgt_ref[g] = wgt
        rc_ref[g] = rc
        local = tn(b_ref[g], wgt).astype(BF16)
        first = tn(c_ref[g], rc).astype(BF16)
        tot = spread[3 * TOK + 8:3 * TOK + 9]
        high, low = split2(tot)
        which = lax.broadcasted_iota(jnp.int32, (16, WIDE), 0)
        tots = jnp.where(which == 0, high.astype(F32), jnp.where(which == 1, low.astype(F32), 0.0)).astype(BF16)
        for j in range(4):
            to = g * 4 + j
            lanes = slice(j * OWN, (j + 1) * OWN)
            out_ref[to, :64, :] = local[:, lanes]
            out_ref[to, 64:128, :] = first[:, lanes]
            out_ref[to, 128:, :] = tots[:, lanes]
        for j in range(4):
            to = g * 4 + lax.rem(my_x + j, 4)

            @pl.when(to != me)
            def _():
                out_copy(to).start()

            @pl.when(to == me)
            def _():
                own_copy().start()

        return carry

    lax.fori_loop(0, GROUPS, produce, 0)

    dlog_ref[...] = jnp.zeros_like(dlog_ref)
    half = lax.broadcasted_iota(jnp.int32, (1, TOK), 1) < STATE
    left = jnp.where(half, 1.0, 0.0)
    left_b = left.astype(BF16)
    right_b = (1.0 - left).astype(BF16)
    bad = jnp.where(valid, 0.0, 1.0)

    def inside(g, carry):
        b, c = b_ref[g], c_ref[g]
        scores = nt(c, b)
        logs = pltpu.roll(logd_ref[...], lax.rem(HEADS - 16 * g, HEADS), 1)
        d_scores = jnp.zeros((TOK, TOK), F32)
        errs = []
        for q in range(8):
            lanes = pl.ds(pl.multiple_of(g * WIDE + q * 128, 128), 128)
            cot_p = cot_ref[:, lanes]
            disc_p = disc_ref[g, :, q * 128:(q + 1) * 128]
            stacked = jnp.concatenate([disc_p * left_b, disc_p * right_b], axis=0)
            d_mixed = nt(cot_p, stacked)
            mixed = []
            for k in range(2):
                head = 2 * q + k
                span = logs[:, head:head + 1] - logt_ref[pl.ds(g * 16 + head, 1), :]
                weights = jnp.exp(jnp.where(valid, span, -1e30))
                d_scores += d_mixed[:, k * TOK:(k + 1) * TOK] * weights
                mixed.append((weights * scores).astype(BF16))
            mixed = jnp.concatenate(mixed, axis=1)
            inner = nn(mixed, stacked)
            both = tn(mixed, cot_p)
            dd = both[:TOK] * left + both[TOK:] * (1.0 - left)
            dd_ref[g, :, q * 128:(q + 1) * 128] = dd.astype(BF16)
            errs.append(cot_p.astype(F32) * inner - disc_p.astype(F32) * dd)
        dlog_ref[...] += per_head(jnp.concatenate(errs, axis=1), gather_matrix(g))
        ds = d_scores.astype(BF16)
        dc_ref[g] = nn(ds, b)
        db_ref[g] = tn(ds, c)
        return carry

    lax.fori_loop(0, GROUPS, inside, 0)

    loads[4].wait()
    pick_row = lax.broadcasted_iota(jnp.int32, (16, 16), 0)
    pick_col = lax.broadcasted_iota(jnp.int32, (16, 16), 1)
    pick = jnp.where(pick_col == pick_row + 4 * my_x, 1.0, 0.0).astype(BF16)
    picked = nn(pick, init_ref[...])
    turned = [picked[h:h + 1, i * 128:(i + 1) * 128] for h in range(4) for i in range(32)]
    turned = jnp.transpose(jnp.concatenate(turned, axis=0)).astype(BF16)
    from_i = lax.broadcasted_iota(jnp.int32, (128, OWN), 0)
    to_p = lax.broadcasted_iota(jnp.int32, (128, OWN), 1)
    even = jnp.where(to_p == 2 * from_i, 1.0, 0.0).astype(BF16)
    odd = jnp.where(to_p == 2 * from_i + 1, 1.0, 0.0).astype(BF16)
    init_state = nn(turned[:64], even) + nn(turned[64:], odd)

    own_copy().wait()

    def arrive(i, carry):
        src = lax.rem(me + n - i, n)
        remote(out_ref.at[src], in_ref.at[src], s1.at[src], r1.at[src], (src, f)).wait_recv()
        return carry

    lax.fori_loop(1, n, arrive, 0)

    def lap_total(j):
        return jnp.sum(in_ref[j, 128:, :].astype(F32), axis=0, keepdims=True)

    def forward(j, state):
        back_ref[j, :64, :] = state.astype(BF16)
        return lap_total(j) * state + in_ref[j, :64, :].astype(F32)

    lax.fori_loop(0, n, forward, init_state)

    def backward(i, state):
        j = n - 1 - i
        back_ref[j, 64:, :] = state.astype(BF16)
        return in_ref[j, 64:128, :].astype(F32) + lap_total(j) * state

    lax.fori_loop(0, n, backward, jnp.zeros((STATE, OWN), F32))

    def back_copy(to):
        return remote(back_ref.at[to], home_ref.at[me], s2.at[to], r2.at[me], (to, f))

    def own_back():
        return pltpu.make_async_copy(back_ref.at[me], home_ref.at[me], lsem.at[6])

    def send_back(i, carry):
        g = lax.rem(my_row + i, GROUPS)
        for j in range(4):
            to = g * 4 + lax.rem(my_x + j, 4)

            @pl.when(to != me)
            def _():
                back_copy(to).start()

            @pl.when(to == me)
            def _():
                own_back().start()

        return carry

    lax.fori_loop(0, GROUPS, send_back, 0)
    own_back().wait()
    dstep_ref[...] = jnp.zeros_like(dstep_ref)

    def save(g):
        return pltpu.make_async_copy(disc_ref.at[g], gval_hbm.at[:, wide(g)], lsem.at[8 + g])

    def consume(i, carry):
        g = lax.rem(my_row + GROUPS - i, GROUPS)
        for j in range(4):
            src = g * 4 + j

            @pl.when(src != me)
            def _():
                remote(back_ref.at[src], home_ref.at[src], s2.at[src], r2.at[src], (src, f)).wait_recv()

        got = jnp.concatenate([home_ref[g * 4 + j] for j in range(4)], axis=1)
        start, end = got[:64], got[64:]
        b, c = b_ref[g], c_ref[g]
        rc, wgt, disc = rc_ref[g], wgt_ref[g], disc_ref[g].astype(F32)
        carried = nn(c, start)
        d_wgt = nn(b, end)
        dc_ref[g] += nt(rc, start)
        db_ref[g] += nt(wgt, end)
        pull = wgt.astype(F32) * d_wgt
        mat = gather_matrix(g)
        err = rc.astype(F32) * carried - pull
        ends = jnp.sum(pull, axis=0, keepdims=True)
        ends += totx_ref[g, :1, :] * jnp.sum(start.astype(F32) * end.astype(F32), axis=0, keepdims=True)
        at_end = lax.broadcasted_iota(jnp.int32, (TOK, WIDE), 0) == TOK - 1
        err = err + jnp.where(at_end, ends, 0.0)
        dlog_ref[...] += per_head(err, mat)
        spread = nn(stack[TOK:2 * TOK], spread_matrix(g))
        d_disc = dd_ref[g].astype(F32) + spread * d_wgt
        val = val_ref[:, wide(g)].astype(F32)
        dstep_ref[...] += per_head(d_disc * val, mat)
        gval = skipx_ref[g, :1, :] * cot_ref[:, wide(g)].astype(F32) + step_ref[g] * d_disc
        disc_ref[g] = gval.astype(BF16)
        save(g).start()
        return carry

    lax.fori_loop(0, GROUPS, consume, 0)
    up_tri = jnp.where(col >= row, 1.0, 0.0).astype(BF16)
    d_inc = exact(up_tri, dlog_ref[...])
    d_step = dstep_ref[...] - rate_ref[...] * d_inc
    d_raw = d_step / (1.0 + jnp.exp(-raw))
    pieces = [db_ref[g] for g in range(GROUPS)] + [dc_ref[g] for g in range(GROUPS)] + [d_raw]
    dall[:128, :] = jnp.concatenate(pieces, axis=1).astype(BF16)

    d_own = dall.at[pl.ds(0, 128), :]
    send_far = link(8, d_own, dall.at[pl.ds(128, 128), :], far)
    send_far.start()
    send_sib = link(9, d_own, dall.at[pl.ds(256, 128), :], sib)
    send_sib.start()
    gin_ref[:, pl.ds(mine, 1024)] = nt(dall[:128, :], w_ref[...]).astype(BF16)
    gin_ref[:, pl.ds(other, 1024)] = nt(dall[:128, :], wsib_ref[...]).astype(BF16)
    save_gin = pltpu.make_async_copy(gin_ref, gin_hbm.at[:, pl.ds(base, 2048)], lsem.at[7])
    save_gin.start()
    send_far.wait_recv()
    send_dfwd = link(10, dall.at[pl.ds(128, 128), :], dall.at[pl.ds(384, 128), :], sib)
    send_dfwd.start()
    send_xo.wait_recv()
    send_fwd.wait_recv()
    send_sib.wait_recv()
    send_dfwd.wait_recv()

    def rows(at, count):
        return pl.ds(pl.multiple_of(at, count), count)

    def x_peer(x):
        return (me - my_x + x, f)

    def z_peer(z):
        return (me + 4 * (z - my_z), f)

    def exchange(k, peer, mine_at, source, target):
        copies = []
        for step_to in range(1, 4):
            to = lax.rem(mine_at + step_to, 4)
            copies.append(remote(source(to), target(mine_at), ssem.at[k + to], rsem.at[k + mine_at], peer(to)))
        return copies

    def landed(k, peer, mine_at, source, target):
        for step_to in range(1, 4):
            at = lax.rem(mine_at + step_to, 4)
            remote(source(at), target(at), ssem.at[k + at], rsem.at[k + at], peer(at)).wait_recv()

    def product(at):
        part[rows(at, 128), :] = tn(xall[:, rows(at, 128)], dall[...]).astype(BF16)

    a_first = (12, x_peer, my_x, lambda x: part.at[rows(128 * x, 128), :], lambda x: ra1.at[x])
    b_first = (16, z_peer, my_z, lambda z: part.at[rows(512 + 128 * z, 128), :], lambda z: rb1.at[z])
    a_sent, b_sent = exchange(*a_first), exchange(*b_first)
    for k in range(3):
        product(128 * lax.rem(my_x + k + 1, 4))
        a_sent[k].start()
        product(512 + 128 * lax.rem(my_z + k + 1, 4))
        b_sent[k].start()
    product(128 * my_x)
    product(512 + 128 * my_z)
    ginfar_ref[:, pl.ds(mine, 1024)] = nt(dall[128:256, :], w_ref[...]).astype(BF16)
    ginfar_ref[:, pl.ds(other, 1024)] = nt(dall[128:256, :], wsib_ref[...]).astype(BF16)
    send_gin = link(11, ginfar_ref, gin_hbm.at[:, pl.ds(base, 2048)], far)
    send_gin.start()
    sent = a_sent + b_sent

    def summed(first, got, at):
        total = first.astype(F32)
        for step_to in range(1, 4):
            total += got[lax.rem(at + step_to, 4)].astype(F32)
        return total

    a_second = (20, z_peer, my_z, lambda z: a1.at[rows(32 * z, 32), :], lambda z: ra2.at[z])
    b_second = (24, x_peer, my_x, lambda x: b1.at[rows(32 * x, 32), :], lambda x: rb2.at[x])
    landed(*a_first)
    a1[...] = summed(part[rows(128 * my_x, 128), :], ra1, my_x).astype(BF16)
    a_sent = exchange(*a_second)
    for one in a_sent:
        one.start()
    landed(*b_first)
    b1[...] = summed(part[rows(512 + 128 * my_z, 128), :], rb1, my_z).astype(BF16)
    b_sent = exchange(*b_second)
    for one in b_sent:
        one.start()
    sent += a_sent + b_sent
    landed(*a_second)
    a2 = summed(a1[rows(32 * my_z, 32), :], ra2, my_z)
    landed(*b_second)
    b2 = summed(b1[rows(32 * my_x, 32), :], rb2, my_x)
    upper = jnp.where(my_y == 0, 1.0, 0.0)
    keep_a = a2[:16] * upper + a2[16:] * (1.0 - upper)
    keep_b = b2[:16] * upper + b2[16:] * (1.0 - upper)
    give_a = a2[:16] * (1.0 - upper) + a2[16:] * upper
    give_b = b2[:16] * (1.0 - upper) + b2[16:] * upper
    s3[...] = jnp.concatenate([give_a, give_b], axis=0).astype(BF16)
    third = link(28, s3, r3, pair)
    third.start()
    third.wait_recv()
    f3[...] = (jnp.concatenate([keep_a, keep_b], axis=0) + r3[...].astype(F32)).astype(BF16)
    fourth = link(29, f3, g3, pair)
    fourth.start()
    at_y, at_not = rows(16 * my_y, 16), rows(16 * (1 - my_y), 16)
    a32[at_y, :] = f3[:16, :]
    b32[at_y, :] = f3[16:, :]
    fourth.wait_recv()
    a32[at_not, :] = g3[:16, :]
    b32[at_not, :] = g3[16:, :]
    a_fifth = (30, z_peer, my_z, lambda z: a32, lambda z: a128.at[rows(32 * z, 32), :])
    b_fifth = (34, x_peer, my_x, lambda x: b32, lambda x: b128.at[rows(32 * x, 32), :])
    a_sent, b_sent = exchange(*a_fifth), exchange(*b_fifth)
    for one in a_sent + b_sent:
        one.start()
    sent += [third, fourth] + a_sent + b_sent
    a128[rows(32 * my_z, 32), :] = a32[...]
    b128[rows(32 * my_x, 32), :] = b32[...]
    a_last = (38, x_peer, my_x, lambda x: a128, lambda x: gw_hbm.at[rows(128 * x, 128), :])
    b_last = (42, z_peer, my_z, lambda z: b128, lambda z: gw_hbm.at[rows(512 + 128 * z, 128), :])
    landed(*a_fifth)
    a_sent = exchange(*a_last)
    for one in a_sent:
        one.start()
    landed(*b_fifth)
    b_sent = exchange(*b_last)
    for one in b_sent:
        one.start()
    sent += a_sent + b_sent
    keep = [
        pltpu.make_async_copy(a128, gw_hbm.at[rows(128 * my_x, 128), :], lsem.at[16]),
        pltpu.make_async_copy(b128, gw_hbm.at[rows(512 + 128 * my_z, 128), :], lsem.at[17]),
    ]
    for one in keep:
        one.start()

    def drain(i, carry):
        to = lax.rem(me + i, n)
        out_copy(to).wait_send()
        back_copy(to).wait_send()
        return carry

    lax.fori_loop(1, n, drain, 0)
    for one in (send_x0, send_x1, send_w, send_xo, send_fwd, send_raw, send_b, send_c,
                send_far, send_sib, send_dfwd, send_gin):
        one.wait_send()
    send_gin.wait_recv()
    save_gin.wait()

    def saved(g, carry):
        save(g).wait()
        return carry

    lax.fori_loop(0, GROUPS, saved, 0)
    for one in keep:
        one.wait()
    landed(*a_last)
    landed(*b_last)
    for one in sent:
        one.wait_send()


def layer(x, w, val, cot, init, resets, bias, rate, skip):
    n = 32
    slab = (GROUPS, TOK, WIDE)
    hbm = pl.BlockSpec(memory_space=pl.ANY)
    vm = pltpu.VMEM
    dma = pltpu.SemaphoreType.DMA
    return pl.pallas_call(
        layer_kernel,
        out_shape=(
            jax.ShapeDtypeStruct((TOK, 4096), BF16),
            jax.ShapeDtypeStruct((TOK, GROUPS * WIDE), BF16),
            jax.ShapeDtypeStruct((1024, COLS), BF16),
        ),
        in_specs=[hbm] * 5 + [VMEM] * 4,
        out_specs=[hbm] * 3,
        scratch_shapes=[
            vm((TOK, 4096), BF16),
            vm((1024, COLS), BF16),
            vm((1024, COLS), BF16),
            vm((4 * TOK, 1024), BF16),
            vm((TOK, 1024), BF16),
            vm((TOK, COLS), F32),
            vm((TOK, COLS), F32),
            vm((TOK, 512), BF16),
            vm((TOK, 512), BF16),
            vm((TOK, HEADS), F32),
            vm((TOK, 512), BF16),
            vm((TOK, 512), BF16),
            vm((TOK, HEADS), F32),
            vm((GROUPS, TOK, STATE), BF16),
            vm((GROUPS, TOK, STATE), BF16),
            vm((TOK, GROUPS * WIDE), BF16),
            vm((TOK, GROUPS * WIDE), BF16),
            vm((16, 4096), BF16),
            vm(slab, BF16),
            vm(slab, BF16),
            vm(slab, BF16),
            vm(slab, F32),
            vm((GROUPS, 8, WIDE), F32),
            vm((GROUPS, 8, WIDE), F32),
            vm(slab, BF16),
            vm((HEADS, TOK), F32),
            vm((TOK, HEADS), F32),
            vm((TOK, HEADS), F32),
            vm((TOK, HEADS), F32),
            vm((GROUPS, TOK, STATE), F32),
            vm((GROUPS, TOK, STATE), F32),
            vm((n, MSG, OWN), BF16),
            vm((n, MSG, OWN), BF16),
            vm((n, 128, OWN), BF16),
            vm((n, 128, OWN), BF16),
            vm((4 * TOK, COLS), BF16),
            vm((TOK, 2048), BF16),
            vm((TOK, 2048), BF16),
            vm((1024, COLS), BF16),
            vm((4, 128, COLS), BF16),
            vm((4, 128, COLS), BF16),
            vm((128, COLS), BF16),
            vm((128, COLS), BF16),
            vm((4, 32, COLS), BF16),
            vm((4, 32, COLS), BF16),
            vm((32, COLS), BF16),
            vm((32, COLS), BF16),
            vm((32, COLS), BF16),
            vm((32, COLS), BF16),
            vm((32, COLS), BF16),
            vm((32, COLS), BF16),
            vm((128, COLS), BF16),
            vm((128, COLS), BF16),
            dma((46,)),
            dma((46,)),
            dma((18,)),
            dma((n,)),
            dma((n,)),
            dma((n,)),
            dma((n,)),
        ],
        compiler_params=pltpu.CompilerParams(
            collective_id=0, has_side_effects=True, vmem_limit_bytes=60 * 2**20
        ),
        name="layer",
    )(x, w, val, cot, init, resets, bias, rate, skip)


def body(inputs, values, cotangent, weight, init_state, resets, dt_bias, decay_rate, skip):
    scale = 1.0 / math.sqrt(lax.axis_size("fsdp") * TOK * lax.axis_size("ctx"))
    gin, gval, gw = layer(inputs[0], weight, values[0], cotangent[0], init_state[0], resets,
                          dt_bias[None], decay_rate[None], skip[None])
    return (gin[None], gval[None], gw.astype(F32) * scale)


def solution(mesh):
    in_specs = (
        P("fsdp", "ctx", None),
        P("fsdp", "ctx", None),
        P("fsdp", "ctx", None),
        P("fsdp", None),
        P("fsdp", None, None),
        P("fsdp", "ctx"),
        P(),
        P(),
        P(),
    )
    out_specs = (P("fsdp", "ctx", None), P("fsdp", "ctx", None), P("fsdp", None))
    return jax.shard_map(body, mesh=mesh, in_specs=in_specs, out_specs=out_specs, check_vma=False)
```

```python
import functools
import math

import jax
import jax.numpy as jnp
from jax import lax
from jax.experimental import pallas as pl
from jax.experimental.pallas import tpu as pltpu
from jax.sharding import PartitionSpec as P

MESH = pl.DeviceIdType.MESH
F32 = jnp.float32
BF16 = jnp.bfloat16
TOK = 128
HEADS = 128
GROUPS = 8
STATE = 64
WIDE = 1024
COLS = 1152
PAIRS = 4
OWN = 256
HALF = 128
SPLIT = 4
VMEM = pl.BlockSpec(memory_space=pltpu.VMEM)


def nn(a, b):
    return lax.dot_general(a, b, (((1,), (0,)), ((), ())), preferred_element_type=F32)


def nt(a, b):
    return lax.dot_general(a, b, (((1,), (1,)), ((), ())), preferred_element_type=F32)


def tn(a, b):
    return lax.dot_general(a, b, (((0,), (0,)), ((), ())), preferred_element_type=F32)


def split2(x):
    high = x.astype(BF16)
    return high, (x - high.astype(F32)).astype(BF16)


def split3(x):
    high, rest = x.astype(BF16), None
    rest = x - high.astype(F32)
    mid = rest.astype(BF16)
    return high, mid, (rest - mid.astype(F32)).astype(BF16)


def exact(mat, x):
    return sum(nn(mat, part) for part in split3(x))


def remote(src, dst, ssem, rsem, to):
    return pltpu.make_async_remote_copy(
        src_ref=src, dst_ref=dst, send_sem=ssem, recv_sem=rsem, device_id=to, device_id_type=MESH
    )


def block_masks(resets_ref):
    flags = resets_ref[...].astype(F32)
    row = lax.broadcasted_iota(jnp.int32, (TOK, TOK), 0)
    col = lax.broadcasted_iota(jnp.int32, (TOK, TOK), 1)
    seg_col = jnp.sum(jnp.where(col <= row, flags, 0.0), axis=1, keepdims=True)
    flag_col = jnp.sum(jnp.where(col == row, flags, 0.0), axis=1, keepdims=True)
    seg_row = jnp.sum(jnp.where(row <= col, flag_col, 0.0), axis=0, keepdims=True)
    valid = (col <= row) & (seg_col == seg_row)
    return row, col, valid, seg_col


def spread_matrix(g):
    head = lax.rem(lax.broadcasted_iota(jnp.int32, (256, WIDE), 0), 128)
    lane = lax.broadcasted_iota(jnp.int32, (256, WIDE), 1) // STATE
    return jnp.where(head == lane + 16 * g, 1.0, 0.0).astype(BF16)


def gather_matrix(g):
    lane = lax.broadcasted_iota(jnp.int32, (WIDE, HEADS), 0) // STATE
    head = lax.broadcasted_iota(jnp.int32, (WIDE, HEADS), 1)
    return jnp.where(head == lane + 16 * g, 1.0, 0.0).astype(BF16)


def per_head(x, mat):
    high, low = split2(x)
    return nn(high, mat) + nn(low, mat)


def layer_kernel(x_hbm, w_hbm, val_hbm, cot_hbm, init_hbm, resets_ref, bias_ref, rate_ref, skip_ref,
                 gin_hbm, gval_hbm, gw_hbm,
                 x_ref, w_ref, wsib_ref, xall, xo_ref, own_ref, away_ref, put_raw, got_raw, put_bc, got_bc,
                 b_ref, c_ref, val_ref, cot_ref, init_ref,
                 disc_ref, wgt_ref, rc_ref, step_ref, skipx_ref, totx_ref, dd_ref, logt_ref, logd_ref,
                 dlog_ref, dstep_ref, db_ref, dc_ref, out_ref, in_ref, back_ref, home_ref, tot_ref, tots_ref, lap_ref,
                 dall, gin_ref, ginfar_ref, part, ra1, rb1, a1, b1, ra2, rb2, fa, fb, a128, b128,
                 ssem, rsem, lsem, s1, r1, s2, r2, s3, r3, zsem, ysem):
    n = lax.axis_size("ctx")
    me, f = lax.axis_index("ctx"), lax.axis_index("fsdp")
    core, chip = lax.rem(f, 2), f // 2
    my_row, my_x = me // 4, lax.rem(me, 4)
    my_z, my_y = lax.rem(my_row, 4), my_row // 4
    sib = (me, f + 1 - 2 * core)
    far = (me, lax.rem(f + 2, 4))
    my_pair, my_eighth = me // 8, lax.rem(me, 8)
    my_plane = my_y * 4 + my_x
    bar = pltpu.get_barrier_semaphore()
    x_peers = [(me - my_x + lax.rem(my_x + k, 4), f) for k in range(1, 4)]
    z_peers = [(me + 4 * (lax.rem(my_z + k, 4) - my_z), f) for k in range(1, 4)]
    y_peer = (lax.rem(me + 16, n), f)
    direct = [far, sib] + x_peers + z_peers + [y_peer]
    for to in direct:
        pl.semaphore_signal(bar, inc=1, device_id=to, device_id_type=MESH)
    mine = pl.multiple_of(core * 1024, 1024)
    other = pl.multiple_of((1 - core) * 1024, 1024)
    base = pl.multiple_of(chip * 2048, 2048)
    far_base = pl.multiple_of((1 - chip) * 2048, 2048)
    own_at = pl.multiple_of(base + mine, 1024)
    other_at = pl.multiple_of(base + other, 1024)
    init_at = pl.multiple_of(my_pair * 16, 16)
    loads = [
        pltpu.make_async_copy(w_hbm, w_ref, lsem.at[0]),
        pltpu.make_async_copy(x_hbm, x_ref, lsem.at[1]),
        pltpu.make_async_copy(cot_hbm, cot_ref, lsem.at[2]),
        pltpu.make_async_copy(val_hbm, val_ref, lsem.at[3]),
        pltpu.make_async_copy(init_hbm.at[pl.ds(init_at, 16), :], init_ref.at[0], lsem.at[4]),
        pltpu.make_async_copy(init_hbm.at[pl.ds(init_at + 64, 16), :], init_ref.at[1], lsem.at[5]),
    ]
    for one in loads:
        one.start()
    pl.semaphore_wait(bar, len(direct))

    def link(k, source, target, to):
        return remote(source, target, ssem.at[k], rsem.at[k], to)

    send_x0 = link(0, x_hbm.at[:, pl.ds(pl.multiple_of(far_base + mine, 1024), 1024)], xall.at[pl.ds(128, 128), :], far)
    send_x1 = link(1, x_hbm.at[:, pl.ds(pl.multiple_of(far_base + other, 1024), 1024)], xo_ref, far)
    send_w = link(2, w_hbm, wsib_ref, sib)
    send_xo = link(3, x_hbm.at[:, pl.ds(other_at, 1024)], xall.at[pl.ds(256, 128), :], sib)
    for one in (send_x0, send_x1, send_w, send_xo):
        one.start()
    for to in z_peers:
        pl.semaphore_signal(zsem, inc=1, device_id=to, device_id_type=MESH)
    row, col, valid, seg_col = block_masks(resets_ref)
    loads[0].wait()
    loads[1].wait()
    xall[:128, :] = x_ref[:, pl.ds(own_at, 1024)]
    own_ref[...] = nn(xall[:128, :], w_ref[...])
    pl.semaphore_wait(zsem, 3)
    pl.semaphore_signal(ysem, inc=1, device_id=y_peer, device_id_type=MESH)
    send_w.wait_recv()
    own_ref[...] += nn(x_ref[:, pl.ds(other_at, 1024)], wsib_ref[...])
    send_x0.wait_recv()
    away_ref[...] = nn(xall[128:256, :], w_ref[...])
    send_x1.wait_recv()
    send_fwd = link(4, xo_ref, xall.at[pl.ds(384, 128), :], sib)
    send_fwd.start()
    put_raw[...] = away_ref[:, 1024:] + nn(xo_ref[...], wsib_ref[:, 1024:])
    send_raw = link(5, put_raw, got_raw, far)
    send_raw.start()

    def pair_cols(u):
        return pl.ds(pl.multiple_of(u * 128, 128), 128), pl.ds(pl.multiple_of(512 + u * 128, 128), 128)

    def bc_copy(u):
        return link(46 + u, put_bc.at[u], got_bc.at[u], far)

    def give(u, carry):
        for k, cols in enumerate(pair_cols(u)):
            product = away_ref[:, cols] + nn(xo_ref[...], wsib_ref[:, cols])
            put_bc[u, :, k * 128:(k + 1) * 128] = product.astype(BF16)
        bc_copy(u).start()
        return carry

    lax.fori_loop(0, PAIRS, give, 0)
    send_raw.wait_recv()
    raw = own_ref[:, 1024:] + got_raw[...] + bias_ref[...]
    step = jnp.maximum(raw, 0.0) + jnp.log1p(jnp.exp(-jnp.abs(raw)))
    low_tri = jnp.where(col <= row, 1.0, 0.0).astype(BF16)
    log_decay = exact(low_tri, -rate_ref[...] * step)
    final = log_decay[TOK - 1:, :]
    last_seg = seg_col[TOK - 1:, :]
    tail = jnp.where(seg_col == last_seg, jnp.exp(final - log_decay), 0.0)
    reach = jnp.where(seg_col == 0.0, jnp.exp(log_decay), 0.0)
    total = jnp.where(last_seg == 0.0, jnp.exp(final), 0.0)
    tot_ref[...] = jnp.broadcast_to(total, (8, HEADS))
    logd_ref[...] = log_decay
    logt_ref[...] = jnp.transpose(log_decay)
    few = lax.broadcasted_iota(jnp.int32, (16, HEADS), 0)
    extra = jnp.where(few < 8, skip_ref[...], total)
    stack = jnp.concatenate([step, tail, reach, extra], axis=0)
    stack = jnp.concatenate(split2(stack), axis=1)
    loads[2].wait()
    loads[3].wait()
    pl.semaphore_wait(ysem, 1)
    def wide(g):
        return pl.ds(pl.multiple_of(g * WIDE, WIDE), WIDE)

    def out_copy(h, to):
        return remote(out_ref.at[h, to], in_ref.at[h, me], s1.at[h, to], r1.at[h, me], (to, f))

    def own_copy(h):
        return pltpu.make_async_copy(out_ref.at[h, me], in_ref.at[h, me], lsem.at[18 + h])

    def tot_copy(to):
        return remote(tot_ref, tots_ref.at[me], s3.at[to], r3.at[me], (to, f))

    def to_eight(copy, own, h, u):
        for j in range(8):
            to = u * 8 + lax.rem(my_eighth + j, 8)

            @pl.when(to != me)
            def _():
                copy(h, to).start()

            @pl.when(to == me)
            def _():
                own(h).start()

    def all_blocks(copy, own, h):
        def block(i, carry):
            to_eight(copy, own, h, lax.rem(my_pair + i, PAIRS))
            return carry

        lax.fori_loop(0, PAIRS, block, 0)

    def all_sent(copy, h):
        def gone(i, carry):
            copy(h, lax.rem(me + i, n)).wait_send()
            return carry

        lax.fori_loop(1, n, gone, 0)

    for h in range(2):
        for u in (2 * h, 2 * h + 1):
            bc_copy(u).wait_recv()
            cols_b, cols_c = pair_cols(u)
            pair_b = (own_ref[:, cols_b] + got_bc[u, :, :128].astype(F32)).astype(BF16)
            pair_c = (own_ref[:, cols_c] + got_bc[u, :, 128:].astype(F32)).astype(BF16)
            for k in range(2):
                b_ref[2 * u + k] = pair_b[:, k * STATE:(k + 1) * STATE]
                c_ref[2 * u + k] = pair_c[:, k * STATE:(k + 1) * STATE]

        def produce(i, carry):
            block = lax.rem(my_pair + i, PAIRS)
            g = 4 * h + block
            spread = nn(stack, spread_matrix(g))
            step_x = spread[:TOK]
            cot = cot_ref[:, wide(g)].astype(F32)
            disc = (step_x * val_ref[:, wide(g)].astype(F32)).astype(BF16)
            wgt = (spread[TOK:2 * TOK] * disc.astype(F32)).astype(BF16)
            rc = (spread[2 * TOK:3 * TOK] * cot).astype(BF16)
            step_ref[g] = step_x
            skipx_ref[g] = spread[3 * TOK:3 * TOK + 8]
            totx_ref[g] = spread[3 * TOK + 8:3 * TOK + 16]
            disc_ref[g] = disc
            wgt_ref[g] = wgt
            rc_ref[g] = rc
            local = tn(b_ref[g], wgt).astype(BF16)
            first = tn(c_ref[g], rc).astype(BF16)
            for j in range(8):
                out_ref[h, block * 8 + j, :64, :] = local[:, j * HALF:(j + 1) * HALF]
                out_ref[h, block * 8 + j, 64:, :] = first[:, j * HALF:(j + 1) * HALF]
            if h == 0:
                to_eight(out_copy, own_copy, h, block)
            return carry

        lax.fori_loop(0, PAIRS, produce, 0)

    def send_totals(i, carry):
        tot_copy(lax.rem(me + i, n)).start()
        return carry

    lax.fori_loop(1, n, send_totals, 0)
    tots_ref[me] = tot_ref[...]

    dlog_ref[...] = jnp.zeros_like(dlog_ref)
    half = lax.broadcasted_iota(jnp.int32, (1, TOK), 1) < STATE
    left = jnp.where(half, 1.0, 0.0)
    left_b = left.astype(BF16)
    right_b = (1.0 - left).astype(BF16)
    bad = jnp.where(valid, 0.0, 1.0)

    def inside(g, carry):
        b, c = b_ref[g], c_ref[g]
        scores = nt(c, b)
        logs = pltpu.roll(logd_ref[...], lax.rem(HEADS - 16 * g, HEADS), 1)
        d_scores = jnp.zeros((TOK, TOK), F32)
        errs = []
        for q in range(8):
            lanes = pl.ds(pl.multiple_of(g * WIDE + q * 128, 128), 128)
            cot_p = cot_ref[:, lanes]
            disc_p = disc_ref[g, :, q * 128:(q + 1) * 128]
            stacked = jnp.concatenate([disc_p * left_b, disc_p * right_b], axis=0)
            d_mixed = nt(cot_p, stacked)
            mixed = []
            for k in range(2):
                head = 2 * q + k
                span = logs[:, head:head + 1] - logt_ref[pl.ds(g * 16 + head, 1), :]
                weights = jnp.exp(jnp.where(valid, span, -1e30))
                d_scores += d_mixed[:, k * TOK:(k + 1) * TOK] * weights
                mixed.append((weights * scores).astype(BF16))
            mixed = jnp.concatenate(mixed, axis=1)
            inner = nn(mixed, stacked)
            both = tn(mixed, cot_p)
            dd = both[:TOK] * left + both[TOK:] * (1.0 - left)
            dd_ref[g, :, q * 128:(q + 1) * 128] = dd.astype(BF16)
            errs.append(cot_p.astype(F32) * inner - disc_p.astype(F32) * dd)
        dlog_ref[...] += per_head(jnp.concatenate(errs, axis=1), gather_matrix(g))
        ds = d_scores.astype(BF16)
        dc_ref[g] = nn(ds, b)
        db_ref[g] = tn(ds, c)
        return carry

    lax.fori_loop(0, SPLIT, inside, 0)
    all_sent(out_copy, 0)
    all_blocks(out_copy, own_copy, 1)
    lax.fori_loop(SPLIT, GROUPS, inside, 0)
    loads[4].wait()
    loads[5].wait()
    pick_row = lax.broadcasted_iota(jnp.int32, (16, 16), 0)
    pick_col = lax.broadcasted_iota(jnp.int32, (16, 16), 1)
    pick = jnp.where(pick_col == pick_row + 2 * my_eighth, 1.0, 0.0).astype(BF16)
    picked = [nn(pick, init_ref[h]) for h in range(2)]
    turned = [picked[h][r:r + 1, i * 128:(i + 1) * 128] for h in range(2) for r in range(2) for i in range(32)]
    turned = jnp.transpose(jnp.concatenate(turned, axis=0)).astype(BF16)
    from_i = lax.broadcasted_iota(jnp.int32, (128, OWN), 0)
    to_p = lax.broadcasted_iota(jnp.int32, (128, OWN), 1)
    even = jnp.where(to_p == 2 * from_i, 1.0, 0.0).astype(BF16)
    odd = jnp.where(to_p == 2 * from_i + 1, 1.0, 0.0).astype(BF16)
    init_state = nn(turned[:64], even) + nn(turned[64:], odd)

    def total_in(i, carry):
        src = lax.rem(me + n - i, n)
        remote(tot_ref, tots_ref.at[src], s3.at[src], r3.at[src], (src, f)).wait_recv()
        return carry

    lax.fori_loop(1, n, total_in, 0)
    from_head = lax.broadcasted_iota(jnp.int32, (HEADS, HALF), 0)
    to_lane = lax.broadcasted_iota(jnp.int32, (HEADS, HALF), 1) // STATE
    for h in range(2):
        owned = jnp.where(from_head == to_lane + 64 * h + 2 * me, 1.0, 0.0).astype(BF16)
        lap_ref[h] = sum(nn(part_of, owned) for part_of in split3(tots_ref[:, 0, :]))

    def back_copy(h, to):
        return remote(back_ref.at[h, to], home_ref.at[h, me], s2.at[h, to], r2.at[h, me], (to, f))

    def own_back(h):
        return pltpu.make_async_copy(back_ref.at[h, me], home_ref.at[h, me], lsem.at[20 + h])

    for h in range(2):
        lanes = slice(h * HALF, (h + 1) * HALF)
        own_copy(h).wait()

        def arrive(i, carry):
            src = lax.rem(me + n - i, n)
            remote(out_ref.at[h, src], in_ref.at[h, src], s1.at[h, src], r1.at[h, src], (src, f)).wait_recv()
            return carry

        lax.fori_loop(1, n, arrive, 0)

        def laps(i, state):
            ahead, behind = state
            j = n - 1 - i
            back_ref[h, i, :64, :] = ahead.astype(BF16)
            back_ref[h, j, 64:, :] = behind.astype(BF16)
            ahead = lap_ref[h, pl.ds(i, 1), :] * ahead + in_ref[h, i, :64, :].astype(F32)
            behind = in_ref[h, j, 64:, :].astype(F32) + lap_ref[h, pl.ds(j, 1), :] * behind
            return ahead, behind

        lax.fori_loop(0, n, laps, (init_state[:, lanes], jnp.zeros((STATE, HALF), F32)))

        if h == 1:
            all_sent(back_copy, 0)
        all_blocks(back_copy, own_back, h)

    for h in range(2):
        own_back(h).wait()
    dstep_ref[...] = jnp.zeros_like(dstep_ref)

    def save(g):
        return pltpu.make_async_copy(disc_ref.at[g], gval_hbm.at[:, wide(g)], lsem.at[8 + g])

    def d_copies(h):
        copies = []
        for k in range(2):
            cols = slice(512 * k + 256 * h, 512 * k + 256 * h + 256)
            mine_d = dall.at[:128, cols]
            copies.append(link(50 + 4 * h + 2 * k, mine_d, dall.at[128:256, cols], far))
            copies.append(link(51 + 4 * h + 2 * k, mine_d, dall.at[256:384, cols], sib))
        return copies

    for h in range(2):

        def consume(i, carry):
            block = lax.rem(my_pair + PAIRS - i, PAIRS)
            g = 4 * h + block
            for j in range(8):
                src = block * 8 + j

                @pl.when(src != me)
                def _():
                    remote(back_ref.at[h, src], home_ref.at[h, src], s2.at[h, src], r2.at[h, src], (src, f)).wait_recv()

            got = jnp.concatenate([home_ref[h, block * 8 + j] for j in range(8)], axis=1)
            start, end = got[:64], got[64:]
            b, c = b_ref[g], c_ref[g]
            rc, wgt, disc = rc_ref[g], wgt_ref[g], disc_ref[g].astype(F32)
            carried = nn(c, start)
            d_wgt = nn(b, end)
            dc_ref[g] += nt(rc, start)
            db_ref[g] += nt(wgt, end)
            pull = wgt.astype(F32) * d_wgt
            mat = gather_matrix(g)
            err = rc.astype(F32) * carried - pull
            ends = jnp.sum(pull, axis=0, keepdims=True)
            ends += totx_ref[g, :1, :] * jnp.sum(start.astype(F32) * end.astype(F32), axis=0, keepdims=True)
            at_end = lax.broadcasted_iota(jnp.int32, (TOK, WIDE), 0) == TOK - 1
            err = err + jnp.where(at_end, ends, 0.0)
            dlog_ref[...] += per_head(err, mat)
            spread = nn(stack[TOK:2 * TOK], spread_matrix(g))
            d_disc = dd_ref[g].astype(F32) + spread * d_wgt
            val = val_ref[:, wide(g)].astype(F32)
            dstep_ref[...] += per_head(d_disc * val, mat)
            gval = skipx_ref[g, :1, :] * cot_ref[:, wide(g)].astype(F32) + step_ref[g] * d_disc
            disc_ref[g] = gval.astype(BF16)
            save(g).start()
            return carry

        lax.fori_loop(0, PAIRS, consume, 0)
        some = range(4 * h, 4 * h + 4)
        dall[:128, 256 * h:256 * h + 256] = jnp.concatenate([db_ref[g] for g in some], axis=1).astype(BF16)
        dall[:128, 512 + 256 * h:768 + 256 * h] = jnp.concatenate([dc_ref[g] for g in some], axis=1).astype(BF16)
        for one in d_copies(h):
            one.start()
    up_tri = jnp.where(col >= row, 1.0, 0.0).astype(BF16)
    d_inc = exact(up_tri, dlog_ref[...])
    d_step = dstep_ref[...] - rate_ref[...] * d_inc
    d_raw = d_step / (1.0 + jnp.exp(-raw))
    dall[:128, 1024:] = d_raw.astype(BF16)

    last_cols = pl.ds(1024, 128)
    d_last = dall.at[pl.ds(0, 128), last_cols]
    send_far = link(8, d_last, dall.at[pl.ds(128, 128), last_cols], far)
    send_far.start()
    send_sib = link(9, d_last, dall.at[pl.ds(256, 128), last_cols], sib)
    send_sib.start()
    gin_ref[:, pl.ds(mine, 1024)] = nt(dall[:128, :], w_ref[...]).astype(BF16)
    gin_ref[:, pl.ds(other, 1024)] = nt(dall[:128, :], wsib_ref[...]).astype(BF16)
    save_gin = pltpu.make_async_copy(gin_ref, gin_hbm.at[:, pl.ds(base, 2048)], lsem.at[7])
    save_gin.start()
    d_all = d_copies(0) + d_copies(1)
    for one in d_all[0::2]:
        one.wait_recv()
    send_far.wait_recv()
    send_dfwd = link(10, dall.at[pl.ds(128, 128), :], dall.at[pl.ds(384, 128), :], sib)
    send_dfwd.start()
    send_xo.wait_recv()
    send_fwd.wait_recv()
    for one in d_all[1::2]:
        one.wait_recv()
    send_sib.wait_recv()
    send_dfwd.wait_recv()

    def rows(at, count):
        return pl.ds(pl.multiple_of(at, count), count)

    def x_peer(x):
        return (me - my_x + x, f)

    def z_peer(z):
        return (me + 4 * (z - my_z), f)

    def row_peer(q):
        return (4 * q + my_x, f)

    def plane_peer(q):
        return (16 * (q // 4) + 4 * my_z + lax.rem(q, 4), f)

    def exchange(k, peer, mine_at, source, target, count=4):
        copies = []
        for step_to in range(1, count):
            to = lax.rem(mine_at + step_to, count)
            copies.append(remote(source(to), target(mine_at), ssem.at[k + to], rsem.at[k + mine_at], peer(to)))
        return copies

    def landed(k, peer, mine_at, source, target, count=4):
        for step_to in range(1, count):
            at = lax.rem(mine_at + step_to, count)
            remote(source(at), target(at), ssem.at[k + at], rsem.at[k + at], peer(at)).wait_recv()

    def product(at):
        part[rows(at, 128), :] = tn(xall[:, rows(at, 128)], dall[...]).astype(BF16)

    a_first = (12, x_peer, my_x, lambda x: part.at[rows(128 * x, 128), :], lambda x: ra1.at[x])
    b_first = (16, z_peer, my_z, lambda z: part.at[rows(512 + 128 * z, 128), :], lambda z: rb1.at[z])
    a_sent, b_sent = exchange(*a_first), exchange(*b_first)
    for k in range(3):
        product(128 * lax.rem(my_x + k + 1, 4))
        a_sent[k].start()
        product(512 + 128 * lax.rem(my_z + k + 1, 4))
        b_sent[k].start()
    product(128 * my_x)
    product(512 + 128 * my_z)
    ginfar_ref[:, pl.ds(mine, 1024)] = nt(dall[128:256, :], w_ref[...]).astype(BF16)
    ginfar_ref[:, pl.ds(other, 1024)] = nt(dall[128:256, :], wsib_ref[...]).astype(BF16)
    send_gin = link(11, ginfar_ref, gin_hbm.at[:, pl.ds(base, 2048)], far)
    send_gin.start()
    sent = a_sent + b_sent

    def summed(first, got, at, count=4):
        total = first.astype(F32)
        for step_to in range(1, count):
            total += got[lax.rem(at + step_to, count)].astype(F32)
        return total

    a_second = (20, row_peer, my_row, lambda q: a1.at[rows(16 * q, 16), :], lambda q: ra2.at[q], 8)
    b_second = (28, plane_peer, my_plane, lambda q: b1.at[rows(16 * q, 16), :], lambda q: rb2.at[q], 8)
    landed(*a_first)
    a1[...] = summed(part[rows(128 * my_x, 128), :], ra1, my_x).astype(BF16)
    a_sent = exchange(*a_second)
    for one in a_sent:
        one.start()
    landed(*b_first)
    b1[...] = summed(part[rows(512 + 128 * my_z, 128), :], rb1, my_z).astype(BF16)
    b_sent = exchange(*b_second)
    for one in b_sent:
        one.start()
    sent += a_sent + b_sent
    landed(*a_second)
    fa[...] = summed(a1[rows(16 * my_row, 16), :], ra2, my_row, 8).astype(BF16)
    a_third = (66, row_peer, my_row, lambda q: fa, lambda q: a128.at[rows(16 * q, 16), :], 8)
    a_sent = exchange(*a_third)
    for one in a_sent:
        one.start()
    landed(*b_second)
    fb[...] = summed(b1[rows(16 * my_plane, 16), :], rb2, my_plane, 8).astype(BF16)
    b_third = (74, plane_peer, my_plane, lambda q: fb, lambda q: b128.at[rows(16 * q, 16), :], 8)
    b_sent = exchange(*b_third)
    for one in b_sent:
        one.start()
    sent += a_sent + b_sent
    a128[rows(16 * my_row, 16), :] = fa[...]
    b128[rows(16 * my_plane, 16), :] = fb[...]
    a_last = (38, x_peer, my_x, lambda x: a128, lambda x: gw_hbm.at[rows(128 * x, 128), :])
    b_last = (42, z_peer, my_z, lambda z: b128, lambda z: gw_hbm.at[rows(512 + 128 * z, 128), :])
    landed(*a_third)
    a_sent = exchange(*a_last)
    for one in a_sent:
        one.start()
    landed(*b_third)
    b_sent = exchange(*b_last)
    for one in b_sent:
        one.start()
    sent += a_sent + b_sent
    keep = [
        pltpu.make_async_copy(a128, gw_hbm.at[rows(128 * my_x, 128), :], lsem.at[16]),
        pltpu.make_async_copy(b128, gw_hbm.at[rows(512 + 128 * my_z, 128), :], lsem.at[17]),
    ]
    for one in keep:
        one.start()

    def drain(i, carry):
        to = lax.rem(me + i, n)
        out_copy(1, to).wait_send()
        back_copy(1, to).wait_send()
        tot_copy(to).wait_send()
        return carry

    lax.fori_loop(1, n, drain, 0)
    for one in (send_x0, send_x1, send_w, send_xo, send_fwd, send_raw,
                send_far, send_sib, send_dfwd, send_gin):
        one.wait_send()
    for one in d_all + [bc_copy(u) for u in range(PAIRS)]:
        one.wait_send()
    send_gin.wait_recv()
    save_gin.wait()

    def saved(g, carry):
        save(g).wait()
        return carry

    lax.fori_loop(0, GROUPS, saved, 0)
    for one in keep:
        one.wait()
    landed(*a_last)
    landed(*b_last)
    for one in sent:
        one.wait_send()


def layer(x, w, val, cot, init, resets, bias, rate, skip):
    n = 32
    slab = (GROUPS, TOK, WIDE)
    hbm = pl.BlockSpec(memory_space=pl.ANY)
    vm = pltpu.VMEM
    dma = pltpu.SemaphoreType.DMA
    return pl.pallas_call(
        layer_kernel,
        out_shape=(
            jax.ShapeDtypeStruct((TOK, 4096), BF16),
            jax.ShapeDtypeStruct((TOK, GROUPS * WIDE), BF16),
            jax.ShapeDtypeStruct((1024, COLS), BF16),
        ),
        in_specs=[hbm] * 5 + [VMEM] * 4,
        out_specs=[hbm] * 3,
        scratch_shapes=[
            vm((TOK, 4096), BF16),
            vm((1024, COLS), BF16),
            vm((1024, COLS), BF16),
            vm((4 * TOK, 1024), BF16),
            vm((TOK, 1024), BF16),
            vm((TOK, COLS), F32),
            vm((TOK, COLS), F32),
            vm((TOK, HEADS), F32),
            vm((TOK, HEADS), F32),
            vm((PAIRS, TOK, 256), BF16),
            vm((PAIRS, TOK, 256), BF16),
            vm((GROUPS, TOK, STATE), BF16),
            vm((GROUPS, TOK, STATE), BF16),
            vm((TOK, GROUPS * WIDE), BF16),
            vm((TOK, GROUPS * WIDE), BF16),
            vm((2, 16, 4096), BF16),
            vm(slab, BF16),
            vm(slab, BF16),
            vm(slab, BF16),
            vm(slab, F32),
            vm((GROUPS, 8, WIDE), F32),
            vm((GROUPS, 8, WIDE), F32),
            vm(slab, BF16),
            vm((HEADS, TOK), F32),
            vm((TOK, HEADS), F32),
            vm((TOK, HEADS), F32),
            vm((TOK, HEADS), F32),
            vm((GROUPS, TOK, STATE), F32),
            vm((GROUPS, TOK, STATE), F32),
            vm((2, n, 128, HALF), BF16),
            vm((2, n, 128, HALF), BF16),
            vm((2, n, 128, HALF), BF16),
            vm((2, n, 128, HALF), BF16),
            vm((8, HEADS), F32),
            vm((n, 8, HEADS), F32),
            vm((2, n, HALF), F32),
            vm((4 * TOK, COLS), BF16),
            vm((TOK, 2048), BF16),
            vm((TOK, 2048), BF16),
            vm((1024, COLS), BF16),
            vm((4, 128, COLS), BF16),
            vm((4, 128, COLS), BF16),
            vm((128, COLS), BF16),
            vm((128, COLS), BF16),
            vm((8, 16, COLS), BF16),
            vm((8, 16, COLS), BF16),
            vm((16, COLS), BF16),
            vm((16, COLS), BF16),
            vm((128, COLS), BF16),
            vm((128, COLS), BF16),
            dma((82,)),
            dma((82,)),
            dma((22,)),
            dma((2, n)),
            dma((2, n)),
            dma((2, n)),
            dma((2, n)),
            dma((n,)),
            dma((n,)),
            pltpu.SemaphoreType.REGULAR,
            pltpu.SemaphoreType.REGULAR,
        ],
        compiler_params=pltpu.CompilerParams(
            collective_id=0, has_side_effects=True, vmem_limit_bytes=60 * 2**20
        ),
        name="layer",
    )(x, w, val, cot, init, resets, bias, rate, skip)


def finish_kernel(scale, gin, gval, gw, gin_out, gval_out, gw_out, narrow, full, gin_v, gval_v, sem_i, sem_o):
    def some(k):
        return pl.ds(128 * k, 128)

    def pick(k):
        return pl.ds(32 * k, 32)

    loads = [pltpu.make_async_copy(gw.at[some(k), :], narrow.at[some(k), :], sem_i.at[k]) for k in range(8)]
    stores = [pltpu.make_async_copy(full.at[some(k), :], gw_out.at[some(k), :], sem_o.at[k]) for k in range(8)]
    loads += [pltpu.make_async_copy(gval.at[pick(k), :], gval_v.at[pick(k), :], sem_i.at[8 + k]) for k in range(4)]
    stores += [pltpu.make_async_copy(gval_v.at[pick(k), :], gval_out.at[pick(k), :], sem_o.at[8 + k]) for k in range(4)]
    loads.append(pltpu.make_async_copy(gin, gin_v, sem_i.at[12]))
    stores.append(pltpu.make_async_copy(gin_v, gin_out, sem_o.at[12]))
    for one in loads:
        one.start()
    for k in range(13):
        loads[k].wait()
        if k < 8:
            full[some(k), :] = narrow[some(k), :].astype(F32) * scale
        stores[k].start()
    for one in stores:
        one.wait()


def finish(scale, gin, gval, gw):
    hbm = pl.BlockSpec(memory_space=pl.ANY)
    return pl.pallas_call(
        functools.partial(finish_kernel, scale),
        out_shape=(
            jax.ShapeDtypeStruct(gin.shape, BF16),
            jax.ShapeDtypeStruct(gval.shape, BF16),
            jax.ShapeDtypeStruct(gw.shape, F32),
        ),
        in_specs=[hbm] * 3,
        out_specs=[hbm] * 3,
        scratch_shapes=[
            pltpu.VMEM((1024, COLS), BF16),
            pltpu.VMEM((1024, COLS), F32),
            pltpu.VMEM((TOK, 4096), BF16),
            pltpu.VMEM((TOK, GROUPS * WIDE), BF16),
            pltpu.SemaphoreType.DMA((13,)),
            pltpu.SemaphoreType.DMA((13,)),
        ],
        compiler_params=pltpu.CompilerParams(vmem_limit_bytes=60 * 2**20),
        name="finish",
    )(gin, gval, gw)


def body(inputs, values, cotangent, weight, init_state, resets, dt_bias, decay_rate, skip):
    scale = 1.0 / math.sqrt(lax.axis_size("fsdp") * TOK * lax.axis_size("ctx"))
    gin, gval, gw = layer(inputs[0], weight, values[0], cotangent[0], init_state[0], resets,
                          dt_bias[None], decay_rate[None], skip[None])
    gin, gval, gw = finish(scale, gin, gval, gw)
    return (gin[None], gval[None], gw)


def solution(mesh):
    in_specs = (
        P("fsdp", "ctx", None),
        P("fsdp", "ctx", None),
        P("fsdp", "ctx", None),
        P("fsdp", None),
        P("fsdp", None, None),
        P("fsdp", "ctx"),
        P(),
        P(),
        P(),
    )
    out_specs = (P("fsdp", "ctx", None), P("fsdp", "ctx", None), P("fsdp", None))
    return jax.shard_map(body, mesh=mesh, in_specs=in_specs, out_specs=out_specs, check_vma=False)
```

```python
import functools
import math

import jax
import jax.numpy as jnp
from jax import lax
from jax.experimental import pallas as pl
from jax.experimental.pallas import tpu as pltpu
from jax.sharding import PartitionSpec as P

MESH = pl.DeviceIdType.MESH
F32 = jnp.float32
BF16 = jnp.bfloat16
TOK = 128
HEADS = 128
GROUPS = 8
STATE = 64
WIDE = 1024
COLS = 1152
PAIRS = 4
OWN = 256
HALF = 128
VMEM = pl.BlockSpec(memory_space=pltpu.VMEM)


def nn(a, b):
    return lax.dot_general(a, b, (((1,), (0,)), ((), ())), preferred_element_type=F32)


def nt(a, b):
    return lax.dot_general(a, b, (((1,), (1,)), ((), ())), preferred_element_type=F32)


def tn(a, b):
    return lax.dot_general(a, b, (((0,), (0,)), ((), ())), preferred_element_type=F32)


def split2(x):
    high = x.astype(BF16)
    return high, (x - high.astype(F32)).astype(BF16)


def split3(x):
    high, rest = x.astype(BF16), None
    rest = x - high.astype(F32)
    mid = rest.astype(BF16)
    return high, mid, (rest - mid.astype(F32)).astype(BF16)


def exact(mat, x):
    return sum(nn(mat, part) for part in split3(x))


def remote(src, dst, ssem, rsem, to):
    return pltpu.make_async_remote_copy(
        src_ref=src, dst_ref=dst, send_sem=ssem, recv_sem=rsem, device_id=to, device_id_type=MESH
    )


def block_masks(resets_ref):
    flags = resets_ref[...].astype(F32)
    row = lax.broadcasted_iota(jnp.int32, (TOK, TOK), 0)
    col = lax.broadcasted_iota(jnp.int32, (TOK, TOK), 1)
    seg_col = jnp.sum(jnp.where(col <= row, flags, 0.0), axis=1, keepdims=True)
    flag_col = jnp.sum(jnp.where(col == row, flags, 0.0), axis=1, keepdims=True)
    seg_row = jnp.sum(jnp.where(row <= col, flag_col, 0.0), axis=0, keepdims=True)
    valid = (col <= row) & (seg_col == seg_row)
    return row, col, valid, seg_col


def spread_matrix(g):
    head = lax.rem(lax.broadcasted_iota(jnp.int32, (256, WIDE), 0), 128)
    lane = lax.broadcasted_iota(jnp.int32, (256, WIDE), 1) // STATE
    return jnp.where(head == lane + 16 * g, 1.0, 0.0).astype(BF16)


def gather_matrix(g):
    lane = lax.broadcasted_iota(jnp.int32, (WIDE, HEADS), 0) // STATE
    head = lax.broadcasted_iota(jnp.int32, (WIDE, HEADS), 1)
    return jnp.where(head == lane + 16 * g, 1.0, 0.0).astype(BF16)


def per_head(x, mat):
    high, low = split2(x)
    return nn(high, mat) + nn(low, mat)


def layer_kernel(x_hbm, w_hbm, val_hbm, cot_hbm, init_hbm, resets_ref, bias_ref, rate_ref, skip_ref,
                 gin_hbm, gval_hbm, gw_hbm,
                 x_ref, w_ref, wsib_ref, xall, xo_ref, own_ref, away_ref, put_raw, got_raw, put_bc, got_bc,
                 b_ref, c_ref, val_ref, cot_ref, init_ref,
                 disc_ref, wgt_ref, rc_ref, step_ref, skipx_ref, totx_ref, dd_ref, logt_ref, logd_ref,
                 dlog_ref, dstep_ref, db_ref, dc_ref, out_ref, in_ref, back_ref, home_ref, tot_ref, tots_ref, lap_ref,
                 dall, gin_ref, ginfar_ref,
                 part_0, part_1, ra1_0, ra1_1, rb1_0, rb1_1, a1_0, a1_1, b1_0, b1_1, ra2_0, ra2_1, rb2_0, rb2_1,
                 fa_0, fa_1, fb_0, fb_1, a128_0, a128_1, b128_0, b128_1,
                 ssem, rsem, lsem, s1, r1, s2, r2, s3, r3, zsem, ysem):
    n = lax.axis_size("ctx")
    me, f = lax.axis_index("ctx"), lax.axis_index("fsdp")
    core, chip = lax.rem(f, 2), f // 2
    my_row, my_x = me // 4, lax.rem(me, 4)
    my_z, my_y = lax.rem(my_row, 4), my_row // 4
    sib = (me, f + 1 - 2 * core)
    far = (me, lax.rem(f + 2, 4))
    my_pair, my_eighth = me // 8, lax.rem(me, 8)
    my_plane = my_y * 4 + my_x
    bar = pltpu.get_barrier_semaphore()
    x_peers = [(me - my_x + lax.rem(my_x + k, 4), f) for k in range(1, 4)]
    z_peers = [(me + 4 * (lax.rem(my_z + k, 4) - my_z), f) for k in range(1, 4)]
    y_peer = (lax.rem(me + 16, n), f)
    direct = [far, sib] + x_peers + z_peers + [y_peer]
    for to in direct:
        pl.semaphore_signal(bar, inc=1, device_id=to, device_id_type=MESH)
    mine = pl.multiple_of(core * 1024, 1024)
    other = pl.multiple_of((1 - core) * 1024, 1024)
    base = pl.multiple_of(chip * 2048, 2048)
    far_base = pl.multiple_of((1 - chip) * 2048, 2048)
    own_at = pl.multiple_of(base + mine, 1024)
    other_at = pl.multiple_of(base + other, 1024)
    init_at = pl.multiple_of(my_pair * 16, 16)
    loads = [
        pltpu.make_async_copy(w_hbm, w_ref, lsem.at[0]),
        pltpu.make_async_copy(x_hbm, x_ref, lsem.at[1]),
        pltpu.make_async_copy(cot_hbm, cot_ref, lsem.at[2]),
        pltpu.make_async_copy(val_hbm, val_ref, lsem.at[3]),
        pltpu.make_async_copy(init_hbm.at[pl.ds(init_at, 16), :], init_ref.at[0], lsem.at[4]),
        pltpu.make_async_copy(init_hbm.at[pl.ds(init_at + 64, 16), :], init_ref.at[1], lsem.at[5]),
    ]
    for one in loads:
        one.start()
    pl.semaphore_wait(bar, len(direct))

    def link(k, source, target, to):
        return remote(source, target, ssem.at[k], rsem.at[k], to)

    send_x0 = link(0, x_hbm.at[:, pl.ds(pl.multiple_of(far_base + mine, 1024), 1024)], xall.at[pl.ds(128, 128), :], far)
    send_x1 = link(1, x_hbm.at[:, pl.ds(pl.multiple_of(far_base + other, 1024), 1024)], xo_ref, far)
    send_w = link(2, w_hbm, wsib_ref, sib)
    send_xo = link(3, x_hbm.at[:, pl.ds(other_at, 1024)], xall.at[pl.ds(256, 128), :], sib)
    for one in (send_x0, send_x1, send_w, send_xo):
        one.start()
    for to in z_peers:
        pl.semaphore_signal(zsem, inc=1, device_id=to, device_id_type=MESH)
    row, col, valid, seg_col = block_masks(resets_ref)
    loads[0].wait()
    loads[1].wait()
    xall[:128, :] = x_ref[:, pl.ds(own_at, 1024)]
    own_ref[...] = nn(xall[:128, :], w_ref[...])
    pl.semaphore_wait(zsem, 3)
    pl.semaphore_signal(ysem, inc=1, device_id=y_peer, device_id_type=MESH)
    send_w.wait_recv()
    own_ref[...] += nn(x_ref[:, pl.ds(other_at, 1024)], wsib_ref[...])
    send_x0.wait_recv()
    away_ref[...] = nn(xall[128:256, :], w_ref[...])
    send_x1.wait_recv()
    send_fwd = link(4, xo_ref, xall.at[pl.ds(384, 128), :], sib)
    send_fwd.start()
    put_raw[...] = away_ref[:, 1024:] + nn(xo_ref[...], wsib_ref[:, 1024:])
    send_raw = link(5, put_raw, got_raw, far)
    send_raw.start()

    def pair_cols(u):
        return pl.ds(pl.multiple_of(u * 128, 128), 128), pl.ds(pl.multiple_of(512 + u * 128, 128), 128)

    def bc_copy(u):
        return link(46 + u, put_bc.at[u], got_bc.at[u], far)

    def give(u, carry):
        for k, cols in enumerate(pair_cols(u)):
            product = away_ref[:, cols] + nn(xo_ref[...], wsib_ref[:, cols])
            put_bc[u, :, k * 128:(k + 1) * 128] = product.astype(BF16)
        bc_copy(u).start()
        return carry

    lax.fori_loop(0, PAIRS, give, 0)
    send_raw.wait_recv()
    raw = own_ref[:, 1024:] + got_raw[...] + bias_ref[...]
    step = jnp.maximum(raw, 0.0) + jnp.log1p(jnp.exp(-jnp.abs(raw)))
    low_tri = jnp.where(col <= row, 1.0, 0.0).astype(BF16)
    log_decay = exact(low_tri, -rate_ref[...] * step)
    final = log_decay[TOK - 1:, :]
    last_seg = seg_col[TOK - 1:, :]
    tail = jnp.where(seg_col == last_seg, jnp.exp(final - log_decay), 0.0)
    reach = jnp.where(seg_col == 0.0, jnp.exp(log_decay), 0.0)
    total = jnp.where(last_seg == 0.0, jnp.exp(final), 0.0)
    tot_ref[...] = jnp.broadcast_to(total, (8, HEADS))
    logd_ref[...] = log_decay
    logt_ref[...] = jnp.transpose(log_decay)
    few = lax.broadcasted_iota(jnp.int32, (16, HEADS), 0)
    extra = jnp.where(few < 8, skip_ref[...], total)
    stack = jnp.concatenate([step, tail, reach, extra], axis=0)
    stack = jnp.concatenate(split2(stack), axis=1)
    loads[2].wait()
    loads[3].wait()
    pl.semaphore_wait(ysem, 1)
    def wide(g):
        return pl.ds(pl.multiple_of(g * WIDE, WIDE), WIDE)

    def out_copy(h, to):
        return remote(out_ref.at[h, to], in_ref.at[h, me], s1.at[h, to], r1.at[h, me], (to, f))

    def own_copy(h):
        return pltpu.make_async_copy(out_ref.at[h, me], in_ref.at[h, me], lsem.at[18 + h])

    def tot_copy(to):
        return remote(tot_ref, tots_ref.at[me], s3.at[to], r3.at[me], (to, f))

    def to_eight(copy, own, h, u):
        for j in range(8):
            to = u * 8 + lax.rem(my_eighth + j, 8)

            @pl.when(to != me)
            def _():
                copy(h, to).start()

            @pl.when(to == me)
            def _():
                own(h).start()

    def all_blocks(copy, own, h):
        def block(i, carry):
            to_eight(copy, own, h, lax.rem(my_pair + i, PAIRS))
            return carry

        lax.fori_loop(0, PAIRS, block, 0)

    def all_sent(copy, h):
        def gone(i, carry):
            copy(h, lax.rem(me + i, n)).wait_send()
            return carry

        lax.fori_loop(1, n, gone, 0)

    for h in range(2):
        for u in (2 * h, 2 * h + 1):
            bc_copy(u).wait_recv()
            cols_b, cols_c = pair_cols(u)
            pair_b = (own_ref[:, cols_b] + got_bc[u, :, :128].astype(F32)).astype(BF16)
            pair_c = (own_ref[:, cols_c] + got_bc[u, :, 128:].astype(F32)).astype(BF16)
            for k in range(2):
                b_ref[2 * u + k] = pair_b[:, k * STATE:(k + 1) * STATE]
                c_ref[2 * u + k] = pair_c[:, k * STATE:(k + 1) * STATE]

        def produce(i, carry):
            block = lax.rem(my_pair + i, PAIRS)
            g = 4 * h + block
            spread = nn(stack, spread_matrix(g))
            step_x = spread[:TOK]
            cot = cot_ref[:, wide(g)].astype(F32)
            disc = (step_x * val_ref[:, wide(g)].astype(F32)).astype(BF16)
            wgt = (spread[TOK:2 * TOK] * disc.astype(F32)).astype(BF16)
            rc = (spread[2 * TOK:3 * TOK] * cot).astype(BF16)
            step_ref[g] = step_x
            skipx_ref[g] = spread[3 * TOK:3 * TOK + 8]
            totx_ref[g] = spread[3 * TOK + 8:3 * TOK + 16]
            disc_ref[g] = disc
            wgt_ref[g] = wgt
            rc_ref[g] = rc
            local = tn(b_ref[g], wgt).astype(BF16)
            first = tn(c_ref[g], rc).astype(BF16)
            for j in range(8):
                out_ref[h, block * 8 + j, :64, :] = local[:, j * HALF:(j + 1) * HALF]
                out_ref[h, block * 8 + j, 64:, :] = first[:, j * HALF:(j + 1) * HALF]
            to_eight(out_copy, own_copy, h, block)
            return carry

        lax.fori_loop(0, PAIRS, produce, 0)

    def send_totals(i, carry):
        tot_copy(lax.rem(me + i, n)).start()
        return carry

    lax.fori_loop(1, n, send_totals, 0)
    tots_ref[me] = tot_ref[...]

    dlog_ref[...] = jnp.zeros_like(dlog_ref)
    half = lax.broadcasted_iota(jnp.int32, (1, TOK), 1) < STATE
    left = jnp.where(half, 1.0, 0.0)
    left_b = left.astype(BF16)
    right_b = (1.0 - left).astype(BF16)
    bad = jnp.where(valid, 0.0, 1.0)

    def inside(g, carry):
        b, c = b_ref[g], c_ref[g]
        scores = nt(c, b)
        logs = pltpu.roll(logd_ref[...], lax.rem(HEADS - 16 * g, HEADS), 1)
        d_scores = jnp.zeros((TOK, TOK), F32)
        errs = []
        for q in range(8):
            lanes = pl.ds(pl.multiple_of(g * WIDE + q * 128, 128), 128)
            cot_p = cot_ref[:, lanes]
            disc_p = disc_ref[g, :, q * 128:(q + 1) * 128]
            stacked = jnp.concatenate([disc_p * left_b, disc_p * right_b], axis=0)
            d_mixed = nt(cot_p, stacked)
            mixed = []
            for k in range(2):
                head = 2 * q + k
                span = logs[:, head:head + 1] - logt_ref[pl.ds(g * 16 + head, 1), :]
                weights = jnp.exp(jnp.where(valid, span, -1e30))
                d_scores += d_mixed[:, k * TOK:(k + 1) * TOK] * weights
                mixed.append((weights * scores).astype(BF16))
            mixed = jnp.concatenate(mixed, axis=1)
            inner = nn(mixed, stacked)
            both = tn(mixed, cot_p)
            dd = both[:TOK] * left + both[TOK:] * (1.0 - left)
            dd_ref[g, :, q * 128:(q + 1) * 128] = dd.astype(BF16)
            errs.append(cot_p.astype(F32) * inner - disc_p.astype(F32) * dd)
        dlog_ref[...] += per_head(jnp.concatenate(errs, axis=1), gather_matrix(g))
        ds = d_scores.astype(BF16)
        dc_ref[g] = nn(ds, b)
        db_ref[g] = tn(ds, c)
        return carry

    lax.fori_loop(0, GROUPS, inside, 0)
    loads[4].wait()
    loads[5].wait()
    pick_row = lax.broadcasted_iota(jnp.int32, (16, 16), 0)
    pick_col = lax.broadcasted_iota(jnp.int32, (16, 16), 1)
    pick = jnp.where(pick_col == pick_row + 2 * my_eighth, 1.0, 0.0).astype(BF16)
    picked = [nn(pick, init_ref[h]) for h in range(2)]
    turned = [picked[h][r:r + 1, i * 128:(i + 1) * 128] for h in range(2) for r in range(2) for i in range(32)]
    turned = jnp.transpose(jnp.concatenate(turned, axis=0)).astype(BF16)
    from_i = lax.broadcasted_iota(jnp.int32, (128, OWN), 0)
    to_p = lax.broadcasted_iota(jnp.int32, (128, OWN), 1)
    even = jnp.where(to_p == 2 * from_i, 1.0, 0.0).astype(BF16)
    odd = jnp.where(to_p == 2 * from_i + 1, 1.0, 0.0).astype(BF16)
    init_state = nn(turned[:64], even) + nn(turned[64:], odd)

    def total_in(i, carry):
        src = lax.rem(me + n - i, n)
        remote(tot_ref, tots_ref.at[src], s3.at[src], r3.at[src], (src, f)).wait_recv()
        return carry

    lax.fori_loop(1, n, total_in, 0)
    from_head = lax.broadcasted_iota(jnp.int32, (HEADS, HALF), 0)
    to_lane = lax.broadcasted_iota(jnp.int32, (HEADS, HALF), 1) // STATE
    for h in range(2):
        owned = jnp.where(from_head == to_lane + 64 * h + 2 * me, 1.0, 0.0).astype(BF16)
        lap_ref[h] = sum(nn(part_of, owned) for part_of in split3(tots_ref[:, 0, :]))

    def back_copy(h, to):
        return remote(back_ref.at[h, to], home_ref.at[h, me], s2.at[h, to], r2.at[h, me], (to, f))

    def own_back(h):
        return pltpu.make_async_copy(back_ref.at[h, me], home_ref.at[h, me], lsem.at[20 + h])

    for h in range(2):
        lanes = slice(h * HALF, (h + 1) * HALF)
        own_copy(h).wait()

        def arrive(i, carry):
            src = lax.rem(me + n - i, n)
            remote(out_ref.at[h, src], in_ref.at[h, src], s1.at[h, src], r1.at[h, src], (src, f)).wait_recv()
            return carry

        lax.fori_loop(1, n, arrive, 0)

        def laps(i, state):
            ahead, behind = state
            j = n - 1 - i
            back_ref[h, i, :64, :] = ahead.astype(BF16)
            back_ref[h, j, 64:, :] = behind.astype(BF16)
            ahead = lap_ref[h, pl.ds(i, 1), :] * ahead + in_ref[h, i, :64, :].astype(F32)
            behind = in_ref[h, j, 64:, :].astype(F32) + lap_ref[h, pl.ds(j, 1), :] * behind
            return ahead, behind

        lax.fori_loop(0, n, laps, (init_state[:, lanes], jnp.zeros((STATE, HALF), F32)))

        if h == 1:
            all_sent(back_copy, 0)
        all_blocks(back_copy, own_back, h)

    for h in range(2):
        own_back(h).wait()
    dstep_ref[...] = jnp.zeros_like(dstep_ref)

    def save(g):
        return pltpu.make_async_copy(disc_ref.at[g], gval_hbm.at[:, wide(g)], lsem.at[8 + g])

    def rows(at, count):
        return pl.ds(pl.multiple_of(at, count), count)

    def x_peer(x):
        return (me - my_x + x, f)

    def z_peer(z):
        return (me + 4 * (z - my_z), f)

    def row_peer(q):
        return (4 * q + my_x, f)

    def plane_peer(q):
        return (16 * (q // 4) + 4 * my_z + lax.rem(q, 4), f)

    def exchange(k, peer, mine_at, source, target, count=4):
        copies = []
        for step_to in range(1, count):
            to = lax.rem(mine_at + step_to, count)
            copies.append(remote(source(to), target(mine_at), ssem.at[k + to], rsem.at[k + mine_at], peer(to)))
        return copies

    def landed(k, peer, mine_at, source, target, count=4):
        for step_to in range(1, count):
            at = lax.rem(mine_at + step_to, count)
            remote(source(at), target(at), ssem.at[k + at], rsem.at[k + at], peer(at)).wait_recv()

    def summed(first, got, at, count=4):
        total = first.astype(F32)
        for step_to in range(1, count):
            total += got[lax.rem(at + step_to, count)].astype(F32)
        return total

    chunk_cols = (slice(0, 512), slice(512, 1152))
    bufs = (
        (part_0, ra1_0, rb1_0, a1_0, b1_0, ra2_0, rb2_0, fa_0, fb_0, a128_0, b128_0),
        (part_1, ra1_1, rb1_1, a1_1, b1_1, ra2_1, rb2_1, fa_1, fb_1, a128_1, b128_1),
    )
    sent = []

    def stages(c):
        part, ra1, rb1, a1, b1, ra2, rb2, fa, fb, a128, b128 = bufs[c]
        k = 100 * c
        cols = chunk_cols[c]
        return (
            (k + 12, x_peer, my_x, lambda x: part.at[rows(128 * x, 128), :], lambda x: ra1.at[x]),
            (k + 16, z_peer, my_z, lambda z: part.at[rows(512 + 128 * z, 128), :], lambda z: rb1.at[z]),
            (k + 20, row_peer, my_row, lambda q: a1.at[rows(16 * q, 16), :], lambda q: ra2.at[q], 8),
            (k + 28, plane_peer, my_plane, lambda q: b1.at[rows(16 * q, 16), :], lambda q: rb2.at[q], 8),
            (k + 66, row_peer, my_row, lambda q: fa, lambda q: a128.at[rows(16 * q, 16), :], 8),
            (k + 74, plane_peer, my_plane, lambda q: fb, lambda q: b128.at[rows(16 * q, 16), :], 8),
            (k + 38, x_peer, my_x, lambda x: a128, lambda x: gw_hbm.at[rows(128 * x, 128), cols]),
            (k + 42, z_peer, my_z, lambda z: b128, lambda z: gw_hbm.at[rows(512 + 128 * z, 128), cols]),
        )

    def go(stage):
        copies = exchange(*stage)
        for one in copies:
            one.start()
        sent.extend(copies)

    def d_copies(h):
        cols = chunk_cols[h]
        own_d, far_d = dall.at[:128, cols], dall.at[128:256, cols]
        return (
            link(50 + 3 * h, own_d, far_d, far),
            link(51 + 3 * h, own_d, dall.at[256:384, cols], sib),
            link(52 + 3 * h, far_d, dall.at[384:512, cols], sib),
        )

    def give_d(h):
        for one in d_copies(h)[:2]:
            one.start()

    def first_stage(h):
        to_far, to_sib, forward = d_copies(h)
        to_far.wait_recv()
        forward.start()
        to_sib.wait_recv()
        forward.wait_recv()
        part, cols = bufs[h][0], chunk_cols[h]

        def product(at):
            part[rows(at, 128), :] = tn(xall[:, rows(at, 128)], dall[:, cols]).astype(BF16)

        a_sent, b_sent = exchange(*stages(h)[0]), exchange(*stages(h)[1])
        for k in range(3):
            product(128 * lax.rem(my_x + k + 1, 4))
            a_sent[k].start()
            product(512 + 128 * lax.rem(my_z + k + 1, 4))
            b_sent[k].start()
        product(128 * my_x)
        product(512 + 128 * my_z)
        sent.extend(a_sent + b_sent)

    def second_stage(c):
        part, ra1, rb1, a1, b1 = bufs[c][:5]
        stage = stages(c)
        landed(*stage[0])
        a1[...] = summed(part[rows(128 * my_x, 128), :], ra1, my_x).astype(BF16)
        go(stage[2])
        landed(*stage[1])
        b1[...] = summed(part[rows(512 + 128 * my_z, 128), :], rb1, my_z).astype(BF16)
        go(stage[3])

    def third_stage(c):
        a1, b1, ra2, rb2, fa, fb, a128, b128 = bufs[c][3:]
        stage = stages(c)
        landed(*stage[2])
        fa[...] = summed(a1[rows(16 * my_row, 16), :], ra2, my_row, 8).astype(BF16)
        go(stage[4])
        landed(*stage[3])
        fb[...] = summed(b1[rows(16 * my_plane, 16), :], rb2, my_plane, 8).astype(BF16)
        go(stage[5])
        a128[rows(16 * my_row, 16), :] = fa[...]
        b128[rows(16 * my_plane, 16), :] = fb[...]

    def keep(c):
        a128, b128 = bufs[c][9:]
        cols = chunk_cols[c]
        return (
            pltpu.make_async_copy(a128, gw_hbm.at[rows(128 * my_x, 128), cols], lsem.at[(16, 22)[c]]),
            pltpu.make_async_copy(b128, gw_hbm.at[rows(512 + 128 * my_z, 128), cols], lsem.at[(17, 23)[c]]),
        )

    def last_stage(c):
        stage = stages(c)
        landed(*stage[4])
        go(stage[6])
        landed(*stage[5])
        go(stage[7])
        for one in keep(c):
            one.start()

    def input_product(at, target):
        d = dall[at:at + 128, :]
        d = jnp.concatenate([d[:, :256], d[:, 512:768], d[:, 256:512], d[:, 768:]], axis=1)
        target[:, pl.ds(mine, 1024)] = nt(d, w_ref[...]).astype(BF16)
        target[:, pl.ds(other, 1024)] = nt(d, wsib_ref[...]).astype(BF16)

    for h in range(2):

        def consume(i, carry):
            block = lax.rem(my_pair + PAIRS - i, PAIRS)
            g = 4 * h + block
            for j in range(8):
                src = block * 8 + j

                @pl.when(src != me)
                def _():
                    remote(back_ref.at[h, src], home_ref.at[h, src], s2.at[h, src], r2.at[h, src], (src, f)).wait_recv()

            got = jnp.concatenate([home_ref[h, block * 8 + j] for j in range(8)], axis=1)
            start, end = got[:64], got[64:]
            b, c = b_ref[g], c_ref[g]
            rc, wgt, disc = rc_ref[g], wgt_ref[g], disc_ref[g].astype(F32)
            carried = nn(c, start)
            d_wgt = nn(b, end)
            dc_ref[g] += nt(rc, start)
            db_ref[g] += nt(wgt, end)
            pull = wgt.astype(F32) * d_wgt
            mat = gather_matrix(g)
            err = rc.astype(F32) * carried - pull
            ends = jnp.sum(pull, axis=0, keepdims=True)
            ends += totx_ref[g, :1, :] * jnp.sum(start.astype(F32) * end.astype(F32), axis=0, keepdims=True)
            at_end = lax.broadcasted_iota(jnp.int32, (TOK, WIDE), 0) == TOK - 1
            err = err + jnp.where(at_end, ends, 0.0)
            dlog_ref[...] += per_head(err, mat)
            spread = nn(stack[TOK:2 * TOK], spread_matrix(g))
            d_disc = dd_ref[g].astype(F32) + spread * d_wgt
            val = val_ref[:, wide(g)].astype(F32)
            dstep_ref[...] += per_head(d_disc * val, mat)
            gval = skipx_ref[g, :1, :] * cot_ref[:, wide(g)].astype(F32) + step_ref[g] * d_disc
            disc_ref[g] = gval.astype(BF16)
            save(g).start()
            return carry

        lax.fori_loop(0, PAIRS, consume, 0)
        some = range(4 * h, 4 * h + 4)
        at = 512 * h
        dall[:128, at:at + 256] = jnp.concatenate([db_ref[g] for g in some], axis=1).astype(BF16)
        dall[:128, at + 256:at + 512] = jnp.concatenate([dc_ref[g] for g in some], axis=1).astype(BF16)
        if h == 0:
            give_d(0)
    up_tri = jnp.where(col >= row, 1.0, 0.0).astype(BF16)
    d_inc = exact(up_tri, dlog_ref[...])
    d_step = dstep_ref[...] - rate_ref[...] * d_inc
    dall[:128, 1024:] = (d_step / (1.0 + jnp.exp(-raw))).astype(BF16)
    give_d(1)
    send_xo.wait_recv()
    send_fwd.wait_recv()
    first_stage(0)
    input_product(0, gin_ref)
    save_gin = pltpu.make_async_copy(gin_ref, gin_hbm.at[:, pl.ds(base, 2048)], lsem.at[7])
    save_gin.start()
    first_stage(1)
    second_stage(0)
    input_product(128, ginfar_ref)
    send_gin = link(11, ginfar_ref, gin_hbm.at[:, pl.ds(base, 2048)], far)
    third_stage(0)
    second_stage(1)
    third_stage(1)
    last_stage(0)
    send_gin.start()
    last_stage(1)

    def drain(i, carry):
        to = lax.rem(me + i, n)
        out_copy(0, to).wait_send()
        out_copy(1, to).wait_send()
        back_copy(1, to).wait_send()
        tot_copy(to).wait_send()
        return carry

    lax.fori_loop(1, n, drain, 0)
    for one in (send_x0, send_x1, send_w, send_xo, send_fwd, send_raw, send_gin):
        one.wait_send()
    for one in [*d_copies(0), *d_copies(1)] + [bc_copy(u) for u in range(PAIRS)]:
        one.wait_send()
    send_gin.wait_recv()
    save_gin.wait()

    def saved(g, carry):
        save(g).wait()
        return carry

    lax.fori_loop(0, GROUPS, saved, 0)
    for c in range(2):
        for one in keep(c):
            one.wait()
        for stage in stages(c)[6:]:
            landed(*stage)
    for one in sent:
        one.wait_send()


def layer(x, w, val, cot, init, resets, bias, rate, skip):
    n = 32
    slab = (GROUPS, TOK, WIDE)
    hbm = pl.BlockSpec(memory_space=pl.ANY)
    vm = pltpu.VMEM
    dma = pltpu.SemaphoreType.DMA
    return pl.pallas_call(
        layer_kernel,
        out_shape=(
            jax.ShapeDtypeStruct((TOK, 4096), BF16),
            jax.ShapeDtypeStruct((TOK, GROUPS * WIDE), BF16),
            jax.ShapeDtypeStruct((1024, COLS), BF16),
        ),
        in_specs=[hbm] * 5 + [VMEM] * 4,
        out_specs=[hbm] * 3,
        scratch_shapes=[
            vm((TOK, 4096), BF16),
            vm((1024, COLS), BF16),
            vm((1024, COLS), BF16),
            vm((4 * TOK, 1024), BF16),
            vm((TOK, 1024), BF16),
            vm((TOK, COLS), F32),
            vm((TOK, COLS), F32),
            vm((TOK, HEADS), F32),
            vm((TOK, HEADS), F32),
            vm((PAIRS, TOK, 256), BF16),
            vm((PAIRS, TOK, 256), BF16),
            vm((GROUPS, TOK, STATE), BF16),
            vm((GROUPS, TOK, STATE), BF16),
            vm((TOK, GROUPS * WIDE), BF16),
            vm((TOK, GROUPS * WIDE), BF16),
            vm((2, 16, 4096), BF16),
            vm(slab, BF16),
            vm(slab, BF16),
            vm(slab, BF16),
            vm(slab, F32),
            vm((GROUPS, 8, WIDE), F32),
            vm((GROUPS, 8, WIDE), F32),
            vm(slab, BF16),
            vm((HEADS, TOK), F32),
            vm((TOK, HEADS), F32),
            vm((TOK, HEADS), F32),
            vm((TOK, HEADS), F32),
            vm((GROUPS, TOK, STATE), F32),
            vm((GROUPS, TOK, STATE), F32),
            vm((2, n, 128, HALF), BF16),
            vm((2, n, 128, HALF), BF16),
            vm((2, n, 128, HALF), BF16),
            vm((2, n, 128, HALF), BF16),
            vm((8, HEADS), F32),
            vm((n, 8, HEADS), F32),
            vm((2, n, HALF), F32),
            vm((4 * TOK, COLS), BF16),
            vm((TOK, 2048), BF16),
            vm((TOK, 2048), BF16),
            *[vm(rows + (cols,), BF16)
              for rows in ((1024,), (4, 128), (4, 128), (128,), (128,), (8, 16), (8, 16), (16,), (16,), (128,), (128,))
              for cols in (512, 640)],
            dma((182,)),
            dma((182,)),
            dma((24,)),
            dma((2, n)),
            dma((2, n)),
            dma((2, n)),
            dma((2, n)),
            dma((n,)),
            dma((n,)),
            pltpu.SemaphoreType.REGULAR,
            pltpu.SemaphoreType.REGULAR,
        ],
        compiler_params=pltpu.CompilerParams(
            collective_id=0, has_side_effects=True, vmem_limit_bytes=60 * 2**20
        ),
        name="layer",
    )(x, w, val, cot, init, resets, bias, rate, skip)


def finish_kernel(scale, gin, gval, gw, gin_out, gval_out, gw_out, narrow, full, gin_v, gval_v, sem_i, sem_o):
    def some(k):
        return pl.ds(128 * k, 128)

    def pick(k):
        return pl.ds(32 * k, 32)

    loads = [pltpu.make_async_copy(gw.at[some(k), :], narrow.at[some(k), :], sem_i.at[k]) for k in range(8)]
    stores = [pltpu.make_async_copy(full.at[some(k), :], gw_out.at[some(k), :], sem_o.at[k]) for k in range(8)]
    loads += [pltpu.make_async_copy(gval.at[pick(k), :], gval_v.at[pick(k), :], sem_i.at[8 + k]) for k in range(4)]
    stores += [pltpu.make_async_copy(gval_v.at[pick(k), :], gval_out.at[pick(k), :], sem_o.at[8 + k]) for k in range(4)]
    loads.append(pltpu.make_async_copy(gin, gin_v, sem_i.at[12]))
    stores.append(pltpu.make_async_copy(gin_v, gin_out, sem_o.at[12]))
    for one in loads:
        one.start()
    for k in range(13):
        loads[k].wait()
        if k < 8:
            for to, at, wide in ((0, 0, 256), (256, 512, 256), (512, 256, 256), (768, 768, 384)):
                full[some(k), to:to + wide] = narrow[some(k), at:at + wide].astype(F32) * scale
        stores[k].start()
    for one in stores:
        one.wait()


def finish(scale, gin, gval, gw):
    hbm = pl.BlockSpec(memory_space=pl.ANY)
    return pl.pallas_call(
        functools.partial(finish_kernel, scale),
        out_shape=(
            jax.ShapeDtypeStruct(gin.shape, BF16),
            jax.ShapeDtypeStruct(gval.shape, BF16),
            jax.ShapeDtypeStruct(gw.shape, F32),
        ),
        in_specs=[hbm] * 3,
        out_specs=[hbm] * 3,
        scratch_shapes=[
            pltpu.VMEM((1024, COLS), BF16),
            pltpu.VMEM((1024, COLS), F32),
            pltpu.VMEM((TOK, 4096), BF16),
            pltpu.VMEM((TOK, GROUPS * WIDE), BF16),
            pltpu.SemaphoreType.DMA((13,)),
            pltpu.SemaphoreType.DMA((13,)),
        ],
        compiler_params=pltpu.CompilerParams(vmem_limit_bytes=60 * 2**20),
        name="finish",
    )(gin, gval, gw)


def body(inputs, values, cotangent, weight, init_state, resets, dt_bias, decay_rate, skip):
    scale = 1.0 / math.sqrt(lax.axis_size("fsdp") * TOK * lax.axis_size("ctx"))
    gin, gval, gw = layer(inputs[0], weight, values[0], cotangent[0], init_state[0], resets,
                          dt_bias[None], decay_rate[None], skip[None])
    gin, gval, gw = finish(scale, gin, gval, gw)
    return (gin[None], gval[None], gw)


def solution(mesh):
    in_specs = (
        P("fsdp", "ctx", None),
        P("fsdp", "ctx", None),
        P("fsdp", "ctx", None),
        P("fsdp", None),
        P("fsdp", None, None),
        P("fsdp", "ctx"),
        P(),
        P(),
        P(),
    )
    out_specs = (P("fsdp", "ctx", None), P("fsdp", "ctx", None), P("fsdp", None))
    return jax.shard_map(body, mesh=mesh, in_specs=in_specs, out_specs=out_specs, check_vma=False)
```

```python
import functools
import math

import jax
import jax.numpy as jnp
from jax import lax
from jax.experimental import pallas as pl
from jax.experimental.pallas import tpu as pltpu
from jax.sharding import PartitionSpec as P

MESH = pl.DeviceIdType.MESH
F32 = jnp.float32
BF16 = jnp.bfloat16
TOK = 128
HEADS = 128
GROUPS = 8
STATE = 64
WIDE = 1024
COLS = 1152
PAIRS = 4
OWN = 256
HALF = 128
VMEM = pl.BlockSpec(memory_space=pltpu.VMEM)


def nn(a, b):
    return lax.dot_general(a, b, (((1,), (0,)), ((), ())), preferred_element_type=F32)


def nt(a, b):
    return lax.dot_general(a, b, (((1,), (1,)), ((), ())), preferred_element_type=F32)


def tn(a, b):
    return lax.dot_general(a, b, (((0,), (0,)), ((), ())), preferred_element_type=F32)


def split2(x):
    high = x.astype(BF16)
    return high, (x - high.astype(F32)).astype(BF16)


def split3(x):
    high, rest = x.astype(BF16), None
    rest = x - high.astype(F32)
    mid = rest.astype(BF16)
    return high, mid, (rest - mid.astype(F32)).astype(BF16)


def exact(mat, x):
    return sum(nn(mat, part) for part in split3(x))


def remote(src, dst, ssem, rsem, to):
    return pltpu.make_async_remote_copy(
        src_ref=src, dst_ref=dst, send_sem=ssem, recv_sem=rsem, device_id=to, device_id_type=MESH
    )


def block_masks(resets_ref):
    flags = resets_ref[...].astype(F32)
    row = lax.broadcasted_iota(jnp.int32, (TOK, TOK), 0)
    col = lax.broadcasted_iota(jnp.int32, (TOK, TOK), 1)
    seg_col = jnp.sum(jnp.where(col <= row, flags, 0.0), axis=1, keepdims=True)
    flag_col = jnp.sum(jnp.where(col == row, flags, 0.0), axis=1, keepdims=True)
    seg_row = jnp.sum(jnp.where(row <= col, flag_col, 0.0), axis=0, keepdims=True)
    valid = (col <= row) & (seg_col == seg_row)
    return row, col, valid, seg_col


def spread_matrix(g):
    head = lax.rem(lax.broadcasted_iota(jnp.int32, (256, WIDE), 0), 128)
    lane = lax.broadcasted_iota(jnp.int32, (256, WIDE), 1) // STATE
    return jnp.where(head == lane + 16 * g, 1.0, 0.0).astype(BF16)


def gather_matrix(g):
    lane = lax.broadcasted_iota(jnp.int32, (WIDE, HEADS), 0) // STATE
    head = lax.broadcasted_iota(jnp.int32, (WIDE, HEADS), 1)
    return jnp.where(head == lane + 16 * g, 1.0, 0.0).astype(BF16)


def per_head(x, mat):
    high, low = split2(x)
    return nn(high, mat) + nn(low, mat)


def layer_kernel(x_hbm, w_hbm, val_hbm, cot_hbm, init_hbm, resets_ref, bias_ref, rate_ref, skip_ref,
                 gin_hbm, gval_hbm, gw_hbm,
                 x_ref, w_ref, wsib_ref, xall, xo_ref, own_ref, away_ref, put_raw, got_raw, put_bc, got_bc,
                 b_ref, c_ref, val_ref, cot_ref, init_ref,
                 disc_ref, wgt_ref, rc_ref, step_ref, skipx_ref, totx_ref, dd_ref, logt_ref, logd_ref,
                 dlog_ref, dstep_ref, db_ref, dc_ref, out_ref, in_ref, back_ref, home_ref, tot_ref, tots_ref, lap_ref,
                 dall, gin_ref, ginfar_ref,
                 part_0, part_1, ra1_0, ra1_1, rb1_0, rb1_1, a1_0, a1_1, b1_0, b1_1, ra2_0, ra2_1, rb2_0, rb2_1,
                 fa_0, fa_1, fb_0, fb_1, a128_0, a128_1, b128_0, b128_1,
                 ssem, rsem, lsem, s1, r1, s2, r2, s3, r3, zsem, ysem):
    n = lax.axis_size("ctx")
    me, f = lax.axis_index("ctx"), lax.axis_index("fsdp")
    core, chip = lax.rem(f, 2), f // 2
    my_row, my_x = me // 4, lax.rem(me, 4)
    my_z, my_y = lax.rem(my_row, 4), my_row // 4
    sib = (me, f + 1 - 2 * core)
    far = (me, lax.rem(f + 2, 4))
    my_pair, my_eighth = me // 8, lax.rem(me, 8)
    my_plane = my_y * 4 + my_x
    bar = pltpu.get_barrier_semaphore()
    x_peers = [(me - my_x + lax.rem(my_x + k, 4), f) for k in range(1, 4)]
    z_peers = [(me + 4 * (lax.rem(my_z + k, 4) - my_z), f) for k in range(1, 4)]
    y_peer = (lax.rem(me + 16, n), f)
    direct = [far, sib] + x_peers + z_peers + [y_peer]
    for to in direct:
        pl.semaphore_signal(bar, inc=1, device_id=to, device_id_type=MESH)
    mine = pl.multiple_of(core * 1024, 1024)
    other = pl.multiple_of((1 - core) * 1024, 1024)
    base = pl.multiple_of(chip * 2048, 2048)
    far_base = pl.multiple_of((1 - chip) * 2048, 2048)
    own_at = pl.multiple_of(base + mine, 1024)
    other_at = pl.multiple_of(base + other, 1024)
    init_at = pl.multiple_of(my_pair * 16, 16)
    loads = [
        pltpu.make_async_copy(w_hbm, w_ref, lsem.at[0]),
        pltpu.make_async_copy(x_hbm, x_ref, lsem.at[1]),
        pltpu.make_async_copy(cot_hbm, cot_ref, lsem.at[2]),
        pltpu.make_async_copy(val_hbm, val_ref, lsem.at[3]),
        pltpu.make_async_copy(init_hbm.at[pl.ds(init_at, 16), :], init_ref.at[0], lsem.at[4]),
        pltpu.make_async_copy(init_hbm.at[pl.ds(init_at + 64, 16), :], init_ref.at[1], lsem.at[5]),
    ]
    for one in loads:
        one.start()
    pl.semaphore_wait(bar, len(direct))

    def link(k, source, target, to):
        return remote(source, target, ssem.at[k], rsem.at[k], to)

    send_x0 = link(0, x_hbm.at[:, pl.ds(pl.multiple_of(far_base + mine, 1024), 1024)], xall.at[pl.ds(128, 128), :], far)
    send_x1 = link(1, x_hbm.at[:, pl.ds(pl.multiple_of(far_base + other, 1024), 1024)], xo_ref, far)
    send_w = link(2, w_hbm, wsib_ref, sib)
    send_xo = link(3, x_hbm.at[:, pl.ds(other_at, 1024)], xall.at[pl.ds(256, 128), :], sib)
    for one in (send_x0, send_x1, send_w, send_xo):
        one.start()
    for to in z_peers:
        pl.semaphore_signal(zsem, inc=1, device_id=to, device_id_type=MESH)
    row, col, valid, seg_col = block_masks(resets_ref)
    loads[0].wait()
    loads[1].wait()
    xall[:128, :] = x_ref[:, pl.ds(own_at, 1024)]
    own_ref[...] = nn(xall[:128, :], w_ref[...])
    pl.semaphore_wait(zsem, 3)
    pl.semaphore_signal(ysem, inc=1, device_id=y_peer, device_id_type=MESH)
    send_w.wait_recv()
    own_ref[...] += nn(x_ref[:, pl.ds(other_at, 1024)], wsib_ref[...])
    send_x0.wait_recv()
    away_ref[...] = nn(xall[128:256, :], w_ref[...])
    send_x1.wait_recv()
    send_fwd = link(4, xo_ref, xall.at[pl.ds(384, 128), :], sib)
    send_fwd.start()
    put_raw[...] = away_ref[:, 1024:] + nn(xo_ref[...], wsib_ref[:, 1024:])
    send_raw = link(5, put_raw, got_raw, far)
    send_raw.start()

    def pair_cols(u):
        return pl.ds(pl.multiple_of(u * 128, 128), 128), pl.ds(pl.multiple_of(512 + u * 128, 128), 128)

    def bc_copy(u):
        return link(46 + u, put_bc.at[u], got_bc.at[u], far)

    def give(u, carry):
        for k, cols in enumerate(pair_cols(u)):
            product = away_ref[:, cols] + nn(xo_ref[...], wsib_ref[:, cols])
            put_bc[u, :, k * 128:(k + 1) * 128] = product.astype(BF16)
        bc_copy(u).start()
        return carry

    lax.fori_loop(0, PAIRS, give, 0)
    send_raw.wait_recv()
    raw = own_ref[:, 1024:] + got_raw[...] + bias_ref[...]
    step = jnp.maximum(raw, 0.0) + jnp.log1p(jnp.exp(-jnp.abs(raw)))
    low_tri = jnp.where(col <= row, 1.0, 0.0).astype(BF16)
    log_decay = exact(low_tri, -rate_ref[...] * step)
    final = log_decay[TOK - 1:, :]
    last_seg = seg_col[TOK - 1:, :]
    tail = jnp.where(seg_col == last_seg, jnp.exp(final - log_decay), 0.0)
    reach = jnp.where(seg_col == 0.0, jnp.exp(log_decay), 0.0)
    total = jnp.where(last_seg == 0.0, jnp.exp(final), 0.0)
    tot_ref[...] = jnp.broadcast_to(total, (8, HEADS))
    logd_ref[...] = log_decay
    logt_ref[...] = jnp.transpose(log_decay)
    few = lax.broadcasted_iota(jnp.int32, (16, HEADS), 0)
    extra = jnp.where(few < 8, skip_ref[...], total)
    stack = jnp.concatenate([step, tail, reach, extra], axis=0)
    stack = jnp.concatenate(split2(stack), axis=1)
    loads[2].wait()
    loads[3].wait()
    pl.semaphore_wait(ysem, 1)
    def wide(g):
        return pl.ds(pl.multiple_of(g * WIDE, WIDE), WIDE)

    def out_copy(h, to):
        return remote(out_ref.at[h, to], in_ref.at[h, me], s1.at[h, to], r1.at[h, me], (to, f))

    def own_copy(h):
        return pltpu.make_async_copy(out_ref.at[h, me], in_ref.at[h, me], lsem.at[18 + h])

    def tot_copy(to):
        return remote(tot_ref, tots_ref.at[me], s3.at[to], r3.at[me], (to, f))

    def spray(copy, own, h):
        own(h).start()

        def turn(t, carry):
            to_x = lax.rem(my_x + t, 4)
            to_z = lax.rem(my_z + t + t // 4, 4)
            near = 16 * my_y + 4 * to_z + to_x
            copy(h, 16 * (1 - my_y) + 4 * to_z + to_x).start()

            @pl.when(t != 0)
            def _():
                copy(h, near).start()

            return carry

        lax.fori_loop(0, 16, turn, 0)

    def all_sent(copy, h):
        def gone(i, carry):
            copy(h, lax.rem(me + i, n)).wait_send()
            return carry

        lax.fori_loop(1, n, gone, 0)

    for h in range(2):
        for u in (2 * h, 2 * h + 1):
            bc_copy(u).wait_recv()
            cols_b, cols_c = pair_cols(u)
            pair_b = (own_ref[:, cols_b] + got_bc[u, :, :128].astype(F32)).astype(BF16)
            pair_c = (own_ref[:, cols_c] + got_bc[u, :, 128:].astype(F32)).astype(BF16)
            for k in range(2):
                b_ref[2 * u + k] = pair_b[:, k * STATE:(k + 1) * STATE]
                c_ref[2 * u + k] = pair_c[:, k * STATE:(k + 1) * STATE]

        def produce(i, carry):
            block = lax.rem(my_pair + i, PAIRS)
            g = 4 * h + block
            spread = nn(stack, spread_matrix(g))
            step_x = spread[:TOK]
            cot = cot_ref[:, wide(g)].astype(F32)
            disc = (step_x * val_ref[:, wide(g)].astype(F32)).astype(BF16)
            wgt = (spread[TOK:2 * TOK] * disc.astype(F32)).astype(BF16)
            rc = (spread[2 * TOK:3 * TOK] * cot).astype(BF16)
            step_ref[g] = step_x
            skipx_ref[g] = spread[3 * TOK:3 * TOK + 8]
            totx_ref[g] = spread[3 * TOK + 8:3 * TOK + 16]
            disc_ref[g] = disc
            wgt_ref[g] = wgt
            rc_ref[g] = rc
            local = tn(b_ref[g], wgt).astype(BF16)
            first = tn(c_ref[g], rc).astype(BF16)
            for j in range(8):
                out_ref[h, block * 8 + j, :64, :] = local[:, j * HALF:(j + 1) * HALF]
                out_ref[h, block * 8 + j, 64:, :] = first[:, j * HALF:(j + 1) * HALF]
            return carry

        lax.fori_loop(0, PAIRS, produce, 0)
        spray(out_copy, own_copy, h)

    def send_totals(i, carry):
        tot_copy(lax.rem(me + i, n)).start()
        return carry

    lax.fori_loop(1, n, send_totals, 0)
    tots_ref[me] = tot_ref[...]

    dlog_ref[...] = jnp.zeros_like(dlog_ref)
    half = lax.broadcasted_iota(jnp.int32, (1, TOK), 1) < STATE
    left = jnp.where(half, 1.0, 0.0)
    left_b = left.astype(BF16)
    right_b = (1.0 - left).astype(BF16)
    bad = jnp.where(valid, 0.0, 1.0)

    def inside(g, carry):
        b, c = b_ref[g], c_ref[g]
        scores = nt(c, b)
        logs = pltpu.roll(logd_ref[...], lax.rem(HEADS - 16 * g, HEADS), 1)
        d_scores = jnp.zeros((TOK, TOK), F32)
        errs = []
        for q in range(8):
            lanes = pl.ds(pl.multiple_of(g * WIDE + q * 128, 128), 128)
            cot_p = cot_ref[:, lanes]
            disc_p = disc_ref[g, :, q * 128:(q + 1) * 128]
            stacked = jnp.concatenate([disc_p * left_b, disc_p * right_b], axis=0)
            d_mixed = nt(cot_p, stacked)
            mixed = []
            for k in range(2):
                head = 2 * q + k
                span = logs[:, head:head + 1] - logt_ref[pl.ds(g * 16 + head, 1), :]
                weights = jnp.exp(jnp.where(valid, span, -1e30))
                d_scores += d_mixed[:, k * TOK:(k + 1) * TOK] * weights
                mixed.append((weights * scores).astype(BF16))
            mixed = jnp.concatenate(mixed, axis=1)
            inner = nn(mixed, stacked)
            both = tn(mixed, cot_p)
            dd = both[:TOK] * left + both[TOK:] * (1.0 - left)
            dd_ref[g, :, q * 128:(q + 1) * 128] = dd.astype(BF16)
            errs.append(cot_p.astype(F32) * inner - disc_p.astype(F32) * dd)
        dlog_ref[...] += per_head(jnp.concatenate(errs, axis=1), gather_matrix(g))
        ds = d_scores.astype(BF16)
        dc_ref[g] = nn(ds, b)
        db_ref[g] = tn(ds, c)
        return carry

    lax.fori_loop(0, GROUPS, inside, 0)
    loads[4].wait()
    loads[5].wait()
    pick_row = lax.broadcasted_iota(jnp.int32, (16, 16), 0)
    pick_col = lax.broadcasted_iota(jnp.int32, (16, 16), 1)
    pick = jnp.where(pick_col == pick_row + 2 * my_eighth, 1.0, 0.0).astype(BF16)
    picked = [nn(pick, init_ref[h]) for h in range(2)]
    turned = [picked[h][r:r + 1, i * 128:(i + 1) * 128] for h in range(2) for r in range(2) for i in range(32)]
    turned = jnp.transpose(jnp.concatenate(turned, axis=0)).astype(BF16)
    from_i = lax.broadcasted_iota(jnp.int32, (128, OWN), 0)
    to_p = lax.broadcasted_iota(jnp.int32, (128, OWN), 1)
    even = jnp.where(to_p == 2 * from_i, 1.0, 0.0).astype(BF16)
    odd = jnp.where(to_p == 2 * from_i + 1, 1.0, 0.0).astype(BF16)
    init_state = nn(turned[:64], even) + nn(turned[64:], odd)

    def total_in(i, carry):
        src = lax.rem(me + n - i, n)
        remote(tot_ref, tots_ref.at[src], s3.at[src], r3.at[src], (src, f)).wait_recv()
        return carry

    lax.fori_loop(1, n, total_in, 0)
    from_head = lax.broadcasted_iota(jnp.int32, (HEADS, HALF), 0)
    to_lane = lax.broadcasted_iota(jnp.int32, (HEADS, HALF), 1) // STATE
    for h in range(2):
        owned = jnp.where(from_head == to_lane + 64 * h + 2 * me, 1.0, 0.0).astype(BF16)
        lap_ref[h] = sum(nn(part_of, owned) for part_of in split3(tots_ref[:, 0, :]))

    def back_copy(h, to):
        return remote(back_ref.at[h, to], home_ref.at[h, me], s2.at[h, to], r2.at[h, me], (to, f))

    def own_back(h):
        return pltpu.make_async_copy(back_ref.at[h, me], home_ref.at[h, me], lsem.at[20 + h])

    for h in range(2):
        lanes = slice(h * HALF, (h + 1) * HALF)
        own_copy(h).wait()

        def arrive(i, carry):
            src = lax.rem(me + n - i, n)
            remote(out_ref.at[h, src], in_ref.at[h, src], s1.at[h, src], r1.at[h, src], (src, f)).wait_recv()
            return carry

        lax.fori_loop(1, n, arrive, 0)

        def laps(i, state):
            ahead, behind = state
            j = n - 1 - i
            back_ref[h, i, :64, :] = ahead.astype(BF16)
            back_ref[h, j, 64:, :] = behind.astype(BF16)
            ahead = lap_ref[h, pl.ds(i, 1), :] * ahead + in_ref[h, i, :64, :].astype(F32)
            behind = in_ref[h, j, 64:, :].astype(F32) + lap_ref[h, pl.ds(j, 1), :] * behind
            return ahead, behind

        lax.fori_loop(0, n, laps, (init_state[:, lanes], jnp.zeros((STATE, HALF), F32)))

        spray(back_copy, own_back, h)

    for h in range(2):
        own_back(h).wait()
    dstep_ref[...] = jnp.zeros_like(dstep_ref)

    def save(g):
        return pltpu.make_async_copy(disc_ref.at[g], gval_hbm.at[:, wide(g)], lsem.at[8 + g])

    def rows(at, count):
        return pl.ds(pl.multiple_of(at, count), count)

    def x_peer(x):
        return (me - my_x + x, f)

    def z_peer(z):
        return (me + 4 * (z - my_z), f)

    def row_peer(q):
        return (4 * q + my_x, f)

    def plane_peer(q):
        return (16 * (q // 4) + 4 * my_z + lax.rem(q, 4), f)

    def exchange(k, peer, mine_at, source, target, count=4):
        copies = []
        for step_to in range(1, count):
            to = lax.rem(mine_at + step_to, count)
            copies.append(remote(source(to), target(mine_at), ssem.at[k + to], rsem.at[k + mine_at], peer(to)))
        return copies

    def landed(k, peer, mine_at, source, target, count=4):
        for step_to in range(1, count):
            at = lax.rem(mine_at + step_to, count)
            remote(source(at), target(at), ssem.at[k + at], rsem.at[k + at], peer(at)).wait_recv()

    def summed(first, got, at, count=4):
        total = first.astype(F32)
        for step_to in range(1, count):
            total += got[lax.rem(at + step_to, count)].astype(F32)
        return total

    chunk_cols = (slice(0, 512), slice(512, 1152))
    bufs = (
        (part_0, ra1_0, rb1_0, a1_0, b1_0, ra2_0, rb2_0, fa_0, fb_0, a128_0, b128_0),
        (part_1, ra1_1, rb1_1, a1_1, b1_1, ra2_1, rb2_1, fa_1, fb_1, a128_1, b128_1),
    )
    sent = []

    def stages(c):
        part, ra1, rb1, a1, b1, ra2, rb2, fa, fb, a128, b128 = bufs[c]
        k = 100 * c
        cols = chunk_cols[c]
        return (
            (k + 12, x_peer, my_x, lambda x: part.at[rows(128 * x, 128), :], lambda x: ra1.at[x]),
            (k + 16, z_peer, my_z, lambda z: part.at[rows(512 + 128 * z, 128), :], lambda z: rb1.at[z]),
            (k + 20, row_peer, my_row, lambda q: a1.at[rows(16 * q, 16), :], lambda q: ra2.at[q], 8),
            (k + 28, plane_peer, my_plane, lambda q: b1.at[rows(16 * q, 16), :], lambda q: rb2.at[q], 8),
            (k + 66, row_peer, my_row, lambda q: fa, lambda q: a128.at[rows(16 * q, 16), :], 8),
            (k + 74, plane_peer, my_plane, lambda q: fb, lambda q: b128.at[rows(16 * q, 16), :], 8),
            (k + 38, x_peer, my_x, lambda x: a128, lambda x: gw_hbm.at[rows(128 * x, 128), cols]),
            (k + 42, z_peer, my_z, lambda z: b128, lambda z: gw_hbm.at[rows(512 + 128 * z, 128), cols]),
        )

    def go(stage):
        copies = exchange(*stage)
        for one in copies:
            one.start()
        sent.extend(copies)

    def d_copies(h):
        cols = chunk_cols[h]
        own_d, far_d = dall.at[:128, cols], dall.at[128:256, cols]
        return (
            link(50 + 3 * h, own_d, far_d, far),
            link(51 + 3 * h, own_d, dall.at[256:384, cols], sib),
            link(52 + 3 * h, far_d, dall.at[384:512, cols], sib),
        )

    def give_d(h):
        for one in d_copies(h)[:2]:
            one.start()

    def first_stage(h):
        to_far, to_sib, forward = d_copies(h)
        to_far.wait_recv()
        forward.start()
        to_sib.wait_recv()
        forward.wait_recv()
        part, cols = bufs[h][0], chunk_cols[h]

        def product(at):
            part[rows(at, 128), :] = tn(xall[:, rows(at, 128)], dall[:, cols]).astype(BF16)

        a_sent, b_sent = exchange(*stages(h)[0]), exchange(*stages(h)[1])
        for k in range(3):
            product(128 * lax.rem(my_x + k + 1, 4))
            a_sent[k].start()
            product(512 + 128 * lax.rem(my_z + k + 1, 4))
            b_sent[k].start()
        product(128 * my_x)
        product(512 + 128 * my_z)
        sent.extend(a_sent + b_sent)

    def second_stage(c):
        part, ra1, rb1, a1, b1 = bufs[c][:5]
        stage = stages(c)
        landed(*stage[0])
        a1[...] = summed(part[rows(128 * my_x, 128), :], ra1, my_x).astype(BF16)
        go(stage[2])
        landed(*stage[1])
        b1[...] = summed(part[rows(512 + 128 * my_z, 128), :], rb1, my_z).astype(BF16)
        go(stage[3])

    def third_stage(c):
        a1, b1, ra2, rb2, fa, fb, a128, b128 = bufs[c][3:]
        stage = stages(c)
        landed(*stage[2])
        fa[...] = summed(a1[rows(16 * my_row, 16), :], ra2, my_row, 8).astype(BF16)
        go(stage[4])
        landed(*stage[3])
        fb[...] = summed(b1[rows(16 * my_plane, 16), :], rb2, my_plane, 8).astype(BF16)
        go(stage[5])
        a128[rows(16 * my_row, 16), :] = fa[...]
        b128[rows(16 * my_plane, 16), :] = fb[...]

    def keep(c):
        a128, b128 = bufs[c][9:]
        cols = chunk_cols[c]
        return (
            pltpu.make_async_copy(a128, gw_hbm.at[rows(128 * my_x, 128), cols], lsem.at[(16, 22)[c]]),
            pltpu.make_async_copy(b128, gw_hbm.at[rows(512 + 128 * my_z, 128), cols], lsem.at[(17, 23)[c]]),
        )

    def last_stage(c):
        stage = stages(c)
        landed(*stage[4])
        go(stage[6])
        landed(*stage[5])
        go(stage[7])
        for one in keep(c):
            one.start()

    def input_product(at, target):
        d = dall[at:at + 128, :]
        d = jnp.concatenate([d[:, :256], d[:, 512:768], d[:, 256:512], d[:, 768:]], axis=1)
        target[:, pl.ds(mine, 1024)] = nt(d, w_ref[...]).astype(BF16)
        target[:, pl.ds(other, 1024)] = nt(d, wsib_ref[...]).astype(BF16)

    for h in range(2):

        def consume(i, carry):
            block = lax.rem(my_pair + PAIRS - i, PAIRS)
            g = 4 * h + block
            for j in range(8):
                src = block * 8 + j

                @pl.when(src != me)
                def _():
                    remote(back_ref.at[h, src], home_ref.at[h, src], s2.at[h, src], r2.at[h, src], (src, f)).wait_recv()

            got = jnp.concatenate([home_ref[h, block * 8 + j] for j in range(8)], axis=1)
            start, end = got[:64], got[64:]
            b, c = b_ref[g], c_ref[g]
            rc, wgt, disc = rc_ref[g], wgt_ref[g], disc_ref[g].astype(F32)
            carried = nn(c, start)
            d_wgt = nn(b, end)
            dc_ref[g] += nt(rc, start)
            db_ref[g] += nt(wgt, end)
            pull = wgt.astype(F32) * d_wgt
            mat = gather_matrix(g)
            err = rc.astype(F32) * carried - pull
            ends = jnp.sum(pull, axis=0, keepdims=True)
            ends += totx_ref[g, :1, :] * jnp.sum(start.astype(F32) * end.astype(F32), axis=0, keepdims=True)
            at_end = lax.broadcasted_iota(jnp.int32, (TOK, WIDE), 0) == TOK - 1
            err = err + jnp.where(at_end, ends, 0.0)
            dlog_ref[...] += per_head(err, mat)
            spread = nn(stack[TOK:2 * TOK], spread_matrix(g))
            d_disc = dd_ref[g].astype(F32) + spread * d_wgt
            val = val_ref[:, wide(g)].astype(F32)
            dstep_ref[...] += per_head(d_disc * val, mat)
            gval = skipx_ref[g, :1, :] * cot_ref[:, wide(g)].astype(F32) + step_ref[g] * d_disc
            disc_ref[g] = gval.astype(BF16)
            save(g).start()
            return carry

        lax.fori_loop(0, PAIRS, consume, 0)
        some = range(4 * h, 4 * h + 4)
        at = 512 * h
        dall[:128, at:at + 256] = jnp.concatenate([db_ref[g] for g in some], axis=1).astype(BF16)
        dall[:128, at + 256:at + 512] = jnp.concatenate([dc_ref[g] for g in some], axis=1).astype(BF16)
        if h == 0:
            give_d(0)
    up_tri = jnp.where(col >= row, 1.0, 0.0).astype(BF16)
    d_inc = exact(up_tri, dlog_ref[...])
    d_step = dstep_ref[...] - rate_ref[...] * d_inc
    dall[:128, 1024:] = (d_step / (1.0 + jnp.exp(-raw))).astype(BF16)
    give_d(1)
    send_xo.wait_recv()
    send_fwd.wait_recv()
    first_stage(0)
    input_product(0, gin_ref)
    save_gin = pltpu.make_async_copy(gin_ref, gin_hbm.at[:, pl.ds(base, 2048)], lsem.at[7])
    save_gin.start()
    first_stage(1)
    second_stage(0)
    input_product(128, ginfar_ref)
    send_gin = link(11, ginfar_ref, gin_hbm.at[:, pl.ds(base, 2048)], far)
    third_stage(0)
    second_stage(1)
    third_stage(1)
    send_gin.start()
    last_stage(0)
    last_stage(1)

    def drain(i, carry):
        to = lax.rem(me + i, n)
        out_copy(0, to).wait_send()
        out_copy(1, to).wait_send()
        back_copy(0, to).wait_send()
        back_copy(1, to).wait_send()
        tot_copy(to).wait_send()
        return carry

    lax.fori_loop(1, n, drain, 0)
    for one in (send_x0, send_x1, send_w, send_xo, send_fwd, send_raw, send_gin):
        one.wait_send()
    for one in [*d_copies(0), *d_copies(1)] + [bc_copy(u) for u in range(PAIRS)]:
        one.wait_send()
    send_gin.wait_recv()
    save_gin.wait()

    def saved(g, carry):
        save(g).wait()
        return carry

    lax.fori_loop(0, GROUPS, saved, 0)
    for c in range(2):
        for one in keep(c):
            one.wait()
        for stage in stages(c)[6:]:
            landed(*stage)
    for one in sent:
        one.wait_send()


def layer(x, w, val, cot, init, resets, bias, rate, skip):
    n = 32
    slab = (GROUPS, TOK, WIDE)
    hbm = pl.BlockSpec(memory_space=pl.ANY)
    vm = pltpu.VMEM
    dma = pltpu.SemaphoreType.DMA
    return pl.pallas_call(
        layer_kernel,
        out_shape=(
            jax.ShapeDtypeStruct((TOK, 4096), BF16),
            jax.ShapeDtypeStruct((TOK, GROUPS * WIDE), BF16),
            jax.ShapeDtypeStruct((1024, COLS), BF16),
        ),
        in_specs=[hbm] * 5 + [VMEM] * 4,
        out_specs=[hbm] * 3,
        scratch_shapes=[
            vm((TOK, 4096), BF16),
            vm((1024, COLS), BF16),
            vm((1024, COLS), BF16),
            vm((4 * TOK, 1024), BF16),
            vm((TOK, 1024), BF16),
            vm((TOK, COLS), F32),
            vm((TOK, COLS), F32),
            vm((TOK, HEADS), F32),
            vm((TOK, HEADS), F32),
            vm((PAIRS, TOK, 256), BF16),
            vm((PAIRS, TOK, 256), BF16),
            vm((GROUPS, TOK, STATE), BF16),
            vm((GROUPS, TOK, STATE), BF16),
            vm((TOK, GROUPS * WIDE), BF16),
            vm((TOK, GROUPS * WIDE), BF16),
            vm((2, 16, 4096), BF16),
            vm(slab, BF16),
            vm(slab, BF16),
            vm(slab, BF16),
            vm(slab, F32),
            vm((GROUPS, 8, WIDE), F32),
            vm((GROUPS, 8, WIDE), F32),
            vm(slab, BF16),
            vm((HEADS, TOK), F32),
            vm((TOK, HEADS), F32),
            vm((TOK, HEADS), F32),
            vm((TOK, HEADS), F32),
            vm((GROUPS, TOK, STATE), F32),
            vm((GROUPS, TOK, STATE), F32),
            vm((2, n, 128, HALF), BF16),
            vm((2, n, 128, HALF), BF16),
            vm((2, n, 128, HALF), BF16),
            vm((2, n, 128, HALF), BF16),
            vm((8, HEADS), F32),
            vm((n, 8, HEADS), F32),
            vm((2, n, HALF), F32),
            vm((4 * TOK, COLS), BF16),
            vm((TOK, 2048), BF16),
            vm((TOK, 2048), BF16),
            *[vm(rows + (cols,), BF16)
              for rows in ((1024,), (4, 128), (4, 128), (128,), (128,), (8, 16), (8, 16), (16,), (16,), (128,), (128,))
              for cols in (512, 640)],
            dma((182,)),
            dma((182,)),
            dma((24,)),
            dma((2, n)),
            dma((2, n)),
            dma((2, n)),
            dma((2, n)),
            dma((n,)),
            dma((n,)),
            pltpu.SemaphoreType.REGULAR,
            pltpu.SemaphoreType.REGULAR,
        ],
        compiler_params=pltpu.CompilerParams(
            collective_id=0, has_side_effects=True, vmem_limit_bytes=60 * 2**20
        ),
        name="layer",
    )(x, w, val, cot, init, resets, bias, rate, skip)


def finish_kernel(scale, gin, gval, gw, gin_out, gval_out, gw_out, narrow, full, gin_v, gval_v, sem_i, sem_o):
    def some(k):
        return pl.ds(128 * k, 128)

    def pick(k):
        return pl.ds(32 * k, 32)

    loads = [pltpu.make_async_copy(gw.at[some(k), :], narrow.at[some(k), :], sem_i.at[k]) for k in range(8)]
    stores = [pltpu.make_async_copy(full.at[some(k), :], gw_out.at[some(k), :], sem_o.at[k]) for k in range(8)]
    loads += [pltpu.make_async_copy(gval.at[pick(k), :], gval_v.at[pick(k), :], sem_i.at[8 + k]) for k in range(4)]
    stores += [pltpu.make_async_copy(gval_v.at[pick(k), :], gval_out.at[pick(k), :], sem_o.at[8 + k]) for k in range(4)]
    loads.append(pltpu.make_async_copy(gin, gin_v, sem_i.at[12]))
    stores.append(pltpu.make_async_copy(gin_v, gin_out, sem_o.at[12]))
    for one in loads:
        one.start()
    for k in range(13):
        loads[k].wait()
        if k < 8:
            for to, at, wide in ((0, 0, 256), (256, 512, 256), (512, 256, 256), (768, 768, 384)):
                full[some(k), to:to + wide] = narrow[some(k), at:at + wide].astype(F32) * scale
        stores[k].start()
    for one in stores:
        one.wait()


def finish(scale, gin, gval, gw):
    hbm = pl.BlockSpec(memory_space=pl.ANY)
    return pl.pallas_call(
        functools.partial(finish_kernel, scale),
        out_shape=(
            jax.ShapeDtypeStruct(gin.shape, BF16),
            jax.ShapeDtypeStruct(gval.shape, BF16),
            jax.ShapeDtypeStruct(gw.shape, F32),
        ),
        in_specs=[hbm] * 3,
        out_specs=[hbm] * 3,
        scratch_shapes=[
            pltpu.VMEM((1024, COLS), BF16),
            pltpu.VMEM((1024, COLS), F32),
            pltpu.VMEM((TOK, 4096), BF16),
            pltpu.VMEM((TOK, GROUPS * WIDE), BF16),
            pltpu.SemaphoreType.DMA((13,)),
            pltpu.SemaphoreType.DMA((13,)),
        ],
        compiler_params=pltpu.CompilerParams(vmem_limit_bytes=60 * 2**20),
        name="finish",
    )(gin, gval, gw)


def body(inputs, values, cotangent, weight, init_state, resets, dt_bias, decay_rate, skip):
    scale = 1.0 / math.sqrt(lax.axis_size("fsdp") * TOK * lax.axis_size("ctx"))
    gin, gval, gw = layer(inputs[0], weight, values[0], cotangent[0], init_state[0], resets,
                          dt_bias[None], decay_rate[None], skip[None])
    gin, gval, gw = finish(scale, gin, gval, gw)
    return (gin[None], gval[None], gw)


def solution(mesh):
    in_specs = (
        P("fsdp", "ctx", None),
        P("fsdp", "ctx", None),
        P("fsdp", "ctx", None),
        P("fsdp", None),
        P("fsdp", None, None),
        P("fsdp", "ctx"),
        P(),
        P(),
        P(),
    )
    out_specs = (P("fsdp", "ctx", None), P("fsdp", "ctx", None), P("fsdp", None))
    return jax.shard_map(body, mesh=mesh, in_specs=in_specs, out_specs=out_specs, check_vma=False)
```

```python
import functools
import math

import jax
import jax.numpy as jnp
from jax import lax
from jax.experimental import pallas as pl
from jax.experimental.pallas import tpu as pltpu
from jax.sharding import PartitionSpec as P

MESH = pl.DeviceIdType.MESH
F32 = jnp.float32
BF16 = jnp.bfloat16
TOK = 128
HEADS = 128
GROUPS = 8
STATE = 64
WIDE = 1024
COLS = 1152
PAIRS = 4
OWN = 256
HALF = 128
VMEM = pl.BlockSpec(memory_space=pltpu.VMEM)


def nn(a, b):
    return lax.dot_general(a, b, (((1,), (0,)), ((), ())), preferred_element_type=F32)


def nt(a, b):
    return lax.dot_general(a, b, (((1,), (1,)), ((), ())), preferred_element_type=F32)


def tn(a, b):
    return lax.dot_general(a, b, (((0,), (0,)), ((), ())), preferred_element_type=F32)


def split2(x):
    high = x.astype(BF16)
    return high, (x - high.astype(F32)).astype(BF16)


def split3(x):
    high, rest = x.astype(BF16), None
    rest = x - high.astype(F32)
    mid = rest.astype(BF16)
    return high, mid, (rest - mid.astype(F32)).astype(BF16)


def exact(mat, x):
    return sum(nn(mat, part) for part in split3(x))


def remote(src, dst, ssem, rsem, to):
    return pltpu.make_async_remote_copy(
        src_ref=src, dst_ref=dst, send_sem=ssem, recv_sem=rsem, device_id=to, device_id_type=MESH
    )


def block_masks(resets_ref):
    flags = resets_ref[...].astype(F32)
    row = lax.broadcasted_iota(jnp.int32, (TOK, TOK), 0)
    col = lax.broadcasted_iota(jnp.int32, (TOK, TOK), 1)
    seg_col = jnp.sum(jnp.where(col <= row, flags, 0.0), axis=1, keepdims=True)
    flag_col = jnp.sum(jnp.where(col == row, flags, 0.0), axis=1, keepdims=True)
    seg_row = jnp.sum(jnp.where(row <= col, flag_col, 0.0), axis=0, keepdims=True)
    valid = (col <= row) & (seg_col == seg_row)
    return row, col, valid, seg_col


def spread_matrix(g):
    head = lax.rem(lax.broadcasted_iota(jnp.int32, (256, WIDE), 0), 128)
    lane = lax.broadcasted_iota(jnp.int32, (256, WIDE), 1) // STATE
    return jnp.where(head == lane + 16 * g, 1.0, 0.0).astype(BF16)


def gather_matrix(g):
    lane = lax.broadcasted_iota(jnp.int32, (WIDE, HEADS), 0) // STATE
    head = lax.broadcasted_iota(jnp.int32, (WIDE, HEADS), 1)
    return jnp.where(head == lane + 16 * g, 1.0, 0.0).astype(BF16)


def per_head(x, mat):
    high, low = split2(x)
    return nn(high, mat) + nn(low, mat)


def layer_kernel(x_hbm, w_hbm, val_hbm, cot_hbm, init_hbm, resets_ref, bias_ref, rate_ref, skip_ref,
                 gin_hbm, gval_hbm, gw_hbm,
                 x_ref, w_ref, wsib_ref, xall, xo_ref, own_ref, away_ref, put_raw, got_raw, put_bc, got_bc,
                 b_ref, c_ref, val_ref, cot_ref, init_ref,
                 disc_ref, wgt_ref, rc_ref, step_ref, skipx_ref, totx_ref, dd_ref, logt_ref, logd_ref,
                 dlog_ref, dstep_ref, db_ref, dc_ref, out_ref, in_ref, back_ref, home_ref, tot_ref, tots_ref, lap_ref,
                 dall, gin_ref, ginfar_ref,
                 part_0, part_1, ra1_0, ra1_1, rb1_0, rb1_1, a1_0, a1_1, b1_0, b1_1, ra2_0, ra2_1, rb2_0, rb2_1,
                 fa_0, fa_1, fb_0, fb_1, a128_0, a128_1, b128_0, b128_1,
                 ssem, rsem, lsem, s1, r1, s2, r2, s3, r3, zsem, ysem):
    n = lax.axis_size("ctx")
    me, f = lax.axis_index("ctx"), lax.axis_index("fsdp")
    core, chip = lax.rem(f, 2), f // 2
    my_row, my_x = me // 4, lax.rem(me, 4)
    my_z, my_y = lax.rem(my_row, 4), my_row // 4
    sib = (me, f + 1 - 2 * core)
    far = (me, lax.rem(f + 2, 4))
    my_pair, my_eighth = me // 8, lax.rem(me, 8)
    my_plane = my_y * 4 + my_x
    bar = pltpu.get_barrier_semaphore()
    x_peers = [(me - my_x + lax.rem(my_x + k, 4), f) for k in range(1, 4)]
    z_peers = [(me + 4 * (lax.rem(my_z + k, 4) - my_z), f) for k in range(1, 4)]
    y_peer = (lax.rem(me + 16, n), f)
    direct = [far, sib] + x_peers + z_peers + [y_peer]
    for to in direct:
        pl.semaphore_signal(bar, inc=1, device_id=to, device_id_type=MESH)
    mine = pl.multiple_of(core * 1024, 1024)
    other = pl.multiple_of((1 - core) * 1024, 1024)
    base = pl.multiple_of(chip * 2048, 2048)
    far_base = pl.multiple_of((1 - chip) * 2048, 2048)
    own_at = pl.multiple_of(base + mine, 1024)
    other_at = pl.multiple_of(base + other, 1024)
    init_at = pl.multiple_of(my_pair * 16, 16)
    loads = [
        pltpu.make_async_copy(w_hbm, w_ref, lsem.at[0]),
        pltpu.make_async_copy(x_hbm, x_ref, lsem.at[1]),
        pltpu.make_async_copy(cot_hbm, cot_ref, lsem.at[2]),
        pltpu.make_async_copy(val_hbm, val_ref, lsem.at[3]),
        pltpu.make_async_copy(init_hbm.at[pl.ds(init_at, 16), :], init_ref.at[0], lsem.at[4]),
        pltpu.make_async_copy(init_hbm.at[pl.ds(init_at + 64, 16), :], init_ref.at[1], lsem.at[5]),
    ]
    for one in loads:
        one.start()
    pl.semaphore_wait(bar, len(direct))

    def link(k, source, target, to):
        return remote(source, target, ssem.at[k], rsem.at[k], to)

    send_x0 = link(0, x_hbm.at[:, pl.ds(pl.multiple_of(far_base + mine, 1024), 1024)], xall.at[pl.ds(128, 128), :], far)
    send_x1 = link(1, x_hbm.at[:, pl.ds(pl.multiple_of(far_base + other, 1024), 1024)], xo_ref, far)
    send_w = link(2, w_hbm, wsib_ref, sib)
    send_xo = link(3, x_hbm.at[:, pl.ds(other_at, 1024)], xall.at[pl.ds(256, 128), :], sib)
    for one in (send_x0, send_x1, send_w, send_xo):
        one.start()
    for to in z_peers:
        pl.semaphore_signal(zsem, inc=1, device_id=to, device_id_type=MESH)
    row, col, valid, seg_col = block_masks(resets_ref)
    loads[0].wait()
    loads[1].wait()
    xall[:128, :] = x_ref[:, pl.ds(own_at, 1024)]
    own_ref[...] = nn(xall[:128, :], w_ref[...])
    pl.semaphore_wait(zsem, 3)
    pl.semaphore_signal(ysem, inc=1, device_id=y_peer, device_id_type=MESH)
    send_w.wait_recv()
    own_ref[...] += nn(x_ref[:, pl.ds(other_at, 1024)], wsib_ref[...])
    send_x0.wait_recv()
    away_ref[...] = nn(xall[128:256, :], w_ref[...])
    send_x1.wait_recv()
    send_fwd = link(4, xo_ref, xall.at[pl.ds(384, 128), :], sib)
    send_fwd.start()
    put_raw[...] = away_ref[:, 1024:] + nn(xo_ref[...], wsib_ref[:, 1024:])
    send_raw = link(5, put_raw, got_raw, far)
    send_raw.start()

    def pair_cols(u):
        return pl.ds(pl.multiple_of(u * 128, 128), 128), pl.ds(pl.multiple_of(512 + u * 128, 128), 128)

    def bc_copy(u):
        return link(46 + u, put_bc.at[u], got_bc.at[u], far)

    def give(u, carry):
        for k, cols in enumerate(pair_cols(u)):
            product = away_ref[:, cols] + nn(xo_ref[...], wsib_ref[:, cols])
            put_bc[u, :, k * 128:(k + 1) * 128] = product.astype(BF16)
        bc_copy(u).start()
        return carry

    lax.fori_loop(0, PAIRS, give, 0)
    send_raw.wait_recv()
    raw = own_ref[:, 1024:] + got_raw[...] + bias_ref[...]
    step = jnp.maximum(raw, 0.0) + jnp.log1p(jnp.exp(-jnp.abs(raw)))
    low_tri = jnp.where(col <= row, 1.0, 0.0).astype(BF16)
    log_decay = exact(low_tri, -rate_ref[...] * step)
    final = log_decay[TOK - 1:, :]
    last_seg = seg_col[TOK - 1:, :]
    tail = jnp.where(seg_col == last_seg, jnp.exp(final - log_decay), 0.0)
    reach = jnp.where(seg_col == 0.0, jnp.exp(log_decay), 0.0)
    total = jnp.where(last_seg == 0.0, jnp.exp(final), 0.0)
    tot_ref[...] = jnp.broadcast_to(total, (8, HEADS))
    logd_ref[...] = log_decay
    logt_ref[...] = jnp.transpose(log_decay)
    few = lax.broadcasted_iota(jnp.int32, (16, HEADS), 0)
    extra = jnp.where(few < 8, skip_ref[...], total)
    stack = jnp.concatenate([step, tail, reach, extra], axis=0)
    stack = jnp.concatenate(split2(stack), axis=1)
    loads[2].wait()
    loads[3].wait()
    pl.semaphore_wait(ysem, 1)
    def wide(g):
        return pl.ds(pl.multiple_of(g * WIDE, WIDE), WIDE)

    def out_copy(h, to):
        return remote(out_ref.at[h, to], in_ref.at[h, me], s1.at[h, to], r1.at[h, me], (to, f))

    def own_copy(h):
        return pltpu.make_async_copy(out_ref.at[h, me], in_ref.at[h, me], lsem.at[18 + h])

    def tot_copy(to):
        return remote(tot_ref, tots_ref.at[me], s3.at[to], r3.at[me], (to, f))

    def spray(copy, own, h):
        own(h).start()

        def turn(t, carry):
            to_x = lax.rem(my_x + t, 4)
            to_z = lax.rem(my_z + t + t // 4, 4)
            near = 16 * my_y + 4 * to_z + to_x
            copy(h, 16 * (1 - my_y) + 4 * to_z + to_x).start()

            @pl.when(t != 0)
            def _():
                copy(h, near).start()

            return carry

        lax.fori_loop(0, 16, turn, 0)

    def all_sent(copy, h):
        def gone(i, carry):
            copy(h, lax.rem(me + i, n)).wait_send()
            return carry

        lax.fori_loop(1, n, gone, 0)

    for h in range(2):
        for u in (2 * h, 2 * h + 1):
            bc_copy(u).wait_recv()
            cols_b, cols_c = pair_cols(u)
            pair_b = (own_ref[:, cols_b] + got_bc[u, :, :128].astype(F32)).astype(BF16)
            pair_c = (own_ref[:, cols_c] + got_bc[u, :, 128:].astype(F32)).astype(BF16)
            for k in range(2):
                b_ref[2 * u + k] = pair_b[:, k * STATE:(k + 1) * STATE]
                c_ref[2 * u + k] = pair_c[:, k * STATE:(k + 1) * STATE]

        def produce(i, carry):
            block = lax.rem(my_pair + i, PAIRS)
            g = 4 * h + block
            spread = nn(stack, spread_matrix(g))
            step_x = spread[:TOK]
            cot = cot_ref[:, wide(g)].astype(F32)
            disc = (step_x * val_ref[:, wide(g)].astype(F32)).astype(BF16)
            wgt = (spread[TOK:2 * TOK] * disc.astype(F32)).astype(BF16)
            rc = (spread[2 * TOK:3 * TOK] * cot).astype(BF16)
            step_ref[g] = step_x
            skipx_ref[g] = spread[3 * TOK:3 * TOK + 8]
            totx_ref[g] = spread[3 * TOK + 8:3 * TOK + 16]
            disc_ref[g] = disc
            wgt_ref[g] = wgt
            rc_ref[g] = rc
            local = tn(b_ref[g], wgt).astype(BF16)
            first = tn(c_ref[g], rc).astype(BF16)
            for j in range(8):
                out_ref[h, block * 8 + j, :64, :] = local[:, j * HALF:(j + 1) * HALF]
                out_ref[h, block * 8 + j, 64:, :] = first[:, j * HALF:(j + 1) * HALF]
            return carry

        lax.fori_loop(0, PAIRS, produce, 0)
        spray(out_copy, own_copy, h)

    def send_totals(i, carry):
        tot_copy(lax.rem(me + i, n)).start()
        return carry

    lax.fori_loop(1, n, send_totals, 0)
    tots_ref[me] = tot_ref[...]

    dlog_ref[...] = jnp.zeros_like(dlog_ref)
    half = lax.broadcasted_iota(jnp.int32, (1, TOK), 1) < STATE
    left = jnp.where(half, 1.0, 0.0)
    left_b = left.astype(BF16)
    right_b = (1.0 - left).astype(BF16)
    bad = jnp.where(valid, 0.0, 1.0)

    def inside(g, carry):
        b, c = b_ref[g], c_ref[g]
        scores = nt(c, b)
        logs = pltpu.roll(logd_ref[...], lax.rem(HEADS - 16 * g, HEADS), 1)
        d_scores = jnp.zeros((TOK, TOK), F32)
        errs = []
        for q in range(8):
            lanes = pl.ds(pl.multiple_of(g * WIDE + q * 128, 128), 128)
            cot_p = cot_ref[:, lanes]
            disc_p = disc_ref[g, :, q * 128:(q + 1) * 128]
            stacked = jnp.concatenate([disc_p * left_b, disc_p * right_b], axis=0)
            d_mixed = nt(cot_p, stacked)
            mixed = []
            for k in range(2):
                head = 2 * q + k
                span = logs[:, head:head + 1] - logt_ref[pl.ds(g * 16 + head, 1), :]
                weights = jnp.exp(jnp.where(valid, span, -1e30))
                d_scores += d_mixed[:, k * TOK:(k + 1) * TOK] * weights
                mixed.append((weights * scores).astype(BF16))
            mixed = jnp.concatenate(mixed, axis=1)
            inner = nn(mixed, stacked)
            both = tn(mixed, cot_p)
            dd = both[:TOK] * left + both[TOK:] * (1.0 - left)
            dd_ref[g, :, q * 128:(q + 1) * 128] = dd.astype(BF16)
            errs.append(cot_p.astype(F32) * inner - disc_p.astype(F32) * dd)
        dlog_ref[...] += per_head(jnp.concatenate(errs, axis=1), gather_matrix(g))
        ds = d_scores.astype(BF16)
        dc_ref[g] = nn(ds, b)
        db_ref[g] = tn(ds, c)
        return carry

    lax.fori_loop(0, GROUPS, inside, 0)
    loads[4].wait()
    loads[5].wait()
    pick_row = lax.broadcasted_iota(jnp.int32, (16, 16), 0)
    pick_col = lax.broadcasted_iota(jnp.int32, (16, 16), 1)
    pick = jnp.where(pick_col == pick_row + 2 * my_eighth, 1.0, 0.0).astype(BF16)
    picked = [nn(pick, init_ref[h]) for h in range(2)]
    turned = [picked[h][r:r + 1, i * 128:(i + 1) * 128] for h in range(2) for r in range(2) for i in range(32)]
    turned = jnp.transpose(jnp.concatenate(turned, axis=0)).astype(BF16)
    from_i = lax.broadcasted_iota(jnp.int32, (128, OWN), 0)
    to_p = lax.broadcasted_iota(jnp.int32, (128, OWN), 1)
    even = jnp.where(to_p == 2 * from_i, 1.0, 0.0).astype(BF16)
    odd = jnp.where(to_p == 2 * from_i + 1, 1.0, 0.0).astype(BF16)
    init_state = nn(turned[:64], even) + nn(turned[64:], odd)

    def total_in(i, carry):
        src = lax.rem(me + n - i, n)
        remote(tot_ref, tots_ref.at[src], s3.at[src], r3.at[src], (src, f)).wait_recv()
        return carry

    lax.fori_loop(1, n, total_in, 0)
    from_head = lax.broadcasted_iota(jnp.int32, (HEADS, HALF), 0)
    to_lane = lax.broadcasted_iota(jnp.int32, (HEADS, HALF), 1) // STATE
    for h in range(2):
        owned = jnp.where(from_head == to_lane + 64 * h + 2 * me, 1.0, 0.0).astype(BF16)
        lap_ref[h] = sum(nn(part_of, owned) for part_of in split3(tots_ref[:, 0, :]))

    def back_copy(h, to):
        return remote(back_ref.at[h, to], home_ref.at[h, me], s2.at[h, to], r2.at[h, me], (to, f))

    def own_back(h):
        return pltpu.make_async_copy(back_ref.at[h, me], home_ref.at[h, me], lsem.at[20 + h])

    for h in range(2):
        lanes = slice(h * HALF, (h + 1) * HALF)
        own_copy(h).wait()

        def arrive(i, carry):
            src = lax.rem(me + n - i, n)
            remote(out_ref.at[h, src], in_ref.at[h, src], s1.at[h, src], r1.at[h, src], (src, f)).wait_recv()
            return carry

        lax.fori_loop(1, n, arrive, 0)

        def laps(i, state):
            ahead, behind = state
            j = n - 1 - i
            back_ref[h, i, :64, :] = ahead.astype(BF16)
            back_ref[h, j, 64:, :] = behind.astype(BF16)
            ahead = lap_ref[h, pl.ds(i, 1), :] * ahead + in_ref[h, i, :64, :].astype(F32)
            behind = in_ref[h, j, 64:, :].astype(F32) + lap_ref[h, pl.ds(j, 1), :] * behind
            return ahead, behind

        lax.fori_loop(0, n, laps, (init_state[:, lanes], jnp.zeros((STATE, HALF), F32)))

        spray(back_copy, own_back, h)

    for h in range(2):
        own_back(h).wait()
    dstep_ref[...] = jnp.zeros_like(dstep_ref)

    def save(g):
        return pltpu.make_async_copy(disc_ref.at[g], gval_hbm.at[:, wide(g)], lsem.at[8 + g])

    def rows(at, count):
        return pl.ds(pl.multiple_of(at, count), count)

    def x_peer(x):
        return (me - my_x + x, f)

    def z_peer(z):
        return (me + 4 * (z - my_z), f)

    def row_peer(q):
        return (4 * q + my_x, f)

    def plane_peer(q):
        return (16 * (q // 4) + 4 * my_z + lax.rem(q, 4), f)

    def exchange(k, peer, mine_at, source, target, count=4):
        copies = []
        for step_to in range(1, count):
            to = lax.rem(mine_at + step_to, count)
            copies.append(remote(source(to), target(mine_at), ssem.at[k + to], rsem.at[k + mine_at], peer(to)))
        return copies

    def landed(k, peer, mine_at, source, target, count=4):
        for step_to in range(1, count):
            at = lax.rem(mine_at + step_to, count)
            remote(source(at), target(at), ssem.at[k + at], rsem.at[k + at], peer(at)).wait_recv()

    def summed(first, got, at, count=4):
        total = first.astype(F32)
        for step_to in range(1, count):
            total += got[lax.rem(at + step_to, count)].astype(F32)
        return total

    chunk_cols = (slice(0, 512), slice(512, 1152))
    bufs = (
        (part_0, ra1_0, rb1_0, a1_0, b1_0, ra2_0, rb2_0, fa_0, fb_0, a128_0, b128_0),
        (part_1, ra1_1, rb1_1, a1_1, b1_1, ra2_1, rb2_1, fa_1, fb_1, a128_1, b128_1),
    )
    sent = []

    def stages(c):
        part, ra1, rb1, a1, b1, ra2, rb2, fa, fb, a128, b128 = bufs[c]
        k = 100 * c
        cols = chunk_cols[c]
        return (
            (k + 12, x_peer, my_x, lambda x: part.at[rows(128 * x, 128), :], lambda x: ra1.at[x]),
            (k + 16, z_peer, my_z, lambda z: part.at[rows(512 + 128 * z, 128), :], lambda z: rb1.at[z]),
            (k + 20, row_peer, my_row, lambda q: a1.at[rows(16 * q, 16), :], lambda q: ra2.at[q], 8),
            (k + 28, plane_peer, my_plane, lambda q: b1.at[rows(16 * q, 16), :], lambda q: rb2.at[q], 8),
            (k + 66, row_peer, my_row, lambda q: fa, lambda q: a128.at[rows(16 * q, 16), :], 8),
            (k + 74, plane_peer, my_plane, lambda q: fb, lambda q: b128.at[rows(16 * q, 16), :], 8),
            (k + 38, x_peer, my_x, lambda x: a128, lambda x: gw_hbm.at[rows(128 * x, 128), cols]),
            (k + 42, z_peer, my_z, lambda z: b128, lambda z: gw_hbm.at[rows(512 + 128 * z, 128), cols]),
        )

    def go(stage):
        copies = exchange(*stage)
        for one in copies:
            one.start()
        sent.extend(copies)

    def d_copies(h):
        cols, whole = slice(512 * h, 512 * h + 512), chunk_cols[h]
        own_d = dall.at[:128, cols]
        return (
            link(50 + 3 * h, own_d, dall.at[128:256, cols], far),
            link(51 + 3 * h, own_d, dall.at[256:384, cols], sib),
            link(52 + 3 * h, dall.at[128:256, whole], dall.at[384:512, whole], sib),
        )

    def d_steps():
        own_d = dall.at[:128, 1024:]
        return (
            link(56, own_d, dall.at[128:256, 1024:], far),
            link(57, own_d, dall.at[256:384, 1024:], sib),
        )

    def give_d(h):
        for one in d_copies(h)[:2]:
            one.start()

    def first_stage(h):
        to_far, to_sib, forward = d_copies(h)
        to_far.wait_recv()
        if h == 1:
            d_steps()[0].wait_recv()
        forward.start()
        to_sib.wait_recv()
        if h == 1:
            d_steps()[1].wait_recv()
        forward.wait_recv()
        part, cols = bufs[h][0], chunk_cols[h]

        def product(at):
            part[rows(at, 128), :] = tn(xall[:, rows(at, 128)], dall[:, cols]).astype(BF16)

        a_sent, b_sent = exchange(*stages(h)[0]), exchange(*stages(h)[1])
        for k in range(3):
            product(128 * lax.rem(my_x + k + 1, 4))
            a_sent[k].start()
            product(512 + 128 * lax.rem(my_z + k + 1, 4))
            b_sent[k].start()
        product(128 * my_x)
        product(512 + 128 * my_z)
        sent.extend(a_sent + b_sent)

    def second_stage(c):
        part, ra1, rb1, a1, b1 = bufs[c][:5]
        stage = stages(c)
        landed(*stage[0])
        a1[...] = summed(part[rows(128 * my_x, 128), :], ra1, my_x).astype(BF16)
        go(stage[2])
        landed(*stage[1])
        b1[...] = summed(part[rows(512 + 128 * my_z, 128), :], rb1, my_z).astype(BF16)
        go(stage[3])

    def third_stage(c):
        a1, b1, ra2, rb2, fa, fb, a128, b128 = bufs[c][3:]
        stage = stages(c)
        landed(*stage[2])
        fa[...] = summed(a1[rows(16 * my_row, 16), :], ra2, my_row, 8).astype(BF16)
        go(stage[4])
        landed(*stage[3])
        fb[...] = summed(b1[rows(16 * my_plane, 16), :], rb2, my_plane, 8).astype(BF16)
        go(stage[5])
        a128[rows(16 * my_row, 16), :] = fa[...]
        b128[rows(16 * my_plane, 16), :] = fb[...]

    def keep(c):
        a128, b128 = bufs[c][9:]
        cols = chunk_cols[c]
        return (
            pltpu.make_async_copy(a128, gw_hbm.at[rows(128 * my_x, 128), cols], lsem.at[(16, 22)[c]]),
            pltpu.make_async_copy(b128, gw_hbm.at[rows(512 + 128 * my_z, 128), cols], lsem.at[(17, 23)[c]]),
        )

    def last_stage(c):
        stage = stages(c)
        landed(*stage[4])
        go(stage[6])
        landed(*stage[5])
        go(stage[7])
        for one in keep(c):
            one.start()

    def input_product(at, target):
        d = dall[at:at + 128, :]
        d = jnp.concatenate([d[:, :256], d[:, 512:768], d[:, 256:512], d[:, 768:]], axis=1)
        target[:, pl.ds(mine, 1024)] = nt(d, w_ref[...]).astype(BF16)
        target[:, pl.ds(other, 1024)] = nt(d, wsib_ref[...]).astype(BF16)

    for h in range(2):

        def consume(i, carry):
            block = lax.rem(my_pair + PAIRS - i, PAIRS)
            g = 4 * h + block
            for j in range(8):
                src = block * 8 + j

                @pl.when(src != me)
                def _():
                    remote(back_ref.at[h, src], home_ref.at[h, src], s2.at[h, src], r2.at[h, src], (src, f)).wait_recv()

            got = jnp.concatenate([home_ref[h, block * 8 + j] for j in range(8)], axis=1)
            start, end = got[:64], got[64:]
            b, c = b_ref[g], c_ref[g]
            rc, wgt, disc = rc_ref[g], wgt_ref[g], disc_ref[g].astype(F32)
            carried = nn(c, start)
            d_wgt = nn(b, end)
            dc_ref[g] += nt(rc, start)
            db_ref[g] += nt(wgt, end)
            pull = wgt.astype(F32) * d_wgt
            mat = gather_matrix(g)
            err = rc.astype(F32) * carried - pull
            ends = jnp.sum(pull, axis=0, keepdims=True)
            ends += totx_ref[g, :1, :] * jnp.sum(start.astype(F32) * end.astype(F32), axis=0, keepdims=True)
            at_end = lax.broadcasted_iota(jnp.int32, (TOK, WIDE), 0) == TOK - 1
            err = err + jnp.where(at_end, ends, 0.0)
            dlog_ref[...] += per_head(err, mat)
            spread = nn(stack[TOK:2 * TOK], spread_matrix(g))
            d_disc = dd_ref[g].astype(F32) + spread * d_wgt
            val = val_ref[:, wide(g)].astype(F32)
            dstep_ref[...] += per_head(d_disc * val, mat)
            gval = skipx_ref[g, :1, :] * cot_ref[:, wide(g)].astype(F32) + step_ref[g] * d_disc
            disc_ref[g] = gval.astype(BF16)
            save(g).start()
            return carry

        lax.fori_loop(0, PAIRS, consume, 0)
        some = range(4 * h, 4 * h + 4)
        at = 512 * h
        dall[:128, at:at + 256] = jnp.concatenate([db_ref[g] for g in some], axis=1).astype(BF16)
        dall[:128, at + 256:at + 512] = jnp.concatenate([dc_ref[g] for g in some], axis=1).astype(BF16)
        give_d(h)
    send_xo.wait_recv()
    send_fwd.wait_recv()
    first_stage(0)
    up_tri = jnp.where(col >= row, 1.0, 0.0).astype(BF16)
    d_inc = exact(up_tri, dlog_ref[...])
    d_step = dstep_ref[...] - rate_ref[...] * d_inc
    dall[:128, 1024:] = (d_step / (1.0 + jnp.exp(-raw))).astype(BF16)
    for one in d_steps():
        one.start()
    input_product(0, gin_ref)
    save_gin = pltpu.make_async_copy(gin_ref, gin_hbm.at[:, pl.ds(base, 2048)], lsem.at[7])
    save_gin.start()
    first_stage(1)
    second_stage(0)
    input_product(128, ginfar_ref)
    send_gin = link(11, ginfar_ref, gin_hbm.at[:, pl.ds(base, 2048)], far)
    third_stage(0)
    second_stage(1)
    third_stage(1)
    send_gin.start()
    last_stage(0)
    last_stage(1)

    def drain(i, carry):
        to = lax.rem(me + i, n)
        out_copy(0, to).wait_send()
        out_copy(1, to).wait_send()
        back_copy(0, to).wait_send()
        back_copy(1, to).wait_send()
        tot_copy(to).wait_send()
        return carry

    lax.fori_loop(1, n, drain, 0)
    for one in (send_x0, send_x1, send_w, send_xo, send_fwd, send_raw, send_gin):
        one.wait_send()
    for one in [*d_copies(0), *d_copies(1), *d_steps()] + [bc_copy(u) for u in range(PAIRS)]:
        one.wait_send()
    send_gin.wait_recv()
    save_gin.wait()

    def saved(g, carry):
        save(g).wait()
        return carry

    lax.fori_loop(0, GROUPS, saved, 0)
    for c in range(2):
        for one in keep(c):
            one.wait()
        for stage in stages(c)[6:]:
            landed(*stage)
    for one in sent:
        one.wait_send()


def layer(x, w, val, cot, init, resets, bias, rate, skip):
    n = 32
    slab = (GROUPS, TOK, WIDE)
    hbm = pl.BlockSpec(memory_space=pl.ANY)
    vm = pltpu.VMEM
    dma = pltpu.SemaphoreType.DMA
    return pl.pallas_call(
        layer_kernel,
        out_shape=(
            jax.ShapeDtypeStruct((TOK, 4096), BF16),
            jax.ShapeDtypeStruct((TOK, GROUPS * WIDE), BF16),
            jax.ShapeDtypeStruct((1024, COLS), BF16),
        ),
        in_specs=[hbm] * 5 + [VMEM] * 4,
        out_specs=[hbm] * 3,
        scratch_shapes=[
            vm((TOK, 4096), BF16),
            vm((1024, COLS), BF16),
            vm((1024, COLS), BF16),
            vm((4 * TOK, 1024), BF16),
            vm((TOK, 1024), BF16),
            vm((TOK, COLS), F32),
            vm((TOK, COLS), F32),
            vm((TOK, HEADS), F32),
            vm((TOK, HEADS), F32),
            vm((PAIRS, TOK, 256), BF16),
            vm((PAIRS, TOK, 256), BF16),
            vm((GROUPS, TOK, STATE), BF16),
            vm((GROUPS, TOK, STATE), BF16),
            vm((TOK, GROUPS * WIDE), BF16),
            vm((TOK, GROUPS * WIDE), BF16),
            vm((2, 16, 4096), BF16),
            vm(slab, BF16),
            vm(slab, BF16),
            vm(slab, BF16),
            vm(slab, F32),
            vm((GROUPS, 8, WIDE), F32),
            vm((GROUPS, 8, WIDE), F32),
            vm(slab, BF16),
            vm((HEADS, TOK), F32),
            vm((TOK, HEADS), F32),
            vm((TOK, HEADS), F32),
            vm((TOK, HEADS), F32),
            vm((GROUPS, TOK, STATE), F32),
            vm((GROUPS, TOK, STATE), F32),
            vm((2, n, 128, HALF), BF16),
            vm((2, n, 128, HALF), BF16),
            vm((2, n, 128, HALF), BF16),
            vm((2, n, 128, HALF), BF16),
            vm((8, HEADS), F32),
            vm((n, 8, HEADS), F32),
            vm((2, n, HALF), F32),
            vm((4 * TOK, COLS), BF16),
            vm((TOK, 2048), BF16),
            vm((TOK, 2048), BF16),
            *[vm(rows + (cols,), BF16)
              for rows in ((1024,), (4, 128), (4, 128), (128,), (128,), (8, 16), (8, 16), (16,), (16,), (128,), (128,))
              for cols in (512, 640)],
            dma((182,)),
            dma((182,)),
            dma((24,)),
            dma((2, n)),
            dma((2, n)),
            dma((2, n)),
            dma((2, n)),
            dma((n,)),
            dma((n,)),
            pltpu.SemaphoreType.REGULAR,
            pltpu.SemaphoreType.REGULAR,
        ],
        compiler_params=pltpu.CompilerParams(
            collective_id=0, has_side_effects=True, vmem_limit_bytes=60 * 2**20
        ),
        name="layer",
    )(x, w, val, cot, init, resets, bias, rate, skip)


def finish_kernel(scale, gin, gval, gw, gin_out, gval_out, gw_out, narrow, full, gin_v, gval_v, sem_i, sem_o):
    def some(k):
        return pl.ds(128 * k, 128)

    def pick(k):
        return pl.ds(32 * k, 32)

    loads = [pltpu.make_async_copy(gw.at[some(k), :], narrow.at[some(k), :], sem_i.at[k]) for k in range(8)]
    stores = [pltpu.make_async_copy(full.at[some(k), :], gw_out.at[some(k), :], sem_o.at[k]) for k in range(8)]
    loads += [pltpu.make_async_copy(gval.at[pick(k), :], gval_v.at[pick(k), :], sem_i.at[8 + k]) for k in range(4)]
    stores += [pltpu.make_async_copy(gval_v.at[pick(k), :], gval_out.at[pick(k), :], sem_o.at[8 + k]) for k in range(4)]
    loads.append(pltpu.make_async_copy(gin, gin_v, sem_i.at[12]))
    stores.append(pltpu.make_async_copy(gin_v, gin_out, sem_o.at[12]))
    for one in loads:
        one.start()
    for k in range(13):
        loads[k].wait()
        if k < 8:
            for to, at, wide in ((0, 0, 256), (256, 512, 256), (512, 256, 256), (768, 768, 384)):
                full[some(k), to:to + wide] = narrow[some(k), at:at + wide].astype(F32) * scale
        stores[k].start()
    for one in stores:
        one.wait()


def finish(scale, gin, gval, gw):
    hbm = pl.BlockSpec(memory_space=pl.ANY)
    return pl.pallas_call(
        functools.partial(finish_kernel, scale),
        out_shape=(
            jax.ShapeDtypeStruct(gin.shape, BF16),
            jax.ShapeDtypeStruct(gval.shape, BF16),
            jax.ShapeDtypeStruct(gw.shape, F32),
        ),
        in_specs=[hbm] * 3,
        out_specs=[hbm] * 3,
        scratch_shapes=[
            pltpu.VMEM((1024, COLS), BF16),
            pltpu.VMEM((1024, COLS), F32),
            pltpu.VMEM((TOK, 4096), BF16),
            pltpu.VMEM((TOK, GROUPS * WIDE), BF16),
            pltpu.SemaphoreType.DMA((13,)),
            pltpu.SemaphoreType.DMA((13,)),
        ],
        compiler_params=pltpu.CompilerParams(vmem_limit_bytes=60 * 2**20),
        name="finish",
    )(gin, gval, gw)


def body(inputs, values, cotangent, weight, init_state, resets, dt_bias, decay_rate, skip):
    scale = 1.0 / math.sqrt(lax.axis_size("fsdp") * TOK * lax.axis_size("ctx"))
    gin, gval, gw = layer(inputs[0], weight, values[0], cotangent[0], init_state[0], resets,
                          dt_bias[None], decay_rate[None], skip[None])
    gin, gval, gw = finish(scale, gin, gval, gw)
    return (gin[None], gval[None], gw)


def solution(mesh):
    in_specs = (
        P("fsdp", "ctx", None),
        P("fsdp", "ctx", None),
        P("fsdp", "ctx", None),
        P("fsdp", None),
        P("fsdp", None, None),
        P("fsdp", "ctx"),
        P(),
        P(),
        P(),
    )
    out_specs = (P("fsdp", "ctx", None), P("fsdp", "ctx", None), P("fsdp", None))
    return jax.shard_map(body, mesh=mesh, in_specs=in_specs, out_specs=out_specs, check_vma=False)
```
